512 devices in a mesh: view: 4 (over x), dev: 128 (over y, z, core).
Axes of the slice: x: 4, y: 8, z: 8, core: 2. Of those that a mesh axis runs over, the one named last changes fastest.
Arguments:
- params: float32 [59, 524288], P(None, 'dev'), may hold values from -6 to 2.8, as said below
- first_moment: float32 [59, 524288], P(None, 'dev'), may hold values from -0.3 to 0.3
- second_moment: float32 [59, 524288], P(None, 'dev'), may hold values from 0.0001 to 0.01
- cam_centers: float32 [4, 3], P('view'), may hold values from -4 to 0.7, as said below
- target: float32 [4, 2048, 3, 256], P('view', 'dev'), may hold values from 0 to 1
- send_rows: int32 [4, 128, 1024], P('view', 'dev'), may hold values from 0 to 4095, as said below
- tile_lists: int32 [4, 2048, 64], P('view', 'dev'), may hold values from 0 to 1023, as said below
- tile_counts: int32 [4, 2048], P('view', 'dev'), may hold values from 1 to 64, as said below
- tile_ids: int32 [4, 2048], P('view', 'dev'), may hold values from 0 to 2047, as said below
- move_order: int32 [128, 4096], P('dev'), may hold values from 0 to 4095, each once within a row
Outputs:
- new_params: float32 [59, 524288], P(None, 'dev')
- new_first: float32 [59, 524288], P(None, 'dev')
- new_second: float32 [59, 524288], P(None, 'dev')
The draws below stay inside these ranges and needn't reach their ends.
Inputs may be any that keep to these rules, and one draw needn't show every extreme that they name: `cam_centers`: for every view the first two coordinates lie in 0.3 to 0.7 and the third in -4 to -2. `params`: rows 0 and 1 lie in -1.8 to 2.8, row 2 in 0 to 1, rows 3 to 5 in -5 to -3, row 6 in 0.5 to 1.5, rows 7 to 9 in -1 to 1, row 10 in -6 to -3, rows 11 to 58 in -1.5 to 1.5. `send_rows`: each of an owner's 4096 Gaussians fills exactly one of its slots over all views and renderers. `tile_lists`: the list of tile slot k names each of its renderer's slots (k % 16) * 64 to (k % 16 + 1) * 64 - 1 exactly once. `tile_counts`: some tile of every view has a full list. Each view's tile_ids is a permutation.
All inputs are finite; a program needn't handle non-finite values.
Results may differ from the reference program's by a relative error of at most 0.0003.
Values sent between devices are 32-bit elements; how exact they have to be, the bound alone decides.
A program may use at most 64 MiB of HBM per device.

```python
import math
import jax
import jax.numpy as jnp
from jax import lax

G_DEV = 4096
PARAMS = 59
TILES_DEV = 16
TILE_SIDE = 16
TILES_X = 64
MOVE_PEER = 1
ADAM_STEP = 1000
VIEWS = 4
OWNERS = 128
GAUSS = 524288
CAP = 8
SLOTS = 1024
TILES = 2048
PIX = 256
LIST = 64
KEEP = 3968


def camera_draw(key):
    key = jax.random.fold_in(key, 13)
    sub_keys = jax.random.split(key, 2)
    plane = jax.random.uniform(sub_keys[0], (VIEWS, 2), jnp.float32, 0.3, 0.7)
    behind = jax.random.uniform(sub_keys[1], (VIEWS, 1), jnp.float32, -4.0, -2.0)
    return jnp.concatenate([plane, behind], axis=1)


def slot_orders(key):
    key = jax.random.fold_in(key, 17)
    owner_keys = jax.random.split(key, OWNERS)
    return jax.vmap(lambda one_key: jax.random.permutation(one_key, G_DEV))(owner_keys).astype(jnp.int32)


def screen_orders(key):
    key = jax.random.fold_in(key, 19)
    view_keys = jax.random.split(key, VIEWS)
    return jax.vmap(lambda one_key: jax.random.permutation(one_key, TILES))(view_keys).astype(jnp.int32)


def list_orders(key):
    key = jax.random.fold_in(key, 23)
    tile_keys = jax.random.split(key, VIEWS * TILES)
    orders = jax.vmap(lambda one_key: jax.random.permutation(one_key, LIST))(tile_keys).astype(jnp.int32)
    return orders.reshape(VIEWS, TILES, LIST)


def draw_params(key, part):
    cameras = camera_draw(key)
    orders = slot_orders(key)
    screens = screen_orders(key)
    lists = list_orders(key)
    key = jax.random.fold_in(key, 7)
    sub_keys = jax.random.split(key, 8)
    place = jnp.argsort(orders, axis=1).astype(jnp.int32)
    view_of = place // SLOTS
    remain = place % SLOTS
    holder = remain // CAP
    slot = jnp.arange(OWNERS, dtype=jnp.int32)[:, None] * CAP + remain % CAP
    tile_slot = holder * TILES_DEV + slot // LIST
    list_place = jnp.argsort(lists, axis=2).astype(jnp.int32)
    entry = list_place[view_of, tile_slot, slot % LIST]
    screen_tile = screens[view_of, tile_slot]
    width_px = TILES_X * TILE_SIDE
    height_px = TILES // TILES_X * TILE_SIDE
    shape_all = (OWNERS, G_DEV)
    jitter_u = jax.random.uniform(sub_keys[0], shape_all, jnp.float32)
    jitter_v = jax.random.uniform(sub_keys[1], shape_all, jnp.float32)
    jitter_depth = jax.random.uniform(sub_keys[2], shape_all, jnp.float32)
    screen_u = ((screen_tile % TILES_X).astype(jnp.float32) + jitter_u) * TILE_SIDE / width_px
    screen_v = ((screen_tile // TILES_X).astype(jnp.float32) + jitter_v) * TILE_SIDE / height_px
    depth = (entry.astype(jnp.float32) + jitter_depth) / LIST
    center_x = cameras[:, 0][view_of]
    center_y = cameras[:, 1][view_of]
    center_z = cameras[:, 2][view_of]
    reach = (depth - center_z) / 1.2
    position = jnp.stack([center_x + (screen_u - 0.5) * reach, center_y + (screen_v - 0.5) * reach, depth]).reshape(3, GAUSS)
    columns = GAUSS
    log_scale = jax.random.uniform(sub_keys[3], (3, columns), jnp.float32, -5.0, -3.0)
    quat_w = jax.random.uniform(sub_keys[4], (1, columns), jnp.float32, 0.5, 1.5)
    quat_rest = jax.random.uniform(sub_keys[5], (3, columns), jnp.float32, -1.0, 1.0)
    opacity_logit = jax.random.uniform(sub_keys[6], (1, columns), jnp.float32, -6.0, -3.0)
    sh_coef = jnp.clip(0.4 * jax.random.normal(sub_keys[7], (48, columns), jnp.float32), -1.5, 1.5)
    return jnp.concatenate([position, log_scale, quat_w, quat_rest, opacity_logit, sh_coef], axis=0)


def draw_cam_centers(key, part):
    return camera_draw(key)


def draw_send_rows(key, part):
    orders = slot_orders(key)
    return orders.reshape(OWNERS, VIEWS, SLOTS).transpose(1, 0, 2)


def draw_tile_lists(key, part):
    lists = list_orders(key)
    base = jnp.arange(TILES, dtype=jnp.int32) % TILES_DEV * LIST
    return (lists + base[None, :, None]).astype(jnp.int32)


def draw_tile_ids(key, part):
    return screen_orders(key)


def draw_tile_counts(key, part):
    key = jax.random.fold_in(key, 11)
    sub_keys = jax.random.split(key, 4)
    devices = TILES // TILES_DEV
    chosen_tile = jax.random.randint(sub_keys[1], (VIEWS, 1), 0, TILES)
    heavy = jax.random.randint(sub_keys[0], (VIEWS, devices), 0, 4) == 0
    heavy = heavy | (jnp.arange(devices, dtype=jnp.int32)[None, :] == chosen_tile // TILES_DEV)
    heavy_tiles = jnp.repeat(heavy, TILES_DEV, axis=1)
    long_lists = jax.random.randint(sub_keys[2], (VIEWS, TILES), LIST // 2, LIST + 1)
    short_lists = jax.random.randint(sub_keys[3], (VIEWS, TILES), 1, LIST // 4 + 1)
    counts_all = jnp.where(heavy_tiles, long_lists, short_lists)
    is_chosen = jnp.arange(TILES, dtype=jnp.int32)[None, :] == chosen_tile
    return jnp.where(is_chosen, LIST, counts_all).astype(jnp.int32)


def block_scale(rng, extent, cuts, smallest, top_value):
    loudness, own = 1.0, jax.random.fold_in(rng, 6)
    for dim, parts in cuts:
        draws = jnp.exp(jax.random.uniform(jax.random.fold_in(own, dim), (parts,), jnp.float32, smallest / len(cuts), top_value / len(cuts)))
        loudness = loudness * jnp.repeat(draws, extent[dim] // parts).reshape([-1 if axis == dim else 1 for axis in range(len(extent))])
    return loudness


def bell_draw(own_key, extent, deviation, bound, cuts=(), kind=jnp.bfloat16):
    array = deviation * jax.random.normal(own_key, extent, jnp.float32)
    if cuts:
        array = array * block_scale(own_key, extent, cuts, -0.22, 0.18)
    return jnp.clip(array, -bound, bound).astype(kind)


def setup_inputs(seed: int = 0) -> dict:
    streams_of = jax.random.split(jax.random.key(seed), 11)
    return {
        "params": draw_params(jax.random.fold_in(streams_of[10], 71), 0),
        "first_moment": bell_draw(streams_of[1], (PARAMS, GAUSS), 0.05, 0.3, ((1, 128),), jnp.float32),
        "second_moment": jnp.clip(jnp.exp(math.log(0.01) - 4.6051702 * jax.random.uniform(streams_of[2], (PARAMS, GAUSS), jnp.float32) ** block_scale(streams_of[2], (PARAMS, GAUSS), ((1, 128),), -0.2, 0.2)), 0.0001, 0.01),
        "cam_centers": draw_cam_centers(jax.random.fold_in(streams_of[10], 71), 0),
        "target": jnp.clip(1.0 * jax.random.uniform(streams_of[4], (VIEWS, TILES, 3, PIX), jnp.float32) ** block_scale(streams_of[4], (VIEWS, TILES, 3, PIX), ((0, 4), (1, 128)), -0.2, 0.2), 0.0, 1.0),
        "send_rows": draw_send_rows(jax.random.fold_in(streams_of[10], 71), 0),
        "tile_lists": draw_tile_lists(jax.random.fold_in(streams_of[10], 71), 0),
        "tile_counts": draw_tile_counts(jax.random.fold_in(streams_of[10], 71), 0),
        "tile_ids": draw_tile_ids(jax.random.fold_in(streams_of[10], 71), 0),
        "move_order": jax.vmap(lambda own: jax.random.permutation(own, G_DEV))(jax.random.split(streams_of[9], OWNERS)).reshape((OWNERS, G_DEV)).astype(jnp.int32),
    }


FOCAL_LEN = 1.2
DILATION = 0.3
SH_C0 = 0.28209479177387814
SH_C1 = 0.4886025119029199
SH_C2 = (1.0925484305920792, -1.0925484305920792, 0.31539156525252005, -1.0925484305920792, 0.5462742152960396)
SH_C3 = (-0.5900435899266435, 2.890611442640554, -0.4570457994644658, 0.3731763325901154, -0.4570457994644658, 1.445305721320277, -0.5900435899266435)
BETA_ONE = 0.9
BETA_TWO = 0.999
ADAM_EPS = 1e-08

def sh_basis(dir_x, dir_y, dir_z):
    dir_xx = dir_x * dir_x
    dir_yy = dir_y * dir_y
    dir_zz = dir_z * dir_z
    return jnp.stack([SH_C0 + 0.0 * dir_x, -SH_C1 * dir_y, SH_C1 * dir_z, -SH_C1 * dir_x, SH_C2[0] * dir_x * dir_y, SH_C2[1] * dir_y * dir_z, SH_C2[2] * (2.0 * dir_zz - dir_xx - dir_yy), SH_C2[3] * dir_x * dir_z, SH_C2[4] * (dir_xx - dir_yy), SH_C3[0] * dir_y * (3.0 * dir_xx - dir_yy), SH_C3[1] * dir_x * dir_y * dir_z, SH_C3[2] * dir_y * (4.0 * dir_zz - dir_xx - dir_yy), SH_C3[3] * dir_z * (2.0 * dir_zz - 3.0 * dir_xx - 3.0 * dir_yy), SH_C3[4] * dir_x * (4.0 * dir_zz - dir_xx - dir_yy), SH_C3[5] * dir_z * (dir_xx - dir_yy), SH_C3[6] * dir_x * (dir_xx - 3.0 * dir_yy)])

def project(values, center, width_px, height_px):
    offset = values[0:3] - center[:, None]
    inverse = 1.0 / offset[2]
    mean_u = 0.5 + FOCAL_LEN * offset[0] * inverse
    mean_v = 0.5 + FOCAL_LEN * offset[1] * inverse
    scale_sq = jnp.exp(2.0 * values[3:6])
    quaternion = values[6:10]
    quaternion = quaternion * lax.rsqrt(lax.optimization_barrier(jnp.sum(quaternion * quaternion, axis=0, keepdims=True)))
    quat_w, quat_x, quat_y, quat_z = (quaternion[0], quaternion[1], quaternion[2], quaternion[3])
    rotation = [[1.0 - 2.0 * (quat_y * quat_y + quat_z * quat_z), 2.0 * (quat_x * quat_y - quat_w * quat_z), 2.0 * (quat_x * quat_z + quat_w * quat_y)], [2.0 * (quat_x * quat_y + quat_w * quat_z), 1.0 - 2.0 * (quat_x * quat_x + quat_z * quat_z), 2.0 * (quat_y * quat_z - quat_w * quat_x)], [2.0 * (quat_x * quat_z - quat_w * quat_y), 2.0 * (quat_y * quat_z + quat_w * quat_x), 1.0 - 2.0 * (quat_x * quat_x + quat_y * quat_y)]]
    focal_now = FOCAL_LEN * inverse
    slope_u = -focal_now * offset[0] * inverse
    slope_v = -focal_now * offset[1] * inverse
    cov_uu = DILATION / (width_px * width_px)
    cov_vv = DILATION / (height_px * height_px)
    cov_uv = 0.0
    for column in range(3):
        axis_u = focal_now * rotation[0][column] + slope_u * rotation[2][column]
        axis_v = focal_now * rotation[1][column] + slope_v * rotation[2][column]
        cov_uu = cov_uu + axis_u * axis_u * scale_sq[column]
        cov_vv = cov_vv + axis_v * axis_v * scale_sq[column]
        cov_uv = cov_uv + axis_u * axis_v * scale_sq[column]
    determinant = cov_uu * cov_vv - cov_uv * cov_uv
    distance = jnp.sqrt(lax.optimization_barrier(jnp.sum(offset * offset, axis=0)))
    sh_values = sh_basis(offset[0] / distance, offset[1] / distance, offset[2] / distance)
    sh_coef = values[11:].reshape(16, 3, values.shape[1])
    colors = 0.5 + lax.optimization_barrier(jnp.sum(sh_values[:, None, :] * sh_coef, axis=0))
    opacity = jax.nn.sigmoid(values[10])
    return jnp.concatenate([jnp.stack([mean_u, mean_v, cov_vv / determinant, -cov_uv / determinant, cov_uu / determinant]), colors, opacity[None, :]], axis=0)

def pixel_coords(tile_id, width_px, height_px):
    within = jnp.arange(TILE_SIDE * TILE_SIDE, dtype=jnp.int32)
    pixel_col = tile_id % TILES_X * TILE_SIDE + within % TILE_SIDE
    pixel_row = tile_id // TILES_X * TILE_SIDE + within // TILE_SIDE
    return ((pixel_col.astype(jnp.float32) + 0.5) / width_px, (pixel_row.astype(jnp.float32) + 0.5) / height_px)

def render_tile(gathered, list_count, tile_id, width_px, height_px):
    pixel_u, pixel_v = pixel_coords(tile_id, width_px, height_px)
    is_live = jnp.arange(gathered.shape[1], dtype=jnp.int32) < list_count
    diff_u = pixel_u[:, None] - gathered[0][None, :]
    diff_v = pixel_v[:, None] - gathered[1][None, :]
    exponent = -0.5 * (gathered[2] * diff_u * diff_u + gathered[4] * diff_v * diff_v) - gathered[3] * diff_u * diff_v
    alphas = jnp.where(is_live[None, :], gathered[8][None, :] * jnp.exp(exponent), 0.0)
    log_keep = jnp.log1p(-alphas)
    before = jnp.cumsum(log_keep, axis=1) - log_keep
    weight = alphas * jnp.exp(before)
    return jnp.einsum('ce,pe->cp', gathered[5:8], weight, precision=lax.Precision.HIGHEST)

def learning_rates():
    rows_all = jnp.arange(PARAMS, dtype=jnp.int32)
    return jnp.where(rows_all < 3, 0.00016, jnp.where(rows_all < 6, 0.005, jnp.where(rows_all < 10, 0.001, jnp.where(rows_all < 11, 0.05, jnp.where(rows_all < 14, 0.0025, 0.000125)))))

def adam_update(values, moment_one, moment_two, gradient, step_sizes):
    bias_one = 1.0 - BETA_ONE ** ADAM_STEP
    bias_two = 1.0 - BETA_TWO ** ADAM_STEP
    new_one = BETA_ONE * moment_one + (1.0 - BETA_ONE) * gradient
    new_two = BETA_TWO * moment_two + (1.0 - BETA_TWO) * gradient * gradient
    updated = values - step_sizes * (new_one / bias_one) / (jnp.sqrt(new_two / bias_two) + ADAM_EPS)
    return (updated, new_one, new_two)

def rebalance(states, move_order):
    in_blocks = states.reshape(PARAMS, OWNERS, G_DEV)
    ordered = jnp.take_along_axis(in_blocks, move_order[None, :, :], axis=2)
    kept = ordered[:, :, :KEEP]
    leaving = ordered[:, :, KEEP:].reshape(PARAMS, OWNERS, OWNERS, MOVE_PEER)
    arriving = leaving.transpose(0, 2, 1, 3).reshape(PARAMS, OWNERS, OWNERS * MOVE_PEER)
    return jnp.concatenate([kept, arriving], axis=2).reshape(PARAMS, GAUSS)

def reference(params, first_moment, second_moment, cam_centers, target, send_rows, tile_lists, tile_counts, tile_ids, move_order):
    width_px = float(TILES_X * TILE_SIDE)
    height_px = float(TILES // TILES_X * TILE_SIDE)
    renderer = jnp.arange(TILES, dtype=jnp.int32) // TILES_DEV

    def sq_error(values):
        running = jnp.zeros((), jnp.float32)
        for camera_index in range(VIEWS):
            features = project(values, cam_centers[camera_index], width_px, height_px)
            global_ids = jnp.arange(OWNERS, dtype=jnp.int32)[:, None] * G_DEV + send_rows[camera_index]
            slot_ids = global_ids.reshape(OWNERS, OWNERS, CAP).transpose(1, 0, 2).reshape(OWNERS, SLOTS)

            def one_tile(tile_args):
                entries, list_count, tile_id, wanted, holder = tile_args
                gathered = features[:, slot_ids[holder][entries]]
                residual = render_tile(gathered, list_count, tile_id, width_px, height_px) - wanted
                return 0.5 * jnp.sum(residual * residual)
            per_tile = lax.map(jax.checkpoint(one_tile), (tile_lists[camera_index], tile_counts[camera_index], tile_ids[camera_index], target[camera_index], renderer))
            running = running + jnp.sum(per_tile)
        return running
    gradient = jax.grad(sq_error)(params)
    updated, new_one, new_two = adam_update(params, first_moment, second_moment, gradient, learning_rates()[:, None])
    return (rebalance(updated, move_order), rebalance(new_one, move_order), rebalance(new_two, move_order))
```

```python
import functools

import jax
import jax.numpy as jnp
from jax import lax
from jax.experimental import pallas as pl
from jax.experimental.pallas import tpu as pltpu
from jax.sharding import PartitionSpec as P

PARAMS = 59
PADDED = 64
FEATS = 9
LANES = 128
TILE_SIDE = 16
TILES_X = 64
ADAM_STEP = 1000
FOCAL_LEN = 1.2
DILATION = 0.3
SH_C0 = 0.28209479177387814
SH_C1 = 0.4886025119029199
SH_C2 = (
    1.0925484305920792,
    -1.0925484305920792,
    0.31539156525252005,
    -1.0925484305920792,
    0.5462742152960396,
)
SH_C3 = (
    -0.5900435899266435,
    2.890611442640554,
    -0.4570457994644658,
    0.3731763325901154,
    -0.4570457994644658,
    1.445305721320277,
    -0.5900435899266435,
)
BETA_ONE = 0.9
BETA_TWO = 0.999
ADAM_EPS = 1e-08
WIDTH = 1024.0
HEIGHT = 512.0


def sh_basis(x, y, z):
    xx, yy, zz = x * x, y * y, z * z
    return [
        SH_C0 + 0.0 * x,
        -SH_C1 * y,
        SH_C1 * z,
        -SH_C1 * x,
        SH_C2[0] * x * y,
        SH_C2[1] * y * z,
        SH_C2[2] * (2.0 * zz - xx - yy),
        SH_C2[3] * x * z,
        SH_C2[4] * (xx - yy),
        SH_C3[0] * y * (3.0 * xx - yy),
        SH_C3[1] * x * y * z,
        SH_C3[2] * y * (4.0 * zz - xx - yy),
        SH_C3[3] * z * (2.0 * zz - 3.0 * xx - 3.0 * yy),
        SH_C3[4] * x * (4.0 * zz - xx - yy),
        SH_C3[5] * z * (xx - yy),
        SH_C3[6] * x * (xx - 3.0 * yy),
    ]


def project(values, center):
    off = [values[i] - center[i] for i in range(3)]
    inverse = 1.0 / off[2]
    mean_u = 0.5 + FOCAL_LEN * off[0] * inverse
    mean_v = 0.5 + FOCAL_LEN * off[1] * inverse
    scale_sq = [jnp.exp(2.0 * values[3 + i]) for i in range(3)]
    quat = values[6:10]
    norm = lax.rsqrt(
        quat[0] * quat[0] + quat[1] * quat[1] + quat[2] * quat[2] + quat[3] * quat[3]
    )
    w, x, y, z = (q * norm for q in quat)
    rotation = [
        [1.0 - 2.0 * (y * y + z * z), 2.0 * (x * y - w * z), 2.0 * (x * z + w * y)],
        [2.0 * (x * y + w * z), 1.0 - 2.0 * (x * x + z * z), 2.0 * (y * z - w * x)],
        [2.0 * (x * z - w * y), 2.0 * (y * z + w * x), 1.0 - 2.0 * (x * x + y * y)],
    ]
    focal_now = FOCAL_LEN * inverse
    slope_u = -focal_now * off[0] * inverse
    slope_v = -focal_now * off[1] * inverse
    cov_uu = DILATION / (WIDTH * WIDTH)
    cov_vv = DILATION / (HEIGHT * HEIGHT)
    cov_uv = 0.0
    for c in range(3):
        axis_u = focal_now * rotation[0][c] + slope_u * rotation[2][c]
        axis_v = focal_now * rotation[1][c] + slope_v * rotation[2][c]
        cov_uu = cov_uu + axis_u * axis_u * scale_sq[c]
        cov_vv = cov_vv + axis_v * axis_v * scale_sq[c]
        cov_uv = cov_uv + axis_u * axis_v * scale_sq[c]
    inv_det = 1.0 / (cov_uu * cov_vv - cov_uv * cov_uv)
    inv_dist = 1.0 / jnp.sqrt(off[0] * off[0] + off[1] * off[1] + off[2] * off[2])
    basis = sh_basis(off[0] * inv_dist, off[1] * inv_dist, off[2] * inv_dist)
    colors = []
    for ch in range(3):
        total = basis[0] * values[11 + ch]
        for k in range(1, 16):
            total = total + basis[k] * values[11 + 3 * k + ch]
        colors.append(0.5 + total)
    opacity = 1.0 / (1.0 + jnp.exp(-values[10]))
    return [
        mean_u,
        mean_v,
        cov_vv * inv_det,
        -cov_uv * inv_det,
        cov_uu * inv_det,
        *colors,
        opacity,
    ]


def pick(array, index):
    return jnp.take_along_axis(array, index, axis=1, mode="promise_in_bounds")


def lane_ids(rows=8):
    return lax.broadcasted_iota(jnp.int32, (rows, LANES), 1)


def row_ids(rows=8):
    return lax.broadcasted_iota(jnp.int32, (rows, LANES), 0)


def fill_dense(array_ref, dense_ref):
    for j in range(32):
        dense_ref[PADDED * j : PADDED * j + PARAMS, :] = array_ref[
            :, LANES * j : LANES * (j + 1)
        ]


def dense_at(dense_ref, chunk, row):
    return dense_ref[pl.ds(chunk * 8 * PADDED + row, 8, stride=PADDED), :]


def project_kernel(center_ref, rows_ref, params_ref, out_ref, dense, feats):
    fill_dense(params_ref, dense)
    center = [center_ref[0, i] for i in range(3)]
    for chunk in range(4):
        values = [dense_at(dense, chunk, p) for p in range(PARAMS)]
        for f, value in enumerate(project(values, center)):
            feats[f, 8 * chunk : 8 * chunk + 8, :] = value
    rows = rows_ref[...]
    high = rows // LANES
    low = lax.rem(rows, LANES)
    slots = [jnp.zeros((8, LANES), jnp.float32)] * FEATS
    for h in range(32):
        chosen = high == h
        for f in range(FEATS):
            source = jnp.broadcast_to(feats[f, h : h + 1, :], (8, LANES))
            slots[f] = jnp.where(chosen, pick(source, low), slots[f])
    lane = lane_ids()
    sub = row_ids()
    for block in range(16):
        index = ((block % 2) * 8 + sub) * 8 + lax.rem(lane, 8)
        message = jnp.zeros((8, LANES), jnp.float32)
        for f in range(FEATS):
            source = jnp.broadcast_to(slots[f][block // 2 : block // 2 + 1, :], (8, LANES))
            message = jnp.where(lane // 8 == f, pick(source, index), message)
        out_ref[8 * block : 8 * block + 8, :] = message


def dot(a, b, dims=((1,), (0,))):
    return lax.dot_general(
        a,
        b,
        (dims, ((), ())),
        precision=lax.Precision.HIGHEST,
        preferred_element_type=jnp.float32,
    )


def render_kernel(
    arrived_ref,
    lists_ref,
    counts_ref,
    ids_ref,
    target_ref,
    out_ref,
    gauss,
    trans,
    gauss_grad,
    weight,
    sums,
):
    lane = lane_ids()
    sub = row_ids()
    half_of = lane // 64
    entry = lax.rem(lane, 64)
    slot = lax.rem(lists_ref[...], 64)
    from_owner = slot // 8
    within = lax.rem(slot, 8)
    feats = [jnp.zeros((8, LANES), jnp.float32)] * FEATS
    for h in range(2):
        for o in range(8):
            block = arrived_ref[pl.ds(8 * h + o, 8, stride=16), :]
            chosen = (from_owner == o) & (half_of == h)
            for f in range(FEATS):
                feats[f] = jnp.where(chosen, pick(block, 8 * f + within), feats[f])
    ids = ids_ref[...]
    center_u = (lax.rem(ids, TILES_X) * TILE_SIDE + TILE_SIDE // 2).astype(jnp.float32)
    center_v = (ids // TILES_X * TILE_SIDE + TILE_SIDE // 2).astype(jnp.float32)
    mean_u = feats[0] * WIDTH - center_u
    mean_v = feats[1] * HEIGHT - center_v
    quad_a = feats[2] * (-0.5 / (WIDTH * WIDTH))
    quad_b = feats[3] * (-1.0 / (WIDTH * HEIGHT))
    quad_c = feats[4] * (-0.5 / (HEIGHT * HEIGHT))
    active = entry < counts_ref[...]
    opacity = jnp.where(active, feats[8], 0.0)
    pixel_u = lax.rem(lane, 16).astype(jnp.float32) - 7.5
    pixel_v = [(lane // 16 + 8 * p).astype(jnp.float32) - 7.5 for p in range(2)]
    ahead = [mean_u, mean_v, quad_a, quad_b, quad_c, *feats[5:8], opacity]

    def forward(e, carried):
        through, acc, place = carried
        through, acc = list(through), list(acc)
        for h in range(2):
            index = jnp.full((8, LANES), h * 64, jnp.int32) + e
            m_u, m_v, q_a, q_b, q_c, c_0, c_1, c_2, alpha_max = (
                pick(array, index) for array in ahead
            )
            place = jnp.where((pick(slot, index) == entry) & (half_of == h), e, place)
            diff_u = pixel_u - m_u
            part = diff_u * q_b
            square = diff_u * diff_u * q_a
            for p in range(2):
                diff_v = pixel_v[p] - m_v
                bell = jnp.exp(square + diff_v * (part + q_c * diff_v))
                alpha = alpha_max * bell
                n = 2 * h + p
                before = through[n]
                gauss[e, n] = bell
                trans[e, n] = before
                share = alpha * before
                through[n] = before - share
                for ch, color in enumerate((c_0, c_1, c_2)):
                    acc[3 * n + ch] = acc[3 * n + ch] + color * share
        return tuple(through), tuple(acc), place

    zero = jnp.zeros((8, LANES), jnp.float32)
    _, acc, place = lax.fori_loop(
        0,
        64,
        forward,
        ((zero + 1.0,) * 4, (zero,) * 12, jnp.zeros((8, LANES), jnp.int32)),
    )
    residual = []
    for h in range(2):
        for p in range(2):
            for ch in range(3):
                wanted = target_ref[pl.ds(6 * h + 2 * ch + p, 8, stride=12), :]
                residual.append(acc[3 * (2 * h + p) + ch] - wanted)

    def backward(i, carried):
        e = 63 - i
        behind = list(carried)
        for h in range(2):
            index = jnp.full((8, LANES), h * 64, jnp.int32) + e
            c_0, c_1, c_2, alpha_max = (pick(array, index) for array in ahead[5:9])
            for p in range(2):
                n = 2 * h + p
                bell = gauss[e, n]
                before = trans[e, n]
                alpha = alpha_max * bell
                shade = (
                    c_0 * residual[3 * n] + c_1 * residual[3 * n + 1] + c_2 * residual[3 * n + 2]
                )
                gap = shade - behind[n]
                behind[n] = behind[n] + alpha * gap
                start = pl.multiple_of(512 * h + 8 * e, 8)
                gauss_grad[p, pl.ds(start, 8), :] = before * gap * bell
                weight[p, pl.ds(start, 8), :] = alpha * before
        return tuple(behind)

    lax.fori_loop(0, 64, backward, (zero,) * 4)

    pix = row_ids(LANES)
    col = lane_ids(LANES)
    for_moments, for_colors = [], []
    for p in range(2):
        u = lax.rem(pix, 16).astype(jnp.float32) - 7.5
        v = (pix // 16 + 8 * p).astype(jnp.float32) - 7.5
        powers = [jnp.ones_like(u), u, v, u * u, u * v, v * v]
        table = jnp.zeros_like(u)
        for m, power in enumerate(powers):
            table = jnp.where(col == m, power, table)
        for_moments.append(table)
        stacked = [zero]
        for ch in range(3):
            for h in range(2):
                stacked.append(residual[3 * (2 * h + p) + ch])
        stacked += [zero] * 9
        for_colors.append(jnp.concatenate(stacked, axis=0).T)

    for k in range(8):
        rows = pl.ds(k, LANES, stride=8)
        total = (
            dot(gauss_grad[0, rows, :], for_moments[0])
            + dot(gauss_grad[1, rows, :], for_moments[1])
            + dot(weight[0, rows, :], for_colors[0])
            + dot(weight[1, rows, :], for_colors[1])
        )
        sums[64 * k : 64 * k + 64, :] = total.T[0:64, :]

    s_0, s_u, s_v, s_uu, s_uv, s_vv = (sums[pl.ds(m, 8, stride=64), :] for m in range(6))
    d_colors = []
    for ch in range(3):
        even = sums[pl.ds(8 + 16 * ch, 8, stride=65), :]
        odd = sums[pl.ds(16 + 16 * ch, 8, stride=65), :]
        d_colors.append(jnp.where(half_of == 0, even, odd))
    m_u = opacity * (s_u - mean_u * s_0)
    m_v = opacity * (s_v - mean_v * s_0)
    m_uu = opacity * (s_uu - mean_u * (2.0 * s_u - mean_u * s_0))
    m_vv = opacity * (s_vv - mean_v * (2.0 * s_v - mean_v * s_0))
    m_uv = opacity * (s_uv - mean_u * s_v - mean_v * (s_u - mean_u * s_0))
    grads = [
        -WIDTH * (2.0 * quad_a * m_u + quad_b * m_v),
        -HEIGHT * (2.0 * quad_c * m_v + quad_b * m_u),
        (-0.5 / (WIDTH * WIDTH)) * m_uu,
        (-1.0 / (WIDTH * HEIGHT)) * m_uv,
        (-0.5 / (HEIGHT * HEIGHT)) * m_vv,
        *d_colors,
        jnp.where(active, s_0, 0.0),
    ]
    for h in range(2):
        for o in range(8):
            base = h * 64 + o * 8 + lax.rem(lane, 8)
            index = h * 64 + pick(place, base)
            message = zero
            for f in range(FEATS):
                message = jnp.where(lane // 8 == f, pick(grads[f], index), message)
            out_ref[pl.ds(8 * h + o, 8, stride=16), :] = message


def step_sizes(rows):
    return jnp.where(
        rows < 3,
        0.00016,
        jnp.where(
            rows < 6,
            0.005,
            jnp.where(
                rows < 10,
                0.001,
                jnp.where(rows < 11, 0.05, jnp.where(rows < 14, 0.0025, 0.000125)),
            ),
        ),
    )


def update_kernel(
    centers_ref,
    order_ref,
    rows_ref,
    returned_ref,
    params_ref,
    first_ref,
    second_ref,
    new_params_ref,
    new_first_ref,
    new_second_ref,
    leaving_ref,
    dense,
    grads,
    by_slot,
    staged,
    before,
    after,
):
    fill_dense(params_ref, dense)
    lane = lane_ids()
    place = jnp.zeros((PADDED, LANES), jnp.float32)
    sub_high = row_ids(32)
    sub_low = row_ids(LANES)
    lane_value = lane_ids(32).astype(jnp.float32)
    for i in range(32):
        rows = rows_ref[i : i + 1, :]
        hit = sub_high == jnp.broadcast_to(rows // LANES, (32, LANES))
        left = jnp.concatenate(
            [jnp.where(hit, float(i), 0.0), jnp.where(hit, lane_value, 0.0)], axis=0
        )
        right = jnp.where(
            sub_low == jnp.broadcast_to(lax.rem(rows, LANES), (LANES, LANES)), 1.0, 0.0
        )
        place = place + lax.dot_general(
            left.astype(jnp.bfloat16),
            right.astype(jnp.bfloat16),
            (((1,), (1,)), ((), ())),
            preferred_element_type=jnp.float32,
        )
    place_high = (place[0:32] + 0.5).astype(jnp.int32)
    place_low = (place[32:64] + 0.5).astype(jnp.int32)
    for view in range(4):
        values = [jnp.zeros((8, LANES), jnp.float32)] * FEATS
        for o in range(16):
            block = returned_ref[view, pl.ds(o, 8, stride=16), :]
            chosen = lane // 8 == o
            for f in range(FEATS):
                values[f] = jnp.where(chosen, pick(block, 8 * f + lax.rem(lane, 8)), values[f])
        for f in range(FEATS):
            by_slot[f, 8 * view : 8 * view + 8, :] = values[f]
    sizes = step_sizes(row_ids(PADDED)[0:PARAMS])
    for chunk in range(4):
        high = place_high[8 * chunk : 8 * chunk + 8]
        low = place_low[8 * chunk : 8 * chunk + 8]

        def collect(h, values):
            chosen = high == h
            return tuple(
                jnp.where(
                    chosen,
                    pick(jnp.broadcast_to(by_slot[f, pl.ds(h, 1), :], (8, LANES)), low),
                    values[f],
                )
                for f in range(FEATS)
            )

        feat_grads = lax.fori_loop(
            0, 32, collect, (jnp.zeros((8, LANES), jnp.float32),) * FEATS
        )
        view = high // 8
        center = []
        for i in range(3):
            at = jnp.zeros((8, LANES), jnp.float32)
            for v in range(4):
                at = jnp.where(view == v, centers_ref[v, i], at)
            center.append(at)
        values = [dense_at(dense, chunk, p) for p in range(PARAMS)]
        _, pull_back = jax.vjp(lambda *args: project(args, center), *values)
        for p, grad in enumerate(pull_back(list(feat_grads))):
            grads[pl.ds(chunk * 8 * PADDED + p, 8, stride=PADDED), :] = grad

    bias_one = 1.0 - BETA_ONE**ADAM_STEP
    bias_two = 1.0 - BETA_TWO**ADAM_STEP
    staged[...] = jnp.zeros_like(staged)

    def adam(j, carried):
        columns = pl.ds(pl.multiple_of(j * LANES, LANES), LANES)
        gradient = grads[pl.ds(pl.multiple_of(j * PADDED, PADDED), PADDED), :][0:PARAMS]
        new_one = BETA_ONE * first_ref[:, columns] + (1.0 - BETA_ONE) * gradient
        new_two = BETA_TWO * second_ref[:, columns] + (1.0 - BETA_TWO) * gradient * gradient
        updated = params_ref[:, columns] - sizes * (new_one / bias_one) / (
            jnp.sqrt(new_two / bias_two) + ADAM_EPS
        )
        staged[0:PARAMS, :] = updated
        staged[PADDED : PADDED + PARAMS, :] = new_one
        staged[2 * PADDED : 2 * PADDED + PARAMS, :] = new_two
        before[columns, 0:LANES] = staged[0:LANES, :].T
        before[columns, LANES : 2 * LANES] = staged[LANES : 2 * LANES, :].T
        return carried

    lax.fori_loop(0, 32, adam, 0)

    def move(t, carried):
        for u in range(16):
            row = order_ref[t * 16 + u]
            after[pl.ds(t * 16 + u, 1), :] = before[pl.ds(row, 1), :]
        return carried

    lax.fori_loop(0, 256, move, 0)
    leaving_ref[...] = after[3968:4096, :]
    for j in range(31):
        write_columns(
            after[LANES * j : LANES * (j + 1), :],
            slice(LANES * j, LANES * (j + 1)),
            new_params_ref,
            new_first_ref,
            new_second_ref,
        )


def write_columns(rows, columns, new_params_ref, new_first_ref, new_second_ref):
    both = rows[:, 0:LANES].T
    new_params_ref[:, columns] = both[0:PARAMS, :]
    new_first_ref[:, columns] = both[PADDED : PADDED + PARAMS, :]
    new_second_ref[:, columns] = rows[:, LANES : 2 * LANES].T[0:PARAMS, :]


def arrive_kernel(rows_ref, p_in, f_in, s_in, new_params_ref, new_first_ref, new_second_ref):
    del p_in, f_in, s_in
    write_columns(
        rows_ref[...], slice(0, LANES), new_params_ref, new_first_ref, new_second_ref
    )


VMEM = pl.BlockSpec(memory_space=pltpu.VMEM)
SMEM = pl.BlockSpec(memory_space=pltpu.SMEM)
WIDE = pltpu.CompilerParams(vmem_limit_bytes=48 * 1024 * 1024)


def f32(*shape):
    return jax.ShapeDtypeStruct(shape, jnp.float32)


def scratch(*shape):
    return pltpu.VMEM(shape, jnp.float32)


def per_device(
    params,
    first_moment,
    second_moment,
    cam_centers,
    target,
    send_rows,
    tile_lists,
    tile_counts,
    tile_ids,
    move_order,
):
    own_rows = send_rows.reshape(8, LANES)
    packed = jnp.concatenate(
        [own_rows.astype(jnp.float32), jnp.pad(cam_centers, ((0, 0), (0, LANES - 3)))], axis=0
    )
    packed_all = lax.all_gather(packed, "view")
    rows_all = packed_all[:, 0:8].reshape(32, LANES).astype(jnp.int32)
    centers_all = packed_all[:, 8, 0:3]

    outgoing = pl.pallas_call(
        project_kernel,
        out_shape=f32(LANES, LANES),
        in_specs=[SMEM, VMEM, VMEM],
        out_specs=VMEM,
        scratch_shapes=[scratch(32 * PADDED, LANES), scratch(FEATS, 32, LANES)],
        compiler_params=WIDE,
        name="project",
    )(cam_centers, own_rows, params)
    arrived = lax.all_to_all(outgoing, "dev", split_axis=0, concat_axis=0, tiled=True)

    def spread(array):
        return jnp.repeat(array.reshape(8, 2), 64, axis=1)

    slot_grads = pl.pallas_call(
        render_kernel,
        out_shape=f32(LANES, LANES),
        in_specs=[VMEM] * 5,
        out_specs=VMEM,
        scratch_shapes=[
            scratch(64, 4, 8, LANES),
            scratch(64, 4, 8, LANES),
            scratch(2, 1024, LANES),
            scratch(2, 1024, LANES),
            scratch(512, LANES),
        ],
        compiler_params=WIDE,
        name="render",
    )(
        arrived,
        tile_lists.reshape(8, LANES),
        spread(tile_counts),
        spread(tile_ids),
        target.reshape(96, LANES),
    )
    returned = lax.all_to_all(slot_grads, "dev", split_axis=0, concat_axis=0, tiled=True)
    returned_all = lax.all_gather(returned, "view")
    new_params, new_first, new_second, leaving = pl.pallas_call(
        update_kernel,
        out_shape=(f32(PARAMS, 4096),) * 3 + (f32(LANES, 2 * LANES),),
        in_specs=[SMEM, SMEM] + [VMEM] * 5,
        out_specs=(VMEM,) * 4,
        scratch_shapes=[
            scratch(32 * PADDED, LANES),
            scratch(32 * PADDED, LANES),
            scratch(FEATS, 32, LANES),
            scratch(2 * LANES, LANES),
            scratch(4096, 2 * LANES),
            scratch(4096, 2 * LANES),
        ],
        compiler_params=WIDE,
        name="update",
    )(
        centers_all,
        move_order.reshape(4096),
        rows_all,
        returned_all,
        params,
        first_moment,
        second_moment,
    )
    arriving = lax.all_to_all(leaving, "dev", split_axis=0, concat_axis=0, tiled=True)
    last = pl.BlockSpec((PARAMS, LANES), lambda i: (0, 31))
    whole = pl.BlockSpec(memory_space=pl.ANY)
    return pl.pallas_call(
        arrive_kernel,
        grid=(1,),
        out_shape=(f32(PARAMS, 4096),) * 3,
        in_specs=[pl.BlockSpec((LANES, 2 * LANES), lambda i: (0, 0)), whole, whole, whole],
        out_specs=(last,) * 3,
        input_output_aliases={1: 0, 2: 1, 3: 2},
        name="arrive",
    )(arriving, new_params, new_first, new_second)


def solution(mesh):
    placed = (
        P(None, "dev"),
        P(None, "dev"),
        P(None, "dev"),
        P("view", None),
        P("view", "dev", None, None),
        P("view", "dev", None),
        P("view", "dev", None),
        P("view", "dev"),
        P("view", "dev"),
        P("dev", None),
    )
    return jax.shard_map(
        per_device,
        mesh=mesh,
        in_specs=placed,
        out_specs=(P(None, "dev"), P(None, "dev"), P(None, "dev")),
        check_vma=False,
    )
```

```python
import functools

import jax
import jax.numpy as jnp
from jax import lax
from jax.experimental import pallas as pl
from jax.experimental.pallas import tpu as pltpu
from jax.sharding import PartitionSpec as P

PARAMS = 59
PADDED = 64
FEATS = 9
LANES = 128
TILE_SIDE = 16
TILES_X = 64
ADAM_STEP = 1000
FOCAL_LEN = 1.2
DILATION = 0.3
SH_C0 = 0.28209479177387814
SH_C1 = 0.4886025119029199
SH_C2 = (
    1.0925484305920792,
    -1.0925484305920792,
    0.31539156525252005,
    -1.0925484305920792,
    0.5462742152960396,
)
SH_C3 = (
    -0.5900435899266435,
    2.890611442640554,
    -0.4570457994644658,
    0.3731763325901154,
    -0.4570457994644658,
    1.445305721320277,
    -0.5900435899266435,
)
BETA_ONE = 0.9
BETA_TWO = 0.999
ADAM_EPS = 1e-08
MESH = pl.DeviceIdType.MESH
WIDTH = 1024.0
HEIGHT = 512.0


def sh_basis(x, y, z):
    xx, yy, zz = x * x, y * y, z * z
    return [
        SH_C0 + 0.0 * x,
        -SH_C1 * y,
        SH_C1 * z,
        -SH_C1 * x,
        SH_C2[0] * x * y,
        SH_C2[1] * y * z,
        SH_C2[2] * (2.0 * zz - xx - yy),
        SH_C2[3] * x * z,
        SH_C2[4] * (xx - yy),
        SH_C3[0] * y * (3.0 * xx - yy),
        SH_C3[1] * x * y * z,
        SH_C3[2] * y * (4.0 * zz - xx - yy),
        SH_C3[3] * z * (2.0 * zz - 3.0 * xx - 3.0 * yy),
        SH_C3[4] * x * (4.0 * zz - xx - yy),
        SH_C3[5] * z * (xx - yy),
        SH_C3[6] * x * (xx - 3.0 * yy),
    ]


def project(values, center):
    off = [values[i] - center[i] for i in range(3)]
    inverse = 1.0 / off[2]
    mean_u = 0.5 + FOCAL_LEN * off[0] * inverse
    mean_v = 0.5 + FOCAL_LEN * off[1] * inverse
    scale_sq = [jnp.exp(2.0 * values[3 + i]) for i in range(3)]
    quat = values[6:10]
    norm = lax.rsqrt(
        quat[0] * quat[0] + quat[1] * quat[1] + quat[2] * quat[2] + quat[3] * quat[3]
    )
    w, x, y, z = (q * norm for q in quat)
    rotation = [
        [1.0 - 2.0 * (y * y + z * z), 2.0 * (x * y - w * z), 2.0 * (x * z + w * y)],
        [2.0 * (x * y + w * z), 1.0 - 2.0 * (x * x + z * z), 2.0 * (y * z - w * x)],
        [2.0 * (x * z - w * y), 2.0 * (y * z + w * x), 1.0 - 2.0 * (x * x + y * y)],
    ]
    focal_now = FOCAL_LEN * inverse
    slope_u = -focal_now * off[0] * inverse
    slope_v = -focal_now * off[1] * inverse
    cov_uu = DILATION / (WIDTH * WIDTH)
    cov_vv = DILATION / (HEIGHT * HEIGHT)
    cov_uv = 0.0
    for c in range(3):
        axis_u = focal_now * rotation[0][c] + slope_u * rotation[2][c]
        axis_v = focal_now * rotation[1][c] + slope_v * rotation[2][c]
        cov_uu = cov_uu + axis_u * axis_u * scale_sq[c]
        cov_vv = cov_vv + axis_v * axis_v * scale_sq[c]
        cov_uv = cov_uv + axis_u * axis_v * scale_sq[c]
    inv_det = 1.0 / (cov_uu * cov_vv - cov_uv * cov_uv)
    inv_dist = 1.0 / jnp.sqrt(off[0] * off[0] + off[1] * off[1] + off[2] * off[2])
    basis = sh_basis(off[0] * inv_dist, off[1] * inv_dist, off[2] * inv_dist)
    colors = []
    for ch in range(3):
        total = basis[0] * values[11 + ch]
        for k in range(1, 16):
            total = total + basis[k] * values[11 + 3 * k + ch]
        colors.append(0.5 + total)
    opacity = 1.0 / (1.0 + jnp.exp(-values[10]))
    return [
        mean_u,
        mean_v,
        cov_vv * inv_det,
        -cov_uv * inv_det,
        cov_uu * inv_det,
        *colors,
        opacity,
    ]


def pick(array, index):
    return jnp.take_along_axis(array, index, axis=1, mode="promise_in_bounds")


def lane_ids(rows=8):
    return lax.broadcasted_iota(jnp.int32, (rows, LANES), 1)


def row_ids(rows=8):
    return lax.broadcasted_iota(jnp.int32, (rows, LANES), 0)


def fill_dense(array_ref, dense_ref):
    for j in range(32):
        dense_ref[PADDED * j : PADDED * j + PARAMS, :] = array_ref[
            :, LANES * j : LANES * (j + 1)
        ]


def dense_at(dense_ref, chunk, row):
    return dense_ref[pl.ds(chunk * 8 * PADDED + row, 8, stride=PADDED), :]


def greet(views, owners):
    view, me = lax.axis_index("view"), lax.axis_index("dev")
    barrier = pltpu.get_barrier_semaphore()
    for i in range(1, views):
        pl.semaphore_signal(
            barrier, inc=1, device_id=(lax.rem(view + i, views), me), device_id_type=MESH
        )

    def signal(i, carried):
        pl.semaphore_signal(
            barrier, inc=1, device_id=(view, lax.rem(me + i, owners)), device_id_type=MESH
        )
        return carried

    lax.fori_loop(1, owners, signal, 0)
    return barrier, views + owners - 2


def send_each(owners, message, landing, send_sem, recv_sem):
    view, me = lax.axis_index("view"), lax.axis_index("dev")

    def send(i, carried):
        other = lax.rem(me + i, owners)
        pltpu.make_async_remote_copy(
            src_ref=message(other),
            dst_ref=landing(me),
            send_sem=send_sem,
            recv_sem=recv_sem,
            device_id=(view, other),
            device_id_type=MESH,
        ).start()
        return carried

    lax.fori_loop(1, owners, send, 0)


def send_views(views, block, landing, send_sem, recv_sem):
    view, me = lax.axis_index("view"), lax.axis_index("dev")
    for i in range(1, views):
        pltpu.make_async_remote_copy(
            src_ref=block,
            dst_ref=landing(view),
            send_sem=send_sem,
            recv_sem=recv_sem,
            device_id=(lax.rem(view + i, views), me),
            device_id_type=MESH,
        ).start()


def wait_bytes(ref, semaphore):
    pltpu.make_async_copy(ref, ref, semaphore).wait()


def project_kernel(
    views,
    owners,
    center_ref,
    packed_ref,
    rows_ref,
    params_ref,
    arrived_ref,
    packed_all_ref,
    dense,
    feats,
    outgoing,
    landed,
    packed_landed,
    sems,
):
    view, me = lax.axis_index("view"), lax.axis_index("dev")
    barrier, expected = greet(views, owners)
    fill_dense(params_ref, dense)
    center = [center_ref[0, i] for i in range(3)]
    for chunk in range(4):
        values = [dense_at(dense, chunk, p) for p in range(PARAMS)]
        for f, value in enumerate(project(values, center)):
            feats[f, 8 * chunk : 8 * chunk + 8, :] = value
    rows = rows_ref[...]
    high = rows // LANES
    low = lax.rem(rows, LANES)
    slots = [jnp.zeros((8, LANES), jnp.float32)] * FEATS
    for h in range(32):
        chosen = high == h
        for f in range(FEATS):
            source = jnp.broadcast_to(feats[f, h : h + 1, :], (8, LANES))
            slots[f] = jnp.where(chosen, pick(source, low), slots[f])
    lane = lane_ids()
    sub = row_ids()
    for block in range(16):
        index = ((block % 2) * 8 + sub) * 8 + lax.rem(lane, 8)
        message = jnp.zeros((8, LANES), jnp.float32)
        for f in range(FEATS):
            source = jnp.broadcast_to(slots[f][block // 2 : block // 2 + 1, :], (8, LANES))
            message = jnp.where(lane // 8 == f, pick(source, index), message)
        outgoing[8 * block : 8 * block + 8, :] = message
    pl.semaphore_wait(barrier, expected)
    send_each(
        owners,
        lambda d: outgoing.at[pl.ds(d, 1)],
        lambda d: landed.at[pl.ds(d, 1)],
        sems.at[0],
        sems.at[1],
    )
    send_views(views, packed_ref, lambda v: packed_landed.at[v], sems.at[2], sems.at[3])
    landed[pl.ds(me, 1), :] = outgoing[pl.ds(me, 1), :]
    packed_landed[view] = packed_ref[...]
    others = pl.ds(0, owners - 1)
    wait_bytes(landed.at[others], sems.at[1])
    wait_bytes(packed_landed.at[pl.ds(0, views - 1)], sems.at[3])
    arrived_ref[...] = landed[...]
    packed_all_ref[...] = packed_landed[...]
    wait_bytes(landed.at[others], sems.at[0])
    wait_bytes(packed_landed.at[pl.ds(0, views - 1)], sems.at[2])


def dot(a, b, dims=((1,), (0,))):
    return lax.dot_general(
        a,
        b,
        (dims, ((), ())),
        precision=lax.Precision.HIGHEST,
        preferred_element_type=jnp.float32,
    )


def render(
    arrived_ref,
    lists_ref,
    counts_ref,
    ids_ref,
    target_ref,
    out_ref,
    gauss,
    trans,
    gauss_grad,
    weight,
    sums,
):
    lane = lane_ids()
    sub = row_ids()
    half_of = lane // 64
    entry = lax.rem(lane, 64)
    slot = lax.rem(lists_ref[...], 64)
    from_owner = slot // 8
    within = lax.rem(slot, 8)
    feats = [jnp.zeros((8, LANES), jnp.float32)] * FEATS
    for h in range(2):
        for o in range(8):
            block = arrived_ref[pl.ds(8 * h + o, 8, stride=16), :]
            chosen = (from_owner == o) & (half_of == h)
            for f in range(FEATS):
                feats[f] = jnp.where(chosen, pick(block, 8 * f + within), feats[f])
    ids = ids_ref[...]
    center_u = (lax.rem(ids, TILES_X) * TILE_SIDE + TILE_SIDE // 2).astype(jnp.float32)
    center_v = (ids // TILES_X * TILE_SIDE + TILE_SIDE // 2).astype(jnp.float32)
    mean_u = feats[0] * WIDTH - center_u
    mean_v = feats[1] * HEIGHT - center_v
    quad_a = feats[2] * (-0.5 / (WIDTH * WIDTH))
    quad_b = feats[3] * (-1.0 / (WIDTH * HEIGHT))
    quad_c = feats[4] * (-0.5 / (HEIGHT * HEIGHT))
    active = entry < counts_ref[...]
    opacity = jnp.where(active, feats[8], 0.0)
    pixel_u = lax.rem(lane, 16).astype(jnp.float32) - 7.5
    pixel_v = [(lane // 16 + 8 * p).astype(jnp.float32) - 7.5 for p in range(2)]
    ahead = [mean_u, mean_v, quad_a, quad_b, quad_c, *feats[5:8], opacity]

    def forward(e, carried):
        through, acc, place = carried
        through, acc = list(through), list(acc)
        for h in range(2):
            index = jnp.full((8, LANES), h * 64, jnp.int32) + e
            m_u, m_v, q_a, q_b, q_c, c_0, c_1, c_2, alpha_max = (
                pick(array, index) for array in ahead
            )
            place = jnp.where((pick(slot, index) == entry) & (half_of == h), e, place)
            diff_u = pixel_u - m_u
            part = diff_u * q_b
            square = diff_u * diff_u * q_a
            for p in range(2):
                diff_v = pixel_v[p] - m_v
                bell = jnp.exp(square + diff_v * (part + q_c * diff_v))
                alpha = alpha_max * bell
                n = 2 * h + p
                before = through[n]
                gauss[e, n] = bell
                trans[e, n] = before
                share = alpha * before
                through[n] = before - share
                for ch, color in enumerate((c_0, c_1, c_2)):
                    acc[3 * n + ch] = acc[3 * n + ch] + color * share
        return tuple(through), tuple(acc), place

    zero = jnp.zeros((8, LANES), jnp.float32)
    _, acc, place = lax.fori_loop(
        0,
        64,
        forward,
        ((zero + 1.0,) * 4, (zero,) * 12, jnp.zeros((8, LANES), jnp.int32)),
        unroll=4,
    )
    residual = []
    for h in range(2):
        for p in range(2):
            for ch in range(3):
                wanted = target_ref[pl.ds(6 * h + 2 * ch + p, 8, stride=12), :]
                residual.append(acc[3 * (2 * h + p) + ch] - wanted)

    def backward(i, carried):
        e = 63 - i
        behind = list(carried)
        for h in range(2):
            index = jnp.full((8, LANES), h * 64, jnp.int32) + e
            c_0, c_1, c_2, alpha_max = (pick(array, index) for array in ahead[5:9])
            for p in range(2):
                n = 2 * h + p
                bell = gauss[e, n]
                before = trans[e, n]
                alpha = alpha_max * bell
                shade = (
                    c_0 * residual[3 * n] + c_1 * residual[3 * n + 1] + c_2 * residual[3 * n + 2]
                )
                gap = shade - behind[n]
                behind[n] = behind[n] + alpha * gap
                start = pl.multiple_of(512 * h + 8 * e, 8)
                gauss_grad[p, pl.ds(start, 8), :] = before * gap * bell
                weight[p, pl.ds(start, 8), :] = alpha * before
        return tuple(behind)

    lax.fori_loop(0, 64, backward, (zero,) * 4, unroll=4)

    pix = row_ids(LANES)
    col = lane_ids(LANES)
    for_moments, for_colors = [], []
    for p in range(2):
        u = lax.rem(pix, 16).astype(jnp.float32) - 7.5
        v = (pix // 16 + 8 * p).astype(jnp.float32) - 7.5
        powers = [jnp.ones_like(u), u, v, u * u, u * v, v * v]
        table = jnp.zeros_like(u)
        for m, power in enumerate(powers):
            table = jnp.where(col == m, power, table)
        for_moments.append(table)
        stacked = [zero]
        for ch in range(3):
            for h in range(2):
                stacked.append(residual[3 * (2 * h + p) + ch])
        stacked += [zero] * 9
        for_colors.append(jnp.concatenate(stacked, axis=0).T)

    for k in range(8):
        rows = pl.ds(k, LANES, stride=8)
        total = (
            dot(gauss_grad[0, rows, :], for_moments[0])
            + dot(gauss_grad[1, rows, :], for_moments[1])
            + dot(weight[0, rows, :], for_colors[0])
            + dot(weight[1, rows, :], for_colors[1])
        )
        sums[64 * k : 64 * k + 64, :] = total.T[0:64, :]

    s_0, s_u, s_v, s_uu, s_uv, s_vv = (sums[pl.ds(m, 8, stride=64), :] for m in range(6))
    d_colors = []
    for ch in range(3):
        even = sums[pl.ds(8 + 16 * ch, 8, stride=65), :]
        odd = sums[pl.ds(16 + 16 * ch, 8, stride=65), :]
        d_colors.append(jnp.where(half_of == 0, even, odd))
    m_u = opacity * (s_u - mean_u * s_0)
    m_v = opacity * (s_v - mean_v * s_0)
    m_uu = opacity * (s_uu - mean_u * (2.0 * s_u - mean_u * s_0))
    m_vv = opacity * (s_vv - mean_v * (2.0 * s_v - mean_v * s_0))
    m_uv = opacity * (s_uv - mean_u * s_v - mean_v * (s_u - mean_u * s_0))
    grads = [
        -WIDTH * (2.0 * quad_a * m_u + quad_b * m_v),
        -HEIGHT * (2.0 * quad_c * m_v + quad_b * m_u),
        (-0.5 / (WIDTH * WIDTH)) * m_uu,
        (-1.0 / (WIDTH * HEIGHT)) * m_uv,
        (-0.5 / (HEIGHT * HEIGHT)) * m_vv,
        *d_colors,
        jnp.where(active, s_0, 0.0),
    ]
    for h in range(2):
        for o in range(8):
            base = h * 64 + o * 8 + lax.rem(lane, 8)
            index = h * 64 + pick(place, base)
            message = zero
            for f in range(FEATS):
                message = jnp.where(lane // 8 == f, pick(grads[f], index), message)
            out_ref[pl.ds(8 * h + o, 8, stride=16), :] = message


def step_sizes(rows):
    return jnp.where(
        rows < 3,
        0.00016,
        jnp.where(
            rows < 6,
            0.005,
            jnp.where(
                rows < 10,
                0.001,
                jnp.where(rows < 11, 0.05, jnp.where(rows < 14, 0.0025, 0.000125)),
            ),
        ),
    )


def slot_places(rows_all):
    place = jnp.zeros((PADDED, LANES), jnp.float32)
    sub_high = row_ids(32)
    sub_low = row_ids(LANES)
    lane_value = lane_ids(32).astype(jnp.float32)
    for i in range(32):
        rows = rows_all[i // 8][i % 8 : i % 8 + 1, :]
        hit = sub_high == jnp.broadcast_to(rows // LANES, (32, LANES))
        left = jnp.concatenate(
            [jnp.where(hit, float(i), 0.0), jnp.where(hit, lane_value, 0.0)], axis=0
        )
        right = jnp.where(
            sub_low == jnp.broadcast_to(lax.rem(rows, LANES), (LANES, LANES)), 1.0, 0.0
        )
        place = place + lax.dot_general(
            left.astype(jnp.bfloat16),
            right.astype(jnp.bfloat16),
            (((1,), (1,)), ((), ())),
            preferred_element_type=jnp.float32,
        )
    return (place[0:32] + 0.5).astype(jnp.int32), (place[32:64] + 0.5).astype(jnp.int32)


def step_kernel(
    views,
    owners,
    order_ref,
    packed_ref,
    arrived_ref,
    lists_ref,
    counts_ref,
    ids_ref,
    target_ref,
    params_hbm,
    first_hbm,
    second_hbm,
    moved_a,
    moved_b,
    gauss,
    trans,
    gauss_grad,
    weight,
    sums,
    params_ref,
    first_ref,
    second_ref,
    slot_grads,
    returned,
    by_slot,
    dense,
    grads,
    before_a,
    before_b,
    leaving,
    arriving,
    load_sems,
    sems,
):
    view, me = lax.axis_index("view"), lax.axis_index("dev")
    barrier, expected = greet(views, owners)
    loads = [
        pltpu.make_async_copy(source, place, load_sems.at[i])
        for i, (source, place) in enumerate(
            ((params_hbm, params_ref), (first_hbm, first_ref), (second_hbm, second_ref))
        )
    ]
    for load in loads:
        load.start()
    lane = lane_ids()
    place_high, place_low = slot_places(
        [packed_ref[v, 0:8, :].astype(jnp.int32) for v in range(views)]
    )
    render(
        arrived_ref,
        lists_ref,
        counts_ref,
        ids_ref,
        target_ref,
        slot_grads,
        gauss,
        trans,
        gauss_grad,
        weight,
        sums,
    )
    pl.semaphore_wait(barrier, expected)
    send_each(
        owners,
        lambda d: slot_grads.at[pl.ds(d, 1)],
        lambda d: returned.at[pl.ds(d, 1)],
        sems.at[0],
        sems.at[1],
    )
    returned[pl.ds(me, 1), :] = slot_grads[pl.ds(me, 1), :]
    for load in loads:
        load.wait()
    fill_dense(params_ref, dense)
    wait_bytes(returned.at[pl.ds(0, owners - 1)], sems.at[1])

    values = [jnp.zeros((8, LANES), jnp.float32)] * FEATS
    for o in range(16):
        block = returned[pl.ds(o, 8, stride=16), :]
        chosen = lane // 8 == o
        for f in range(FEATS):
            values[f] = jnp.where(chosen, pick(block, 8 * f + lax.rem(lane, 8)), values[f])
    for f in range(FEATS):
        by_slot[view, 8 * f : 8 * f + 8, :] = values[f]
    send_views(views, by_slot.at[view], lambda v: by_slot.at[v], sems.at[2], sems.at[3])
    wait_bytes(by_slot.at[pl.ds(0, views - 1)], sems.at[3])

    sizes = step_sizes(row_ids(PADDED)[0:PARAMS])
    for pair in range(2):
        chunks = (2 * pair, 2 * pair + 1)
        high = [place_high[8 * c : 8 * c + 8] for c in chunks]
        low = [place_low[8 * c : 8 * c + 8] for c in chunks]
        totals = ((jnp.zeros((8, LANES), jnp.float32),) * FEATS,) * 2
        for v in range(views):

            def collect(k, totals):
                chosen = [h == 8 * v + k for h in high]
                found = []
                sources = [
                    jnp.broadcast_to(by_slot[v, pl.ds(8 * f + k, 1), :], (8, LANES))
                    for f in range(FEATS)
                ]
                for c in range(2):
                    found.append(
                        tuple(
                            jnp.where(chosen[c], pick(sources[f], low[c]), totals[c][f])
                            for f in range(FEATS)
                        )
                    )
                return tuple(found)

            totals = lax.fori_loop(0, 8, collect, totals, unroll=4)
        for c in range(2):
            chunk = chunks[c]
            owner_view = high[c] // 8
            center = []
            for i in range(3):
                at = jnp.zeros((8, LANES), jnp.float32)
                for v in range(views):
                    at = jnp.where(
                        owner_view == v,
                        jnp.broadcast_to(packed_ref[v, 8:9, i : i + 1], (8, LANES)),
                        at,
                    )
                center.append(at)
            arguments = [dense_at(dense, chunk, p) for p in range(PARAMS)]
            _, pull_back = jax.vjp(lambda *args: project(args, center), *arguments)
            for p, grad in enumerate(pull_back(list(totals[c]))):
                grads[pl.ds(chunk * 8 * PADDED + p, 8, stride=PADDED), :] = grad

    bias_one = 1.0 - BETA_ONE**ADAM_STEP
    bias_two = 1.0 - BETA_TWO**ADAM_STEP
    fill = jnp.zeros((PADDED - PARAMS, LANES), jnp.float32)
    empty = jnp.zeros((PADDED, LANES), jnp.float32)

    def adam(j, carried):
        columns = pl.ds(pl.multiple_of(j * LANES, LANES), LANES)
        gradient = grads[pl.ds(pl.multiple_of(j * PADDED, PADDED), PADDED), :][0:PARAMS]
        new_one = BETA_ONE * first_ref[:, columns] + (1.0 - BETA_ONE) * gradient
        new_two = BETA_TWO * second_ref[:, columns] + (1.0 - BETA_TWO) * gradient * gradient
        updated = params_ref[:, columns] - sizes * (new_one / bias_one) / (
            jnp.sqrt(new_two / bias_two) + ADAM_EPS
        )
        before_a[columns, :] = jnp.concatenate([updated, fill, new_one, fill], axis=0).T
        before_b[columns, :] = jnp.concatenate([new_two, fill, empty], axis=0).T
        return carried

    lax.fori_loop(0, 32, adam, 0, unroll=4)

    kept = order_ref.shape[0] - owners
    for t in range(owners):
        row = order_ref[kept + t]
        leaving[0, t : t + 1, :] = before_a[pl.ds(row, 1), :]
        leaving[1, t : t + 1, :] = before_b[pl.ds(row, 1), :]
    send_each(
        owners,
        lambda d: leaving.at[:, pl.ds(d, 1)],
        lambda d: arriving.at[:, pl.ds(d, 1)],
        sems.at[4],
        sems.at[5],
    )
    arriving[:, pl.ds(me, 1), :] = leaving[:, pl.ds(me, 1), :]

    def move(t, carried):
        for u in range(32):
            row = order_ref[t * 32 + u]
            moved_a[pl.ds(t * 32 + u, 1), :] = before_a[pl.ds(row, 1), :]
            moved_b[pl.ds(t * 32 + u, 1), :] = before_b[pl.ds(row, 1), :]
        return carried

    lax.fori_loop(0, kept // 32, move, 0)
    others = pl.ds(0, owners - 1)
    wait_bytes(arriving.at[:, others], sems.at[5])
    moved_a[kept:, :] = arriving[0]
    moved_b[kept:, :] = arriving[1]
    wait_bytes(returned.at[others], sems.at[0])
    wait_bytes(by_slot.at[pl.ds(0, views - 1)], sems.at[2])
    wait_bytes(arriving.at[:, others], sems.at[4])


def write_kernel(moved_a, moved_b, new_params_ref, new_first_ref, new_second_ref):
    for j in range(moved_a.shape[0] // LANES):
        columns = slice(LANES * j, LANES * (j + 1))
        both = moved_a[columns, :].T
        new_params_ref[:, columns] = both[0:PARAMS, :]
        new_first_ref[:, columns] = both[PADDED : PADDED + PARAMS, :]
        new_second_ref[:, columns] = moved_b[columns, :].T[0:PARAMS, :]


VMEM = pl.BlockSpec(memory_space=pltpu.VMEM)
SMEM = pl.BlockSpec(memory_space=pltpu.SMEM)
ANY = pl.BlockSpec(memory_space=pl.ANY)
VMEM_BYTES = 48 * 1024 * 1024


def f32(*shape):
    return jax.ShapeDtypeStruct(shape, jnp.float32)


def scratch(*shape):
    return pltpu.VMEM(shape, jnp.float32)


def per_device(
    params,
    first_moment,
    second_moment,
    cam_centers,
    target,
    send_rows,
    tile_lists,
    tile_counts,
    tile_ids,
    move_order,
):
    views, owners = lax.axis_size("view"), lax.axis_size("dev")
    own_rows = send_rows.reshape(8, LANES)
    packed = jnp.concatenate(
        [own_rows.astype(jnp.float32), jnp.pad(cam_centers, ((0, 7), (0, LANES - 3)))], axis=0
    )
    arrived, packed_all = pl.pallas_call(
        functools.partial(project_kernel, views, owners),
        out_shape=(f32(owners, LANES), f32(views, 16, LANES)),
        in_specs=[SMEM, VMEM, VMEM, VMEM],
        out_specs=(VMEM, VMEM),
        scratch_shapes=[
            scratch(32 * PADDED, LANES),
            scratch(FEATS, 32, LANES),
            scratch(owners, LANES),
            scratch(owners, LANES),
            scratch(views, 16, LANES),
            pltpu.SemaphoreType.DMA((4,)),
        ],
        compiler_params=pltpu.CompilerParams(
            vmem_limit_bytes=VMEM_BYTES, collective_id=0, has_side_effects=True
        ),
        name="project",
    )(cam_centers, packed, own_rows, params)

    def spread(array):
        return jnp.repeat(array.reshape(8, 2), 64, axis=1)

    moved = pl.pallas_call(
        functools.partial(step_kernel, views, owners),
        out_shape=(f32(4096, LANES),) * 2,
        in_specs=[SMEM] + [VMEM] * 6 + [ANY] * 3,
        out_specs=(VMEM,) * 2,
        scratch_shapes=[
            scratch(64, 4, 8, LANES),
            scratch(64, 4, 8, LANES),
            scratch(2, 1024, LANES),
            scratch(2, 1024, LANES),
            scratch(512, LANES),
            scratch(PARAMS, 4096),
            scratch(PARAMS, 4096),
            scratch(PARAMS, 4096),
            scratch(owners, LANES),
            scratch(owners, LANES),
            scratch(views, 8 * FEATS, LANES),
            scratch(32 * PADDED, LANES),
            scratch(32 * PADDED, LANES),
            scratch(4096, LANES),
            scratch(4096, LANES),
            scratch(2, owners, LANES),
            scratch(2, owners, LANES),
            pltpu.SemaphoreType.DMA((3,)),
            pltpu.SemaphoreType.DMA((6,)),
        ],
        compiler_params=pltpu.CompilerParams(
            vmem_limit_bytes=VMEM_BYTES, collective_id=1, has_side_effects=True
        ),
        name="step",
    )(
        move_order.reshape(4096),
        packed_all,
        arrived,
        tile_lists.reshape(8, LANES),
        spread(tile_counts),
        spread(tile_ids),
        target.reshape(96, LANES),
        params,
        first_moment,
        second_moment,
    )
    return pl.pallas_call(
        write_kernel,
        grid=(4,),
        out_shape=(f32(PARAMS, 4096),) * 3,
        in_specs=[pl.BlockSpec((1024, LANES), lambda i: (i, 0))] * 2,
        out_specs=(pl.BlockSpec((PARAMS, 1024), lambda i: (0, i)),) * 3,
        name="write",
    )(*moved)


def solution(mesh):
    placed = (
        P(None, "dev"),
        P(None, "dev"),
        P(None, "dev"),
        P("view", None),
        P("view", "dev", None, None),
        P("view", "dev", None),
        P("view", "dev", None),
        P("view", "dev"),
        P("view", "dev"),
        P("dev", None),
    )
    return jax.shard_map(
        per_device,
        mesh=mesh,
        in_specs=placed,
        out_specs=(P(None, "dev"), P(None, "dev"), P(None, "dev")),
        check_vma=False,
    )
```

```python
import functools

import jax
import jax.numpy as jnp
from jax import lax
from jax.experimental import pallas as pl
from jax.experimental.pallas import tpu as pltpu
from jax.sharding import PartitionSpec as P

PARAMS = 59
PADDED = 64
FEATS = 9
LANES = 128
TILE_SIDE = 16
TILES_X = 64
ADAM_STEP = 1000
FOCAL_LEN = 1.2
DILATION = 0.3
SH_C0 = 0.28209479177387814
SH_C1 = 0.4886025119029199
SH_C2 = (
    1.0925484305920792,
    -1.0925484305920792,
    0.31539156525252005,
    -1.0925484305920792,
    0.5462742152960396,
)
SH_C3 = (
    -0.5900435899266435,
    2.890611442640554,
    -0.4570457994644658,
    0.3731763325901154,
    -0.4570457994644658,
    1.445305721320277,
    -0.5900435899266435,
)
BETA_ONE = 0.9
BETA_TWO = 0.999
ADAM_EPS = 1e-08
MESH = pl.DeviceIdType.MESH
MOVED_EARLY = 1984
WIDTH = 1024.0
HEIGHT = 512.0


def sh_basis(x, y, z):
    xx, yy, zz = x * x, y * y, z * z
    return [
        SH_C0 + 0.0 * x,
        -SH_C1 * y,
        SH_C1 * z,
        -SH_C1 * x,
        SH_C2[0] * x * y,
        SH_C2[1] * y * z,
        SH_C2[2] * (2.0 * zz - xx - yy),
        SH_C2[3] * x * z,
        SH_C2[4] * (xx - yy),
        SH_C3[0] * y * (3.0 * xx - yy),
        SH_C3[1] * x * y * z,
        SH_C3[2] * y * (4.0 * zz - xx - yy),
        SH_C3[3] * z * (2.0 * zz - 3.0 * xx - 3.0 * yy),
        SH_C3[4] * x * (4.0 * zz - xx - yy),
        SH_C3[5] * z * (xx - yy),
        SH_C3[6] * x * (xx - 3.0 * yy),
    ]


def project(values, center):
    off = [values[i] - center[i] for i in range(3)]
    inverse = 1.0 / off[2]
    mean_u = 0.5 + FOCAL_LEN * off[0] * inverse
    mean_v = 0.5 + FOCAL_LEN * off[1] * inverse
    scale_sq = [jnp.exp(2.0 * values[3 + i]) for i in range(3)]
    quat = values[6:10]
    norm = lax.rsqrt(
        quat[0] * quat[0] + quat[1] * quat[1] + quat[2] * quat[2] + quat[3] * quat[3]
    )
    w, x, y, z = (q * norm for q in quat)
    rotation = [
        [1.0 - 2.0 * (y * y + z * z), 2.0 * (x * y - w * z), 2.0 * (x * z + w * y)],
        [2.0 * (x * y + w * z), 1.0 - 2.0 * (x * x + z * z), 2.0 * (y * z - w * x)],
        [2.0 * (x * z - w * y), 2.0 * (y * z + w * x), 1.0 - 2.0 * (x * x + y * y)],
    ]
    focal_now = FOCAL_LEN * inverse
    slope_u = -focal_now * off[0] * inverse
    slope_v = -focal_now * off[1] * inverse
    cov_uu = DILATION / (WIDTH * WIDTH)
    cov_vv = DILATION / (HEIGHT * HEIGHT)
    cov_uv = 0.0
    for c in range(3):
        axis_u = focal_now * rotation[0][c] + slope_u * rotation[2][c]
        axis_v = focal_now * rotation[1][c] + slope_v * rotation[2][c]
        cov_uu = cov_uu + axis_u * axis_u * scale_sq[c]
        cov_vv = cov_vv + axis_v * axis_v * scale_sq[c]
        cov_uv = cov_uv + axis_u * axis_v * scale_sq[c]
    inv_det = 1.0 / (cov_uu * cov_vv - cov_uv * cov_uv)
    inv_dist = 1.0 / jnp.sqrt(off[0] * off[0] + off[1] * off[1] + off[2] * off[2])
    basis = sh_basis(off[0] * inv_dist, off[1] * inv_dist, off[2] * inv_dist)
    colors = []
    for ch in range(3):
        total = basis[0] * values[11 + ch]
        for k in range(1, 16):
            total = total + basis[k] * values[11 + 3 * k + ch]
        colors.append(0.5 + total)
    opacity = 1.0 / (1.0 + jnp.exp(-values[10]))
    return [
        mean_u,
        mean_v,
        cov_vv * inv_det,
        -cov_uv * inv_det,
        cov_uu * inv_det,
        *colors,
        opacity,
    ]


def pick(array, index):
    return jnp.take_along_axis(array, index, axis=1, mode="promise_in_bounds")


def lane_ids(rows=8):
    return lax.broadcasted_iota(jnp.int32, (rows, LANES), 1)


def row_ids(rows=8):
    return lax.broadcasted_iota(jnp.int32, (rows, LANES), 0)


def fill_dense(array_ref, dense_ref):
    for j in range(32):
        dense_ref[PADDED * j : PADDED * j + PARAMS, :] = array_ref[
            :, LANES * j : LANES * (j + 1)
        ]


def dense_at(dense_ref, chunk, row):
    return dense_ref[pl.ds(chunk * 8 * PADDED + row, 8, stride=PADDED), :]


def greet(views, owners):
    view, me = lax.axis_index("view"), lax.axis_index("dev")
    barrier = pltpu.get_barrier_semaphore()
    for i in range(1, views):
        pl.semaphore_signal(
            barrier, inc=1, device_id=(lax.rem(view + i, views), me), device_id_type=MESH
        )

    def signal(i, carried):
        pl.semaphore_signal(
            barrier, inc=1, device_id=(view, lax.rem(me + i, owners)), device_id_type=MESH
        )
        return carried

    lax.fori_loop(1, owners, signal, 0)
    return barrier, views + owners - 2


def send_each(owners, message, landing, send_sem, recv_sem):
    view, me = lax.axis_index("view"), lax.axis_index("dev")

    def send(i, carried):
        other = lax.rem(me + i, owners)
        pltpu.make_async_remote_copy(
            src_ref=message(other),
            dst_ref=landing(me),
            send_sem=send_sem,
            recv_sem=recv_sem,
            device_id=(view, other),
            device_id_type=MESH,
        ).start()
        return carried

    lax.fori_loop(1, owners, send, 0)


def send_views(views, block, landing, send_sem, recv_sem):
    view, me = lax.axis_index("view"), lax.axis_index("dev")
    for i in range(1, views):
        pltpu.make_async_remote_copy(
            src_ref=block,
            dst_ref=landing(view),
            send_sem=send_sem,
            recv_sem=recv_sem,
            device_id=(lax.rem(view + i, views), me),
            device_id_type=MESH,
        ).start()


def wait_bytes(ref, semaphore):
    pltpu.make_async_copy(ref, ref, semaphore).wait()


def slot_messages(rows, center, dense, feats, outgoing):
    for chunk in range(4):
        values = [dense_at(dense, chunk, p) for p in range(PARAMS)]
        for f, value in enumerate(project(values, center)):
            feats[f, 8 * chunk : 8 * chunk + 8, :] = value
    high = rows // LANES
    low = lax.rem(rows, LANES)
    slots = [jnp.zeros((8, LANES), jnp.float32)] * FEATS
    for h in range(32):
        chosen = high == h
        for f in range(FEATS):
            source = jnp.broadcast_to(feats[f, h : h + 1, :], (8, LANES))
            slots[f] = jnp.where(chosen, pick(source, low), slots[f])
    lane = lane_ids()
    sub = row_ids()
    for block in range(16):
        index = ((block % 2) * 8 + sub) * 8 + lax.rem(lane, 8)
        message = jnp.zeros((8, LANES), jnp.float32)
        for f in range(FEATS):
            source = jnp.broadcast_to(slots[f][block // 2 : block // 2 + 1, :], (8, LANES))
            message = jnp.where(lane // 8 == f, pick(source, index), message)
        outgoing[8 * block : 8 * block + 8, :] = message


def dot(a, b, dims=((1,), (0,))):
    return lax.dot_general(
        a,
        b,
        (dims, ((), ())),
        precision=lax.Precision.HIGHEST,
        preferred_element_type=jnp.float32,
    )


def render(
    arrived_ref,
    lists,
    counts,
    ids,
    wanted_ref,
    out_ref,
    gauss,
    trans,
    gauss_grad,
    weight,
    sums,
):
    lane = lane_ids()
    sub = row_ids()
    half_of = lane // 64
    entry = lax.rem(lane, 64)
    slot = lax.rem(lists, 64)
    from_owner = slot // 8
    within = lax.rem(slot, 8)
    feats = [jnp.zeros((8, LANES), jnp.float32)] * FEATS
    for h in range(2):
        for o in range(8):
            block = arrived_ref[pl.ds(8 * h + o, 8, stride=16), :]
            chosen = (from_owner == o) & (half_of == h)
            for f in range(FEATS):
                feats[f] = jnp.where(chosen, pick(block, 8 * f + within), feats[f])
    center_u = (lax.rem(ids, TILES_X) * TILE_SIDE + TILE_SIDE // 2).astype(jnp.float32)
    center_v = (ids // TILES_X * TILE_SIDE + TILE_SIDE // 2).astype(jnp.float32)
    mean_u = feats[0] * WIDTH - center_u
    mean_v = feats[1] * HEIGHT - center_v
    quad_a = feats[2] * (-0.5 / (WIDTH * WIDTH))
    quad_b = feats[3] * (-1.0 / (WIDTH * HEIGHT))
    quad_c = feats[4] * (-0.5 / (HEIGHT * HEIGHT))
    active = entry < counts
    opacity = jnp.where(active, feats[8], 0.0)
    pixel_u = lax.rem(lane, 16).astype(jnp.float32) - 7.5
    pixel_v = [(lane // 16 + 8 * p).astype(jnp.float32) - 7.5 for p in range(2)]
    ahead = [mean_u, mean_v, quad_a, quad_b, quad_c, *feats[5:8], opacity]

    def forward(e, carried):
        through, acc, place = carried
        through, acc = list(through), list(acc)
        for h in range(2):
            index = jnp.full((8, LANES), h * 64, jnp.int32) + e
            m_u, m_v, q_a, q_b, q_c, c_0, c_1, c_2, alpha_max = (
                pick(array, index) for array in ahead
            )
            place = jnp.where((pick(slot, index) == entry) & (half_of == h), e, place)
            diff_u = pixel_u - m_u
            part = diff_u * q_b
            square = diff_u * diff_u * q_a
            for p in range(2):
                diff_v = pixel_v[p] - m_v
                bell = jnp.exp(square + diff_v * (part + q_c * diff_v))
                alpha = alpha_max * bell
                n = 2 * h + p
                before = through[n]
                gauss[e, n] = bell
                trans[e, n] = before
                share = alpha * before
                through[n] = before - share
                for ch, color in enumerate((c_0, c_1, c_2)):
                    acc[3 * n + ch] = acc[3 * n + ch] + color * share
        return tuple(through), tuple(acc), place

    zero = jnp.zeros((8, LANES), jnp.float32)
    _, acc, place = lax.fori_loop(
        0,
        64,
        forward,
        ((zero + 1.0,) * 4, (zero,) * 12, jnp.zeros((8, LANES), jnp.int32)),
        unroll=16,
    )
    residual = []
    for h in range(2):
        for p in range(2):
            for ch in range(3):
                wanted = wanted_ref[pl.ds(16 * (2 * ch + p) + h, 8, stride=2), :]
                residual.append(acc[3 * (2 * h + p) + ch] - wanted)

    def backward(i, carried):
        e = 63 - i
        behind = list(carried)
        for h in range(2):
            index = jnp.full((8, LANES), h * 64, jnp.int32) + e
            c_0, c_1, c_2, alpha_max = (pick(array, index) for array in ahead[5:9])
            for p in range(2):
                n = 2 * h + p
                bell = gauss[e, n]
                before = trans[e, n]
                alpha = alpha_max * bell
                shade = (
                    c_0 * residual[3 * n] + c_1 * residual[3 * n + 1] + c_2 * residual[3 * n + 2]
                )
                gap = shade - behind[n]
                behind[n] = behind[n] + alpha * gap
                start = pl.multiple_of(512 * h + 8 * e, 8)
                gauss_grad[p, pl.ds(start, 8), :] = before * gap * bell
                weight[p, pl.ds(start, 8), :] = alpha * before
        return tuple(behind)

    lax.fori_loop(0, 64, backward, (zero,) * 4, unroll=16)

    pix = row_ids(LANES)
    col = lane_ids(LANES)
    for_moments, for_colors = [], []
    for p in range(2):
        u = lax.rem(pix, 16).astype(jnp.float32) - 7.5
        v = (pix // 16 + 8 * p).astype(jnp.float32) - 7.5
        powers = [jnp.ones_like(u), u, v, u * u, u * v, v * v]
        table = jnp.zeros_like(u)
        for m, power in enumerate(powers):
            table = jnp.where(col == m, power, table)
        for_moments.append(table)
        stacked = [zero]
        for ch in range(3):
            for h in range(2):
                stacked.append(residual[3 * (2 * h + p) + ch])
        stacked += [zero] * 9
        for_colors.append(jnp.concatenate(stacked, axis=0).T)

    for k in range(8):
        rows = pl.ds(k, LANES, stride=8)
        total = (
            dot(gauss_grad[0, rows, :], for_moments[0])
            + dot(gauss_grad[1, rows, :], for_moments[1])
            + dot(weight[0, rows, :], for_colors[0])
            + dot(weight[1, rows, :], for_colors[1])
        )
        sums[64 * k : 64 * k + 64, :] = total.T[0:64, :]

    s_0, s_u, s_v, s_uu, s_uv, s_vv = (sums[pl.ds(m, 8, stride=64), :] for m in range(6))
    d_colors = []
    for ch in range(3):
        even = sums[pl.ds(8 + 16 * ch, 8, stride=65), :]
        odd = sums[pl.ds(16 + 16 * ch, 8, stride=65), :]
        d_colors.append(jnp.where(half_of == 0, even, odd))
    m_u = opacity * (s_u - mean_u * s_0)
    m_v = opacity * (s_v - mean_v * s_0)
    m_uu = opacity * (s_uu - mean_u * (2.0 * s_u - mean_u * s_0))
    m_vv = opacity * (s_vv - mean_v * (2.0 * s_v - mean_v * s_0))
    m_uv = opacity * (s_uv - mean_u * s_v - mean_v * (s_u - mean_u * s_0))
    grads = [
        -WIDTH * (2.0 * quad_a * m_u + quad_b * m_v),
        -HEIGHT * (2.0 * quad_c * m_v + quad_b * m_u),
        (-0.5 / (WIDTH * WIDTH)) * m_uu,
        (-1.0 / (WIDTH * HEIGHT)) * m_uv,
        (-0.5 / (HEIGHT * HEIGHT)) * m_vv,
        *d_colors,
        jnp.where(active, s_0, 0.0),
    ]
    for h in range(2):
        for o in range(8):
            base = h * 64 + o * 8 + lax.rem(lane, 8)
            index = h * 64 + pick(place, base)
            message = zero
            for f in range(FEATS):
                message = jnp.where(lane // 8 == f, pick(grads[f], index), message)
            out_ref[pl.ds(8 * h + o, 8, stride=16), :] = message


def step_sizes(rows):
    return jnp.where(
        rows < 3,
        0.00016,
        jnp.where(
            rows < 6,
            0.005,
            jnp.where(
                rows < 10,
                0.001,
                jnp.where(rows < 11, 0.05, jnp.where(rows < 14, 0.0025, 0.000125)),
            ),
        ),
    )


def slot_places(rows_all):
    place = jnp.zeros((PADDED, LANES), jnp.float32)
    sub_high = row_ids(32)
    sub_low = row_ids(LANES)
    lane_value = lane_ids(32).astype(jnp.float32)
    for i in range(32):
        rows = rows_all[i // 8][i % 8 : i % 8 + 1, :]
        hit = sub_high == jnp.broadcast_to(rows // LANES, (32, LANES))
        left = jnp.concatenate(
            [jnp.where(hit, float(i), 0.0), jnp.where(hit, lane_value, 0.0)], axis=0
        )
        right = jnp.where(
            sub_low == jnp.broadcast_to(lax.rem(rows, LANES), (LANES, LANES)), 1.0, 0.0
        )
        place = place + lax.dot_general(
            left.astype(jnp.bfloat16),
            right.astype(jnp.bfloat16),
            (((1,), (1,)), ((), ())),
            preferred_element_type=jnp.float32,
        )
    return (place[0:32] + 0.5).astype(jnp.int32), (place[32:64] + 0.5).astype(jnp.int32)


def per_tile(ref):
    row, half_of = row_ids(), lane_ids() // 64
    spread = jnp.zeros((8, LANES), jnp.int32)
    for k in range(16):
        spread = jnp.where((row == k // 2) & (half_of == k % 2), ref[0, k], spread)
    return spread


def step_kernel(
    views,
    owners,
    center_ref,
    order_ref,
    counts_ref,
    ids_ref,
    order_lanes_ref,
    rows_ref,
    lists_ref,
    target_ref,
    params_hbm,
    first_hbm,
    second_hbm,
    new_params_ref,
    new_first_ref,
    new_second_ref,
    params_ref,
    first_ref,
    second_ref,
    dense,
    feats,
    outgoing,
    landed,
    packed,
    packed_landed,
    before_a,
    before_b,
    moved_a,
    moved_b,
    leaving,
    arriving,
    order_rows,
    list_rows,
    wanted,
    gauss,
    trans,
    gauss_grad,
    weight,
    sums,
    slot_grads,
    returned,
    by_slot,
    leaving_grads,
    arriving_grads,
    grads,
    load_sems,
    sems,
):
    view, me = lax.axis_index("view"), lax.axis_index("dev")
    loads = [
        pltpu.make_async_copy(source, place, load_sems.at[i])
        for i, (source, place) in enumerate(
            ((params_hbm, params_ref), (first_hbm, first_ref), (second_hbm, second_ref))
        )
    ]
    for load in loads:
        load.start()
    barrier, expected = greet(views, owners)
    lane = lane_ids()
    others = pl.ds(0, owners - 1)
    other_views = pl.ds(0, views - 1)
    kept = order_ref.shape[1] - owners
    zero = jnp.zeros((8, LANES), jnp.float32)

    for i in range(8):
        packed[i : i + 1, :] = rows_ref[0, :, LANES * i : LANES * (i + 1)].astype(jnp.float32)
    here = zero
    for i in range(3):
        here = jnp.where(lane == i, center_ref[0, i], here)
    packed[8:16, :] = here
    loads[0].wait()
    fill_dense(params_ref, dense)
    slot_messages(
        packed[0:8, :].astype(jnp.int32),
        [center_ref[0, i] for i in range(3)],
        dense,
        feats,
        outgoing,
    )

    fill = jnp.zeros((PADDED - PARAMS, LANES), jnp.float32)
    empty = jnp.zeros((PADDED, LANES), jnp.float32)
    loads[1].wait()
    loads[2].wait()

    def to_rows(j, carried):
        columns = pl.ds(pl.multiple_of(j * LANES, LANES), LANES)
        before_a[columns, :] = jnp.concatenate(
            [params_ref[:, columns], fill, first_ref[:, columns], fill], axis=0
        ).T
        before_b[columns, :] = jnp.concatenate([second_ref[:, columns], fill, empty], axis=0).T
        return carried

    lax.fori_loop(0, 32, to_rows, 0, unroll=8)

    pl.semaphore_wait(barrier, expected)
    send_each(
        owners,
        lambda d: outgoing.at[pl.ds(d, 1)],
        lambda d: landed.at[pl.ds(d, 1)],
        sems.at[0],
        sems.at[1],
    )
    send_views(views, packed, lambda v: packed_landed.at[v], sems.at[2], sems.at[3])
    landed[pl.ds(me, 1), :] = outgoing[pl.ds(me, 1), :]
    packed_landed[view] = packed[...]

    for t in range(owners):
        row = order_ref[0, kept + t]
        leaving[0, t : t + 1, :] = before_a[pl.ds(row, 1), :]
        leaving[1, t : t + 1, :] = before_b[pl.ds(row, 1), :]
    send_each(
        owners,
        lambda d: leaving.at[:, pl.ds(d, 1)],
        lambda d: arriving.at[:, pl.ds(d, 1)],
        sems.at[4],
        sems.at[5],
    )
    arriving[:, pl.ds(me, 1), :] = leaving[:, pl.ds(me, 1), :]

    def move(t, carried):
        for u in range(32):
            row = order_ref[0, t * 32 + u]
            moved_a[pl.ds(t * 32 + u, 1), :] = before_a[pl.ds(row, 1), :]
            moved_b[pl.ds(t * 32 + u, 1), :] = before_b[pl.ds(row, 1), :]
        return carried

    lax.fori_loop(0, MOVED_EARLY // 32, move, 0)
    for k in range(16):
        list_rows[k : k + 1, 0:64] = lists_ref[0, k : k + 1, :]
    for ch in range(3):
        for p in range(2):
            n = 16 * (2 * ch + p)
            wanted[n : n + 16, :] = target_ref[ch, :, LANES * p : LANES * (p + 1)]
    even = list_rows[pl.ds(0, 8, stride=2), :]
    odd = list_rows[pl.ds(1, 8, stride=2), :]
    lists = jnp.where(lane < 64, even, pick(odd, lax.rem(lane, 64)))

    wait_bytes(landed.at[others], sems.at[1])
    render(
        landed,
        lists,
        per_tile(counts_ref),
        per_tile(ids_ref),
        wanted,
        slot_grads,
        gauss,
        trans,
        gauss_grad,
        weight,
        sums,
    )
    send_each(
        owners,
        lambda d: slot_grads.at[pl.ds(d, 1)],
        lambda d: returned.at[pl.ds(d, 1)],
        sems.at[6],
        sems.at[7],
    )
    returned[pl.ds(me, 1), :] = slot_grads[pl.ds(me, 1), :]

    lax.fori_loop(MOVED_EARLY // 32, kept // 32, move, 0)
    wait_bytes(arriving.at[:, others], sems.at[5])
    moved_a[kept:, :] = arriving[0]
    moved_b[kept:, :] = arriving[1]

    def to_columns(j, carried):
        columns = pl.ds(pl.multiple_of(j * LANES, LANES), LANES)
        both = moved_a[columns, :].T
        new_params_ref[:, columns] = both[0:PARAMS, :]
        new_first_ref[:, columns] = both[PADDED : PADDED + PARAMS, :]
        new_second_ref[:, columns] = moved_b[columns, :].T[0:PARAMS, :]
        dense[pl.ds(pl.multiple_of(j * PADDED, PADDED), PADDED), :] = both[0:PADDED, :]
        return carried

    lax.fori_loop(0, 32, to_columns, 0, unroll=8)
    for j in range(32):
        order_rows[j : j + 1, :] = order_lanes_ref[:, LANES * j : LANES * (j + 1)]
    wait_bytes(packed_landed.at[other_views], sems.at[3])
    place_high, place_low = slot_places(
        [packed_landed[v, 0:8, :].astype(jnp.int32) for v in range(views)]
    )
    place = place_high * LANES + place_low
    slot_high, slot_low = [], []
    for chunk in range(4):
        order = order_rows[8 * chunk : 8 * chunk + 8, :]
        high, low = order // LANES, lax.rem(order, LANES)
        found = jnp.zeros((8, LANES), jnp.int32)
        for h in range(32):
            source = jnp.broadcast_to(place[h : h + 1, :], (8, LANES))
            found = jnp.where(high == h, pick(source, low), found)
        slot_high.append(found // LANES)
        slot_low.append(lax.rem(found, LANES))
    centers = [
        [
            jnp.broadcast_to(packed_landed[v, 8:9, i : i + 1], (8, LANES))
            for v in range(views)
        ]
        for i in range(3)
    ]

    wait_bytes(returned.at[others], sems.at[7])
    values = [zero] * FEATS
    for o in range(16):
        block = returned[pl.ds(o, 8, stride=16), :]
        chosen = lane // 8 == o
        for f in range(FEATS):
            values[f] = jnp.where(chosen, pick(block, 8 * f + lax.rem(lane, 8)), values[f])
    for f in range(FEATS):
        by_slot[view, 8 * f : 8 * f + 8, :] = values[f]
    send_views(views, by_slot.at[view], lambda v: by_slot.at[v], sems.at[8], sems.at[9])
    wait_bytes(by_slot.at[other_views], sems.at[9])

    def collect(chunk):
        found = [zero] * FEATS
        for h in range(32):
            chosen = slot_high[chunk] == h
            for f in range(FEATS):
                row = 8 * f + h % 8
                source = jnp.broadcast_to(by_slot[h // 8, row : row + 1, :], (8, LANES))
                found[f] = jnp.where(chosen, pick(source, slot_low[chunk]), found[f])
        return found

    bias_one = 1.0 - BETA_ONE**ADAM_STEP
    bias_two = 1.0 - BETA_TWO**ADAM_STEP
    sizes = step_sizes(row_ids(PADDED)[0:PARAMS])

    def finish(chunk, feat_grads, view_of):
        center = []
        for i in range(3):
            at = zero
            for v in range(views):
                at = jnp.where(view_of == v, centers[i][v], at)
            center.append(at)
        arguments = [dense_at(dense, chunk, p) for p in range(PARAMS)]
        _, pull_back = jax.vjp(lambda *args: project(args, center), *arguments)
        for p, grad in enumerate(pull_back(list(feat_grads))):
            grads[pl.ds(chunk * 8 * PADDED + p, 8, stride=PADDED), :] = grad
        for j in range(8 * chunk, 8 * chunk + 8):
            columns = slice(LANES * j, LANES * (j + 1))
            gradient = grads[PADDED * j : PADDED * j + PARAMS, :]
            new_one = BETA_ONE * new_first_ref[:, columns] + (1.0 - BETA_ONE) * gradient
            new_two = BETA_TWO * new_second_ref[:, columns] + (1.0 - BETA_TWO) * gradient * gradient
            new_params_ref[:, columns] = new_params_ref[:, columns] - sizes * (
                new_one / bias_one
            ) / (jnp.sqrt(new_two / bias_two) + ADAM_EPS)
            new_first_ref[:, columns] = new_one
            new_second_ref[:, columns] = new_two

    last = collect(3)
    last_view = slot_high[3] // 8
    rows = [found[7:8, :] for found in last] + [last_view[7:8, :].astype(jnp.float32)]
    rows.append(jnp.zeros((LANES - len(rows), LANES), jnp.float32))
    leaving_grads[...] = jnp.concatenate(rows, axis=0).T
    send_each(
        owners,
        lambda d: leaving_grads.at[pl.ds(d, 1)],
        lambda d: arriving_grads.at[pl.ds(d, 1)],
        sems.at[10],
        sems.at[11],
    )
    arriving_grads[pl.ds(me, 1), :] = leaving_grads[pl.ds(me, 1), :]
    for chunk in range(3):
        finish(chunk, collect(chunk), slot_high[chunk] // 8)
    wait_bytes(arriving_grads.at[others], sems.at[11])
    arrived = arriving_grads[...].T
    is_last = row_ids() == 7
    last = [
        jnp.where(is_last, jnp.broadcast_to(arrived[f : f + 1, :], (8, LANES)), last[f])
        for f in range(FEATS)
    ]
    arrived_view = (arrived[FEATS : FEATS + 1, :] + 0.5).astype(jnp.int32)
    finish(
        3, last, jnp.where(is_last, jnp.broadcast_to(arrived_view, (8, LANES)), last_view)
    )
    wait_bytes(landed.at[others], sems.at[0])
    wait_bytes(packed_landed.at[other_views], sems.at[2])
    wait_bytes(arriving.at[:, others], sems.at[4])
    wait_bytes(returned.at[others], sems.at[6])
    wait_bytes(by_slot.at[other_views], sems.at[8])
    wait_bytes(arriving_grads.at[others], sems.at[10])


VMEM = pl.BlockSpec(memory_space=pltpu.VMEM)
SMEM = pl.BlockSpec(memory_space=pltpu.SMEM)
ANY = pl.BlockSpec(memory_space=pl.ANY)
VMEM_BYTES = 48 * 1024 * 1024


def f32(*shape):
    return jax.ShapeDtypeStruct(shape, jnp.float32)


def scratch(*shape):
    return pltpu.VMEM(shape, jnp.float32)


def per_device(
    params,
    first_moment,
    second_moment,
    cam_centers,
    target,
    send_rows,
    tile_lists,
    tile_counts,
    tile_ids,
    move_order,
):
    views, owners = lax.axis_size("view"), lax.axis_size("dev")
    return pl.pallas_call(
        functools.partial(step_kernel, views, owners),
        out_shape=(f32(PARAMS, 4096),) * 3,
        in_specs=[SMEM] * 4 + [VMEM] * 4 + [ANY] * 3,
        out_specs=(VMEM,) * 3,
        scratch_shapes=[
            scratch(PARAMS, 4096),
            scratch(PARAMS, 4096),
            scratch(PARAMS, 4096),
            scratch(32 * PADDED, LANES),
            scratch(FEATS, 32, LANES),
            scratch(owners, LANES),
            scratch(owners, LANES),
            scratch(16, LANES),
            scratch(views, 16, LANES),
            scratch(4096, LANES),
            scratch(4096, LANES),
            scratch(4096, LANES),
            scratch(4096, LANES),
            scratch(2, owners, LANES),
            scratch(2, owners, LANES),
            pltpu.VMEM((32, LANES), jnp.int32),
            pltpu.VMEM((16, LANES), jnp.int32),
            scratch(96, LANES),
            scratch(64, 4, 8, LANES),
            scratch(64, 4, 8, LANES),
            scratch(2, 1024, LANES),
            scratch(2, 1024, LANES),
            scratch(512, LANES),
            scratch(owners, LANES),
            scratch(owners, LANES),
            scratch(views, 8 * FEATS, LANES),
            scratch(owners, LANES),
            scratch(owners, LANES),
            scratch(32 * PADDED, LANES),
            pltpu.SemaphoreType.DMA((3,)),
            pltpu.SemaphoreType.DMA((12,)),
        ],
        compiler_params=pltpu.CompilerParams(
            vmem_limit_bytes=VMEM_BYTES, collective_id=0, has_side_effects=True
        ),
        name="step",
    )(
        cam_centers,
        move_order,
        tile_counts,
        tile_ids,
        move_order,
        send_rows,
        tile_lists,
        target[0].transpose(1, 0, 2),
        params,
        first_moment,
        second_moment,
    )


def solution(mesh):
    placed = (
        P(None, "dev"),
        P(None, "dev"),
        P(None, "dev"),
        P("view", None),
        P("view", "dev", None, None),
        P("view", "dev", None),
        P("view", "dev", None),
        P("view", "dev"),
        P("view", "dev"),
        P("dev", None),
    )
    return jax.shard_map(
        per_device,
        mesh=mesh,
        in_specs=placed,
        out_specs=(P(None, "dev"), P(None, "dev"), P(None, "dev")),
        check_vma=False,
    )
```

```python
import functools

import jax
import jax.numpy as jnp
from jax import lax
from jax.experimental import pallas as pl
from jax.experimental.pallas import tpu as pltpu
from jax.sharding import PartitionSpec as P

PARAMS = 59
PADDED = 64
FEATS = 9
LANES = 128
TILE_SIDE = 16
TILES_X = 64
ADAM_STEP = 1000
FOCAL_LEN = 1.2
DILATION = 0.3
SH_C0 = 0.28209479177387814
SH_C1 = 0.4886025119029199
SH_C2 = (
    1.0925484305920792,
    -1.0925484305920792,
    0.31539156525252005,
    -1.0925484305920792,
    0.5462742152960396,
)
SH_C3 = (
    -0.5900435899266435,
    2.890611442640554,
    -0.4570457994644658,
    0.3731763325901154,
    -0.4570457994644658,
    1.445305721320277,
    -0.5900435899266435,
)
BETA_ONE = 0.9
BETA_TWO = 0.999
ADAM_EPS = 1e-08
MESH = pl.DeviceIdType.MESH
MOVED_EARLY = 2816
WIDTH = 1024.0
HEIGHT = 512.0


def sh_basis(x, y, z):
    xx, yy, zz = x * x, y * y, z * z
    return [
        SH_C0 + 0.0 * x,
        -SH_C1 * y,
        SH_C1 * z,
        -SH_C1 * x,
        SH_C2[0] * x * y,
        SH_C2[1] * y * z,
        SH_C2[2] * (2.0 * zz - xx - yy),
        SH_C2[3] * x * z,
        SH_C2[4] * (xx - yy),
        SH_C3[0] * y * (3.0 * xx - yy),
        SH_C3[1] * x * y * z,
        SH_C3[2] * y * (4.0 * zz - xx - yy),
        SH_C3[3] * z * (2.0 * zz - 3.0 * xx - 3.0 * yy),
        SH_C3[4] * x * (4.0 * zz - xx - yy),
        SH_C3[5] * z * (xx - yy),
        SH_C3[6] * x * (xx - 3.0 * yy),
    ]


def project(values, center):
    off = [values[i] - center[i] for i in range(3)]
    inverse = 1.0 / off[2]
    mean_u = 0.5 + FOCAL_LEN * off[0] * inverse
    mean_v = 0.5 + FOCAL_LEN * off[1] * inverse
    scale_sq = [jnp.exp(2.0 * values[3 + i]) for i in range(3)]
    quat = values[6:10]
    norm = lax.rsqrt(
        quat[0] * quat[0] + quat[1] * quat[1] + quat[2] * quat[2] + quat[3] * quat[3]
    )
    w, x, y, z = (q * norm for q in quat)
    rotation = [
        [1.0 - 2.0 * (y * y + z * z), 2.0 * (x * y - w * z), 2.0 * (x * z + w * y)],
        [2.0 * (x * y + w * z), 1.0 - 2.0 * (x * x + z * z), 2.0 * (y * z - w * x)],
        [2.0 * (x * z - w * y), 2.0 * (y * z + w * x), 1.0 - 2.0 * (x * x + y * y)],
    ]
    focal_now = FOCAL_LEN * inverse
    slope_u = -focal_now * off[0] * inverse
    slope_v = -focal_now * off[1] * inverse
    cov_uu = DILATION / (WIDTH * WIDTH)
    cov_vv = DILATION / (HEIGHT * HEIGHT)
    cov_uv = 0.0
    for c in range(3):
        axis_u = focal_now * rotation[0][c] + slope_u * rotation[2][c]
        axis_v = focal_now * rotation[1][c] + slope_v * rotation[2][c]
        cov_uu = cov_uu + axis_u * axis_u * scale_sq[c]
        cov_vv = cov_vv + axis_v * axis_v * scale_sq[c]
        cov_uv = cov_uv + axis_u * axis_v * scale_sq[c]
    inv_det = 1.0 / (cov_uu * cov_vv - cov_uv * cov_uv)
    inv_dist = 1.0 / jnp.sqrt(off[0] * off[0] + off[1] * off[1] + off[2] * off[2])
    basis = sh_basis(off[0] * inv_dist, off[1] * inv_dist, off[2] * inv_dist)
    colors = []
    for ch in range(3):
        total = basis[0] * values[11 + ch]
        for k in range(1, 16):
            total = total + basis[k] * values[11 + 3 * k + ch]
        colors.append(0.5 + total)
    opacity = 1.0 / (1.0 + jnp.exp(-values[10]))
    return [
        mean_u,
        mean_v,
        cov_vv * inv_det,
        -cov_uv * inv_det,
        cov_uu * inv_det,
        *colors,
        opacity,
    ]


def pick(array, index):
    return jnp.take_along_axis(array, index, axis=1, mode="promise_in_bounds")


def lane_ids(rows=8):
    return lax.broadcasted_iota(jnp.int32, (rows, LANES), 1)


def row_ids(rows=8):
    return lax.broadcasted_iota(jnp.int32, (rows, LANES), 0)


def fill_dense(array_ref, dense_ref):
    for j in range(32):
        dense_ref[PADDED * j : PADDED * j + PARAMS, :] = array_ref[
            :, LANES * j : LANES * (j + 1)
        ]


def dense_at(dense_ref, chunk, row):
    return dense_ref[pl.ds(chunk * 8 * PADDED + row, 8, stride=PADDED), :]


def greet(views, owners):
    view, me = lax.axis_index("view"), lax.axis_index("dev")
    barrier = pltpu.get_barrier_semaphore()
    for i in range(1, views):
        pl.semaphore_signal(
            barrier, inc=1, device_id=(lax.rem(view + i, views), me), device_id_type=MESH
        )

    def signal(i, carried):
        pl.semaphore_signal(
            barrier, inc=1, device_id=(view, lax.rem(me + i, owners)), device_id_type=MESH
        )
        return carried

    lax.fori_loop(1, owners, signal, 0)
    return barrier, views + owners - 2


def send_each(owners, message, landing, send_sem, recv_sem):
    view, me = lax.axis_index("view"), lax.axis_index("dev")

    def send(i, carried):
        other = lax.rem(me + i, owners)
        pltpu.make_async_remote_copy(
            src_ref=message(other),
            dst_ref=landing(me),
            send_sem=send_sem,
            recv_sem=recv_sem,
            device_id=(view, other),
            device_id_type=MESH,
        ).start()
        return carried

    lax.fori_loop(1, owners, send, 0)


def send_views(views, block, landing, send_sem, recv_sem):
    view, me = lax.axis_index("view"), lax.axis_index("dev")
    for i in range(1, views):
        pltpu.make_async_remote_copy(
            src_ref=block,
            dst_ref=landing(view),
            send_sem=send_sem,
            recv_sem=recv_sem,
            device_id=(lax.rem(view + i, views), me),
            device_id_type=MESH,
        ).start()


def wait_bytes(ref, semaphore):
    pltpu.make_async_copy(ref, ref, semaphore).wait()


def slot_messages(rows, center, dense, feats, outgoing):
    for chunk in range(4):
        values = [dense_at(dense, chunk, p) for p in range(PARAMS)]
        for f, value in enumerate(project(values, center)):
            feats[f, 8 * chunk : 8 * chunk + 8, :] = value
    high = rows // LANES
    low = lax.rem(rows, LANES)
    slots = [jnp.zeros((8, LANES), jnp.float32)] * FEATS
    for h in range(32):
        chosen = high == h
        for f in range(FEATS):
            source = jnp.broadcast_to(feats[f, h : h + 1, :], (8, LANES))
            slots[f] = jnp.where(chosen, pick(source, low), slots[f])
    lane = lane_ids()
    sub = row_ids()
    for block in range(16):
        index = ((block % 2) * 8 + sub) * 8 + lax.rem(lane, 8)
        message = jnp.zeros((8, LANES), jnp.float32)
        for f in range(FEATS):
            source = jnp.broadcast_to(slots[f][block // 2 : block // 2 + 1, :], (8, LANES))
            message = jnp.where(lane // 8 == f, pick(source, index), message)
        outgoing[8 * block : 8 * block + 8, :] = message


def dot(a, b, dims=((1,), (0,))):
    return lax.dot_general(
        a,
        b,
        (dims, ((), ())),
        precision=lax.Precision.HIGHEST,
        preferred_element_type=jnp.float32,
    )


def render(
    arrived_ref,
    lists,
    counts,
    ids,
    wanted_ref,
    out_ref,
    gauss,
    trans,
    gauss_grad,
    weight,
    sums,
):
    lane = lane_ids()
    sub = row_ids()
    half_of = lane // 64
    entry = lax.rem(lane, 64)
    slot = lax.rem(lists, 64)
    from_owner = slot // 8
    within = lax.rem(slot, 8)
    feats = [jnp.zeros((8, LANES), jnp.float32)] * FEATS
    for h in range(2):
        for o in range(8):
            block = arrived_ref[pl.ds(8 * h + o, 8, stride=16), :]
            chosen = (from_owner == o) & (half_of == h)
            for f in range(FEATS):
                feats[f] = jnp.where(chosen, pick(block, 8 * f + within), feats[f])
    center_u = (lax.rem(ids, TILES_X) * TILE_SIDE + TILE_SIDE // 2).astype(jnp.float32)
    center_v = (ids // TILES_X * TILE_SIDE + TILE_SIDE // 2).astype(jnp.float32)
    mean_u = feats[0] * WIDTH - center_u
    mean_v = feats[1] * HEIGHT - center_v
    quad_a = feats[2] * (-0.5 / (WIDTH * WIDTH))
    quad_b = feats[3] * (-1.0 / (WIDTH * HEIGHT))
    quad_c = feats[4] * (-0.5 / (HEIGHT * HEIGHT))
    active = entry < counts
    opacity = jnp.where(active, feats[8], 0.0)
    pixel_u = lax.rem(lane, 16).astype(jnp.float32) - 7.5
    pixel_v = [(lane // 16 + 8 * p).astype(jnp.float32) - 7.5 for p in range(2)]
    ahead = [mean_u, mean_v, quad_a, quad_b, quad_c, *feats[5:8], opacity]

    def forward(e, carried):
        through, acc, place = carried
        through, acc = list(through), list(acc)
        for h in range(2):
            index = jnp.full((8, LANES), h * 64, jnp.int32) + e
            m_u, m_v, q_a, q_b, q_c, c_0, c_1, c_2, alpha_max = (
                pick(array, index) for array in ahead
            )
            place = jnp.where((pick(slot, index) == entry) & (half_of == h), e, place)
            diff_u = pixel_u - m_u
            part = diff_u * q_b
            square = diff_u * diff_u * q_a
            for p in range(2):
                diff_v = pixel_v[p] - m_v
                bell = jnp.exp(square + diff_v * (part + q_c * diff_v))
                alpha = alpha_max * bell
                n = 2 * h + p
                before = through[n]
                gauss[e, n] = bell
                trans[e, n] = before
                share = alpha * before
                through[n] = before - share
                for ch, color in enumerate((c_0, c_1, c_2)):
                    acc[3 * n + ch] = acc[3 * n + ch] + color * share
        return tuple(through), tuple(acc), place

    zero = jnp.zeros((8, LANES), jnp.float32)
    _, acc, place = lax.fori_loop(
        0,
        64,
        forward,
        ((zero + 1.0,) * 4, (zero,) * 12, jnp.zeros((8, LANES), jnp.int32)),
        unroll=16,
    )
    residual = []
    for h in range(2):
        for p in range(2):
            for ch in range(3):
                wanted = wanted_ref[pl.ds(16 * (2 * ch + p) + h, 8, stride=2), :]
                residual.append(acc[3 * (2 * h + p) + ch] - wanted)

    def backward(i, carried):
        e = 63 - i
        behind = list(carried)
        for h in range(2):
            index = jnp.full((8, LANES), h * 64, jnp.int32) + e
            c_0, c_1, c_2, alpha_max = (pick(array, index) for array in ahead[5:9])
            for p in range(2):
                n = 2 * h + p
                bell = gauss[e, n]
                before = trans[e, n]
                alpha = alpha_max * bell
                shade = (
                    c_0 * residual[3 * n] + c_1 * residual[3 * n + 1] + c_2 * residual[3 * n + 2]
                )
                gap = shade - behind[n]
                behind[n] = behind[n] + alpha * gap
                start = pl.multiple_of(512 * h + 8 * e, 8)
                gauss_grad[p, pl.ds(start, 8), :] = before * gap * bell
                weight[p, pl.ds(start, 8), :] = alpha * before
        return tuple(behind)

    lax.fori_loop(0, 64, backward, (zero,) * 4, unroll=16)

    pix = row_ids(LANES)
    col = lane_ids(LANES)
    for_moments, for_colors = [], []
    for p in range(2):
        u = lax.rem(pix, 16).astype(jnp.float32) - 7.5
        v = (pix // 16 + 8 * p).astype(jnp.float32) - 7.5
        powers = [jnp.ones_like(u), u, v, u * u, u * v, v * v]
        table = jnp.zeros_like(u)
        for m, power in enumerate(powers):
            table = jnp.where(col == m, power, table)
        for_moments.append(table)
        stacked = [zero]
        for ch in range(3):
            for h in range(2):
                stacked.append(residual[3 * (2 * h + p) + ch])
        stacked += [zero] * 9
        for_colors.append(jnp.concatenate(stacked, axis=0).T)

    for k in range(8):
        rows = pl.ds(k, LANES, stride=8)
        total = (
            dot(gauss_grad[0, rows, :], for_moments[0])
            + dot(gauss_grad[1, rows, :], for_moments[1])
            + dot(weight[0, rows, :], for_colors[0])
            + dot(weight[1, rows, :], for_colors[1])
        )
        sums[64 * k : 64 * k + 64, :] = total.T[0:64, :]

    s_0, s_u, s_v, s_uu, s_uv, s_vv = (sums[pl.ds(m, 8, stride=64), :] for m in range(6))
    d_colors = []
    for ch in range(3):
        even = sums[pl.ds(8 + 16 * ch, 8, stride=65), :]
        odd = sums[pl.ds(16 + 16 * ch, 8, stride=65), :]
        d_colors.append(jnp.where(half_of == 0, even, odd))
    m_u = opacity * (s_u - mean_u * s_0)
    m_v = opacity * (s_v - mean_v * s_0)
    m_uu = opacity * (s_uu - mean_u * (2.0 * s_u - mean_u * s_0))
    m_vv = opacity * (s_vv - mean_v * (2.0 * s_v - mean_v * s_0))
    m_uv = opacity * (s_uv - mean_u * s_v - mean_v * (s_u - mean_u * s_0))
    grads = [
        -WIDTH * (2.0 * quad_a * m_u + quad_b * m_v),
        -HEIGHT * (2.0 * quad_c * m_v + quad_b * m_u),
        (-0.5 / (WIDTH * WIDTH)) * m_uu,
        (-1.0 / (WIDTH * HEIGHT)) * m_uv,
        (-0.5 / (HEIGHT * HEIGHT)) * m_vv,
        *d_colors,
        jnp.where(active, s_0, 0.0),
    ]
    for h in range(2):
        for o in range(8):
            base = h * 64 + o * 8 + lax.rem(lane, 8)
            index = h * 64 + pick(place, base)
            message = zero
            for f in range(FEATS):
                message = jnp.where(lane // 8 == f, pick(grads[f], index), message)
            out_ref[pl.ds(8 * h + o, 8, stride=16), :] = message


def step_sizes(rows):
    return jnp.where(
        rows < 3,
        0.00016,
        jnp.where(
            rows < 6,
            0.005,
            jnp.where(
                rows < 10,
                0.001,
                jnp.where(rows < 11, 0.05, jnp.where(rows < 14, 0.0025, 0.000125)),
            ),
        ),
    )


def slot_places(rows_all):
    place = jnp.zeros((PADDED, LANES), jnp.float32)
    sub_high = row_ids(32)
    sub_low = row_ids(LANES)
    lane_value = lane_ids(32).astype(jnp.float32)
    for i in range(32):
        rows = rows_all[i // 8][i % 8 : i % 8 + 1, :]
        hit = sub_high == jnp.broadcast_to(rows // LANES, (32, LANES))
        left = jnp.concatenate(
            [jnp.where(hit, float(i), 0.0), jnp.where(hit, lane_value, 0.0)], axis=0
        )
        right = jnp.where(
            sub_low == jnp.broadcast_to(lax.rem(rows, LANES), (LANES, LANES)), 1.0, 0.0
        )
        place = place + lax.dot_general(
            left.astype(jnp.bfloat16),
            right.astype(jnp.bfloat16),
            (((1,), (1,)), ((), ())),
            preferred_element_type=jnp.float32,
        )
    return (place[0:32] + 0.5).astype(jnp.int32), (place[32:64] + 0.5).astype(jnp.int32)


def per_tile(ref):
    values = ref[...]
    row, half_of = row_ids(), lane_ids() // 64
    spread = jnp.zeros((8, LANES), jnp.int32)
    for k in range(16):
        one = jnp.broadcast_to(values[:, k : k + 1], (8, LANES))
        spread = jnp.where((row == k // 2) & (half_of == k % 2), one, spread)
    return spread


def step_kernel(
    views,
    owners,
    params_hbm,
    first_hbm,
    second_hbm,
    center_hbm,
    rows_hbm,
    order_hbm,
    lists_hbm,
    target_hbm,
    counts_hbm,
    ids_hbm,
    new_params_hbm,
    new_first_hbm,
    new_second_hbm,
    new_params_ref,
    new_first_ref,
    new_second_ref,
    params_ref,
    first_ref,
    second_ref,
    center_ref,
    rows_ref,
    order_ref,
    order_lanes_ref,
    lists_ref,
    target_ref,
    counts_ref,
    ids_ref,
    dense,
    feats,
    outgoing,
    landed,
    packed,
    packed_landed,
    before_a,
    before_b,
    moved_a,
    moved_b,
    leaving,
    arriving,
    order_rows,
    list_rows,
    wanted,
    gauss,
    trans,
    gauss_grad,
    weight,
    sums,
    slot_grads,
    returned,
    by_slot,
    leaving_grads,
    arriving_grads,
    grads,
    load_sems,
    store_sems,
    sems,
):
    view, me = lax.axis_index("view"), lax.axis_index("dev")
    copies = (
        (center_hbm, center_ref),
        (rows_hbm, rows_ref),
        (params_hbm, params_ref),
        (first_hbm, first_ref),
        (second_hbm, second_ref),
        (order_hbm, order_ref),
        (order_hbm, order_lanes_ref),
        (lists_hbm, lists_ref),
        (target_hbm, target_ref),
        (counts_hbm, counts_ref),
        (ids_hbm, ids_ref),
    )
    loads = [
        pltpu.make_async_copy(source, place, load_sems.at[i])
        for i, (source, place) in enumerate(copies)
    ]
    for load in loads:
        load.start()
    barrier, expected = greet(views, owners)
    lane = lane_ids()
    others = pl.ds(0, owners - 1)
    other_views = pl.ds(0, views - 1)
    kept = order_ref.shape[1] - owners
    zero = jnp.zeros((8, LANES), jnp.float32)

    for load in loads[0:3]:
        load.wait()
    center = [jnp.broadcast_to(center_ref[:, i : i + 1], (8, LANES)) for i in range(3)]
    for i in range(8):
        packed[i : i + 1, :] = rows_ref[0, :, LANES * i : LANES * (i + 1)].astype(jnp.float32)
    here = zero
    for i in range(3):
        here = jnp.where(lane == i, center[i], here)
    packed[8:16, :] = here
    fill_dense(params_ref, dense)
    slot_messages(
        packed[0:8, :].astype(jnp.int32),
        center,
        dense,
        feats,
        outgoing,
    )

    fill = jnp.zeros((PADDED - PARAMS, LANES), jnp.float32)
    empty = jnp.zeros((PADDED, LANES), jnp.float32)
    loads[3].wait()
    loads[4].wait()

    def to_rows(j, carried):
        columns = pl.ds(pl.multiple_of(j * LANES, LANES), LANES)
        before_a[columns, :] = jnp.concatenate(
            [params_ref[:, columns], fill, first_ref[:, columns], fill], axis=0
        ).T
        before_b[columns, :] = jnp.concatenate([second_ref[:, columns], fill, empty], axis=0).T
        return carried

    lax.fori_loop(0, 32, to_rows, 0, unroll=8)

    for load in loads[5:]:
        load.wait()
    for t in range(owners):
        row = order_ref[0, kept + t]
        leaving[0, t : t + 1, :] = before_a[pl.ds(row, 1), :]
        leaving[1, t : t + 1, :] = before_b[pl.ds(row, 1), :]

    pl.semaphore_wait(barrier, expected)
    send_each(
        owners,
        lambda d: outgoing.at[pl.ds(d, 1)],
        lambda d: landed.at[pl.ds(d, 1)],
        sems.at[0],
        sems.at[1],
    )
    send_views(views, packed, lambda v: packed_landed.at[v], sems.at[2], sems.at[3])
    landed[pl.ds(me, 1), :] = outgoing[pl.ds(me, 1), :]
    packed_landed[view] = packed[...]

    send_each(
        owners,
        lambda d: leaving.at[:, pl.ds(d, 1)],
        lambda d: arriving.at[:, pl.ds(d, 1)],
        sems.at[4],
        sems.at[5],
    )
    arriving[:, pl.ds(me, 1), :] = leaving[:, pl.ds(me, 1), :]

    def move(t, carried):
        for u in range(32):
            row = order_ref[0, t * 32 + u]
            moved_a[pl.ds(t * 32 + u, 1), :] = before_a[pl.ds(row, 1), :]
            moved_b[pl.ds(t * 32 + u, 1), :] = before_b[pl.ds(row, 1), :]
        return carried

    lax.fori_loop(0, MOVED_EARLY // 32, move, 0)
    for k in range(16):
        list_rows[k : k + 1, 0:64] = lists_ref[0, k : k + 1, :]
    for ch in range(3):
        for p in range(2):
            n = 16 * (2 * ch + p)
            wanted[n : n + 16, :] = target_ref[ch, :, LANES * p : LANES * (p + 1)]
    even = list_rows[pl.ds(0, 8, stride=2), :]
    odd = list_rows[pl.ds(1, 8, stride=2), :]
    lists = jnp.where(lane < 64, even, pick(odd, lax.rem(lane, 64)))

    wait_bytes(landed.at[others], sems.at[1])
    render(
        landed,
        lists,
        per_tile(counts_ref),
        per_tile(ids_ref),
        wanted,
        slot_grads,
        gauss,
        trans,
        gauss_grad,
        weight,
        sums,
    )
    send_each(
        owners,
        lambda d: slot_grads.at[pl.ds(d, 1)],
        lambda d: returned.at[pl.ds(d, 1)],
        sems.at[6],
        sems.at[7],
    )
    returned[pl.ds(me, 1), :] = slot_grads[pl.ds(me, 1), :]

    lax.fori_loop(MOVED_EARLY // 32, kept // 32, move, 0)
    wait_bytes(arriving.at[:, others], sems.at[5])
    moved_a[kept:, :] = arriving[0]
    moved_b[kept:, :] = arriving[1]

    def to_columns(j, carried):
        columns = pl.ds(pl.multiple_of(j * LANES, LANES), LANES)
        both = moved_a[columns, :].T
        new_params_ref[:, columns] = both[0:PARAMS, :]
        new_first_ref[:, columns] = both[PADDED : PADDED + PARAMS, :]
        new_second_ref[:, columns] = moved_b[columns, :].T[0:PARAMS, :]
        dense[pl.ds(pl.multiple_of(j * PADDED, PADDED), PADDED), :] = both[0:PADDED, :]
        return carried

    lax.fori_loop(0, 32, to_columns, 0, unroll=8)
    wait_bytes(returned.at[others], sems.at[7])
    values = [zero] * FEATS
    for o in range(16):
        block = returned[pl.ds(o, 8, stride=16), :]
        chosen = lane // 8 == o
        for f in range(FEATS):
            values[f] = jnp.where(chosen, pick(block, 8 * f + lax.rem(lane, 8)), values[f])
    for f in range(FEATS):
        by_slot[view, 8 * f : 8 * f + 8, :] = values[f]
    send_views(views, by_slot.at[view], lambda v: by_slot.at[v], sems.at[8], sems.at[9])

    for j in range(32):
        order_rows[j : j + 1, :] = order_lanes_ref[:, LANES * j : LANES * (j + 1)]
    wait_bytes(packed_landed.at[other_views], sems.at[3])
    place_high, place_low = slot_places(
        [packed_landed[v, 0:8, :].astype(jnp.int32) for v in range(views)]
    )
    place = place_high * LANES + place_low
    slot_high, slot_low = [], []
    for chunk in range(4):
        order = order_rows[8 * chunk : 8 * chunk + 8, :]
        high, low = order // LANES, lax.rem(order, LANES)
        found = jnp.zeros((8, LANES), jnp.int32)
        for h in range(32):
            source = jnp.broadcast_to(place[h : h + 1, :], (8, LANES))
            found = jnp.where(high == h, pick(source, low), found)
        slot_high.append(found // LANES)
        slot_low.append(lax.rem(found, LANES))
    centers = [
        [
            jnp.broadcast_to(packed_landed[v, 8:9, i : i + 1], (8, LANES))
            for v in range(views)
        ]
        for i in range(3)
    ]

    wait_bytes(by_slot.at[other_views], sems.at[9])

    def collect(chunk):
        found = [zero] * FEATS
        for h in range(32):
            chosen = slot_high[chunk] == h
            for f in range(FEATS):
                row = 8 * f + h % 8
                source = jnp.broadcast_to(by_slot[h // 8, row : row + 1, :], (8, LANES))
                found[f] = jnp.where(chosen, pick(source, slot_low[chunk]), found[f])
        return found

    bias_one = 1.0 - BETA_ONE**ADAM_STEP
    bias_two = 1.0 - BETA_TWO**ADAM_STEP
    sizes = step_sizes(row_ids(PADDED)[0:PARAMS])

    stores = []

    def finish(chunk, feat_grads, view_of):
        center = []
        for i in range(3):
            at = zero
            for v in range(views):
                at = jnp.where(view_of == v, centers[i][v], at)
            center.append(at)
        arguments = [dense_at(dense, chunk, p) for p in range(PARAMS)]
        _, pull_back = jax.vjp(lambda *args: project(args, center), *arguments)
        for p, grad in enumerate(pull_back(list(feat_grads))):
            grads[pl.ds(chunk * 8 * PADDED + p, 8, stride=PADDED), :] = grad
        for j in range(8 * chunk, 8 * chunk + 8):
            columns = slice(LANES * j, LANES * (j + 1))
            gradient = grads[PADDED * j : PADDED * j + PARAMS, :]
            new_one = BETA_ONE * new_first_ref[:, columns] + (1.0 - BETA_ONE) * gradient
            new_two = BETA_TWO * new_second_ref[:, columns] + (1.0 - BETA_TWO) * gradient * gradient
            new_params_ref[:, columns] = new_params_ref[:, columns] - sizes * (
                new_one / bias_one
            ) / (jnp.sqrt(new_two / bias_two) + ADAM_EPS)
            new_first_ref[:, columns] = new_one
            new_second_ref[:, columns] = new_two
        columns = pl.ds(8 * LANES * chunk, 8 * LANES)
        for i, (source, place) in enumerate(
            (
                (new_params_ref, new_params_hbm),
                (new_first_ref, new_first_hbm),
                (new_second_ref, new_second_hbm),
            )
        ):
            copy = pltpu.make_async_copy(
                source.at[:, columns], place.at[:, columns], store_sems.at[3 * chunk + i]
            )
            copy.start()
            stores.append(copy)

    last = collect(3)
    last_view = slot_high[3] // 8
    rows = [found[7:8, :] for found in last] + [last_view[7:8, :].astype(jnp.float32)]
    rows.append(jnp.zeros((LANES - len(rows), LANES), jnp.float32))
    leaving_grads[...] = jnp.concatenate(rows, axis=0).T
    send_each(
        owners,
        lambda d: leaving_grads.at[pl.ds(d, 1)],
        lambda d: arriving_grads.at[pl.ds(d, 1)],
        sems.at[10],
        sems.at[11],
    )
    arriving_grads[pl.ds(me, 1), :] = leaving_grads[pl.ds(me, 1), :]
    for chunk in range(3):
        finish(chunk, collect(chunk), slot_high[chunk] // 8)
    wait_bytes(arriving_grads.at[others], sems.at[11])
    arrived = arriving_grads[...].T
    is_last = row_ids() == 7
    last = [
        jnp.where(is_last, jnp.broadcast_to(arrived[f : f + 1, :], (8, LANES)), last[f])
        for f in range(FEATS)
    ]
    arrived_view = (arrived[FEATS : FEATS + 1, :] + 0.5).astype(jnp.int32)
    finish(
        3, last, jnp.where(is_last, jnp.broadcast_to(arrived_view, (8, LANES)), last_view)
    )
    wait_bytes(landed.at[others], sems.at[0])
    wait_bytes(packed_landed.at[other_views], sems.at[2])
    wait_bytes(arriving.at[:, others], sems.at[4])
    wait_bytes(returned.at[others], sems.at[6])
    wait_bytes(by_slot.at[other_views], sems.at[8])
    wait_bytes(arriving_grads.at[others], sems.at[10])
    for copy in stores:
        copy.wait()


def write_kernel(
    params, first, second, new_params, new_first, new_second, held, load_sems, store_sems
):
    loads, stores = [], []
    for i, (source, place) in enumerate(
        ((params, new_params), (first, new_first), (second, new_second))
    ):
        for part in range(4):
            columns = pl.ds(1024 * part, 1024)
            n = len(loads)
            middle = held.at[i, :, columns]
            loads.append(pltpu.make_async_copy(source.at[:, columns], middle, load_sems.at[n]))
            stores.append(pltpu.make_async_copy(middle, place.at[:, columns], store_sems.at[n]))
    for load in loads:
        load.start()
    for load, store in zip(loads, stores):
        load.wait()
        store.start()
    for store in stores:
        store.wait()


VMEM = pl.BlockSpec(memory_space=pltpu.VMEM)
SMEM = pl.BlockSpec(memory_space=pltpu.SMEM)
ANY = pl.BlockSpec(memory_space=pl.ANY)
HBM = pl.BlockSpec(memory_space=pltpu.HBM)
VMEM_BYTES = 60 * 1024 * 1024


def f32(*shape):
    return jax.ShapeDtypeStruct(shape, jnp.float32)


def scratch(*shape):
    return pltpu.VMEM(shape, jnp.float32)


def per_device(
    params,
    first_moment,
    second_moment,
    cam_centers,
    target,
    send_rows,
    tile_lists,
    tile_counts,
    tile_ids,
    move_order,
):
    views, owners = lax.axis_size("view"), lax.axis_size("dev")
    by_channel = target[0].transpose(1, 0, 2)
    updated = pl.pallas_call(
        functools.partial(step_kernel, views, owners),
        out_shape=(f32(PARAMS, 4096),) * 3,
        in_specs=[HBM] * 10,
        out_specs=(ANY,) * 3,
        scratch_shapes=[
            scratch(PARAMS, 4096),
            scratch(PARAMS, 4096),
            scratch(PARAMS, 4096),
            scratch(PARAMS, 4096),
            scratch(PARAMS, 4096),
            scratch(PARAMS, 4096),
            scratch(*cam_centers.shape),
            pltpu.VMEM(send_rows.shape, jnp.int32),
            pltpu.SMEM(move_order.shape, jnp.int32),
            pltpu.VMEM(move_order.shape, jnp.int32),
            pltpu.VMEM(tile_lists.shape, jnp.int32),
            scratch(*by_channel.shape),
            pltpu.VMEM(tile_counts.shape, jnp.int32),
            pltpu.VMEM(tile_ids.shape, jnp.int32),
            scratch(32 * PADDED, LANES),
            scratch(FEATS, 32, LANES),
            scratch(owners, LANES),
            scratch(owners, LANES),
            scratch(16, LANES),
            scratch(views, 16, LANES),
            scratch(4096, LANES),
            scratch(4096, LANES),
            scratch(4096, LANES),
            scratch(4096, LANES),
            scratch(2, owners, LANES),
            scratch(2, owners, LANES),
            pltpu.VMEM((32, LANES), jnp.int32),
            pltpu.VMEM((16, LANES), jnp.int32),
            scratch(96, LANES),
            scratch(64, 4, 8, LANES),
            scratch(64, 4, 8, LANES),
            scratch(2, 1024, LANES),
            scratch(2, 1024, LANES),
            scratch(512, LANES),
            scratch(owners, LANES),
            scratch(owners, LANES),
            scratch(views, 8 * FEATS, LANES),
            scratch(owners, LANES),
            scratch(owners, LANES),
            scratch(32 * PADDED, LANES),
            pltpu.SemaphoreType.DMA((11,)),
            pltpu.SemaphoreType.DMA((12,)),
            pltpu.SemaphoreType.DMA((12,)),
        ],
        compiler_params=pltpu.CompilerParams(
            vmem_limit_bytes=VMEM_BYTES, collective_id=0, has_side_effects=True
        ),
        name="step",
    )(
        params,
        first_moment,
        second_moment,
        cam_centers,
        send_rows,
        move_order,
        tile_lists,
        by_channel,
        tile_counts,
        tile_ids,
    )
    return pl.pallas_call(
        write_kernel,
        out_shape=(f32(PARAMS, 4096),) * 3,
        in_specs=[ANY] * 3,
        out_specs=(HBM,) * 3,
        scratch_shapes=[
            scratch(3, PARAMS, 4096),
            pltpu.SemaphoreType.DMA((12,)),
            pltpu.SemaphoreType.DMA((12,)),
        ],
        compiler_params=pltpu.CompilerParams(vmem_limit_bytes=VMEM_BYTES),
        name="write",
    )(*updated)


def solution(mesh):
    placed = (
        P(None, "dev"),
        P(None, "dev"),
        P(None, "dev"),
        P("view", None),
        P("view", "dev", None, None),
        P("view", "dev", None),
        P("view", "dev", None),
        P("view", "dev"),
        P("view", "dev"),
        P("dev", None),
    )
    return jax.shard_map(
        per_device,
        mesh=mesh,
        in_specs=placed,
        out_specs=(P(None, "dev"), P(None, "dev"), P(None, "dev")),
        check_vma=False,
    )
```

```python
import functools

import jax
import jax.numpy as jnp
from jax import lax
from jax.experimental import pallas as pl
from jax.experimental.pallas import tpu as pltpu
from jax.sharding import PartitionSpec as P

PARAMS = 59
PADDED = 64
FEATS = 9
LANES = 128
TILE_SIDE = 16
TILES_X = 64
ADAM_STEP = 1000
FOCAL_LEN = 1.2
DILATION = 0.3
SH_C0 = 0.28209479177387814
SH_C1 = 0.4886025119029199
SH_C2 = (
    1.0925484305920792,
    -1.0925484305920792,
    0.31539156525252005,
    -1.0925484305920792,
    0.5462742152960396,
)
SH_C3 = (
    -0.5900435899266435,
    2.890611442640554,
    -0.4570457994644658,
    0.3731763325901154,
    -0.4570457994644658,
    1.445305721320277,
    -0.5900435899266435,
)
BETA_ONE = 0.9
BETA_TWO = 0.999
ADAM_EPS = 1e-08
MESH = pl.DeviceIdType.MESH
MOVED_EARLY = 2816
WIDTH = 1024.0
HEIGHT = 512.0


def sh_basis(x, y, z):
    xx, yy, zz = x * x, y * y, z * z
    return [
        SH_C0 + 0.0 * x,
        -SH_C1 * y,
        SH_C1 * z,
        -SH_C1 * x,
        SH_C2[0] * x * y,
        SH_C2[1] * y * z,
        SH_C2[2] * (2.0 * zz - xx - yy),
        SH_C2[3] * x * z,
        SH_C2[4] * (xx - yy),
        SH_C3[0] * y * (3.0 * xx - yy),
        SH_C3[1] * x * y * z,
        SH_C3[2] * y * (4.0 * zz - xx - yy),
        SH_C3[3] * z * (2.0 * zz - 3.0 * xx - 3.0 * yy),
        SH_C3[4] * x * (4.0 * zz - xx - yy),
        SH_C3[5] * z * (xx - yy),
        SH_C3[6] * x * (xx - 3.0 * yy),
    ]


def project(values, center):
    off = [values[i] - center[i] for i in range(3)]
    inverse = 1.0 / off[2]
    mean_u = 0.5 + FOCAL_LEN * off[0] * inverse
    mean_v = 0.5 + FOCAL_LEN * off[1] * inverse
    scale_sq = [jnp.exp(2.0 * values[3 + i]) for i in range(3)]
    quat = values[6:10]
    norm = lax.rsqrt(
        quat[0] * quat[0] + quat[1] * quat[1] + quat[2] * quat[2] + quat[3] * quat[3]
    )
    w, x, y, z = (q * norm for q in quat)
    rotation = [
        [1.0 - 2.0 * (y * y + z * z), 2.0 * (x * y - w * z), 2.0 * (x * z + w * y)],
        [2.0 * (x * y + w * z), 1.0 - 2.0 * (x * x + z * z), 2.0 * (y * z - w * x)],
        [2.0 * (x * z - w * y), 2.0 * (y * z + w * x), 1.0 - 2.0 * (x * x + y * y)],
    ]
    focal_now = FOCAL_LEN * inverse
    slope_u = -focal_now * off[0] * inverse
    slope_v = -focal_now * off[1] * inverse
    cov_uu = DILATION / (WIDTH * WIDTH)
    cov_vv = DILATION / (HEIGHT * HEIGHT)
    cov_uv = 0.0
    for c in range(3):
        axis_u = focal_now * rotation[0][c] + slope_u * rotation[2][c]
        axis_v = focal_now * rotation[1][c] + slope_v * rotation[2][c]
        cov_uu = cov_uu + axis_u * axis_u * scale_sq[c]
        cov_vv = cov_vv + axis_v * axis_v * scale_sq[c]
        cov_uv = cov_uv + axis_u * axis_v * scale_sq[c]
    inv_det = 1.0 / (cov_uu * cov_vv - cov_uv * cov_uv)
    inv_dist = 1.0 / jnp.sqrt(off[0] * off[0] + off[1] * off[1] + off[2] * off[2])
    basis = sh_basis(off[0] * inv_dist, off[1] * inv_dist, off[2] * inv_dist)
    colors = []
    for ch in range(3):
        total = basis[0] * values[11 + ch]
        for k in range(1, 16):
            total = total + basis[k] * values[11 + 3 * k + ch]
        colors.append(0.5 + total)
    opacity = 1.0 / (1.0 + jnp.exp(-values[10]))
    return [
        mean_u,
        mean_v,
        cov_vv * inv_det,
        -cov_uv * inv_det,
        cov_uu * inv_det,
        *colors,
        opacity,
    ]


def pick(array, index):
    return jnp.take_along_axis(array, index, axis=1, mode="promise_in_bounds")


def lane_ids(rows=8):
    return lax.broadcasted_iota(jnp.int32, (rows, LANES), 1)


def row_ids(rows=8):
    return lax.broadcasted_iota(jnp.int32, (rows, LANES), 0)


def fill_dense(array_ref, dense_ref):
    for j in range(32):
        dense_ref[PADDED * j : PADDED * j + PARAMS, :] = array_ref[
            :, LANES * j : LANES * (j + 1)
        ]


def dense_at(dense_ref, chunk, row):
    return dense_ref[pl.ds(chunk * 8 * PADDED + row, 8, stride=PADDED), :]


def for_others(owners, body):
    def step(i, carried):
        body(i)
        return carried

    for low, high in ((40, 88), (24, 40), (88, 104), (1, 24), (104, 128)):
        lax.fori_loop(low * owners // 128, high * owners // 128, step, 0, unroll=8)


def greet(views, owners):
    view, me = lax.axis_index("view"), lax.axis_index("dev")
    barrier = pltpu.get_barrier_semaphore()
    for i in range(1, views):
        pl.semaphore_signal(
            barrier, inc=1, device_id=(lax.rem(view + i, views), me), device_id_type=MESH
        )

    def signal(i):
        pl.semaphore_signal(
            barrier, inc=1, device_id=(view, lax.rem(me + i, owners)), device_id_type=MESH
        )

    for_others(owners, signal)
    return barrier, views + owners - 2


def send_each(owners, message, landing, send_sem, recv_sem):
    view, me = lax.axis_index("view"), lax.axis_index("dev")

    def send(i):
        other = lax.rem(me + i, owners)
        pltpu.make_async_remote_copy(
            src_ref=message(other),
            dst_ref=landing(me),
            send_sem=send_sem,
            recv_sem=recv_sem,
            device_id=(view, other),
            device_id_type=MESH,
        ).start()

    for_others(owners, send)


def send_views(views, block, landing, send_sem, recv_sem):
    view, me = lax.axis_index("view"), lax.axis_index("dev")
    for i in range(1, views):
        pltpu.make_async_remote_copy(
            src_ref=block,
            dst_ref=landing(view),
            send_sem=send_sem,
            recv_sem=recv_sem,
            device_id=(lax.rem(view + i, views), me),
            device_id_type=MESH,
        ).start()


def wait_bytes(ref, semaphore):
    pltpu.make_async_copy(ref, ref, semaphore).wait()


def slot_messages(rows, center, dense, feats, outgoing):
    for chunk in range(4):
        values = [dense_at(dense, chunk, p) for p in range(PARAMS)]
        for f, value in enumerate(project(values, center)):
            feats[f, 8 * chunk : 8 * chunk + 8, :] = value
    high = rows // LANES
    low = lax.rem(rows, LANES)
    slots = [jnp.zeros((8, LANES), jnp.float32)] * FEATS
    for h in range(32):
        chosen = high == h
        for f in range(FEATS):
            source = jnp.broadcast_to(feats[f, h : h + 1, :], (8, LANES))
            slots[f] = jnp.where(chosen, pick(source, low), slots[f])
    lane = lane_ids()
    sub = row_ids()
    for block in range(16):
        index = ((block % 2) * 8 + sub) * 8 + lax.rem(lane, 8)
        message = jnp.zeros((8, LANES), jnp.float32)
        for f in range(FEATS):
            source = jnp.broadcast_to(slots[f][block // 2 : block // 2 + 1, :], (8, LANES))
            message = jnp.where(lane // 8 == f, pick(source, index), message)
        outgoing[8 * block : 8 * block + 8, :] = message


def dot(a, b, dims=((1,), (0,))):
    return lax.dot_general(
        a,
        b,
        (dims, ((), ())),
        precision=lax.Precision.HIGHEST,
        preferred_element_type=jnp.float32,
    )


def render(
    arrived_ref,
    lists,
    counts,
    ids,
    wanted_ref,
    out_ref,
    gauss,
    trans,
    gauss_grad,
    weight,
    sums,
):
    lane = lane_ids()
    sub = row_ids()
    half_of = lane // 64
    entry = lax.rem(lane, 64)
    slot = lax.rem(lists, 64)
    from_owner = slot // 8
    within = lax.rem(slot, 8)
    feats = [jnp.zeros((8, LANES), jnp.float32)] * FEATS
    for h in range(2):
        for o in range(8):
            block = arrived_ref[pl.ds(8 * h + o, 8, stride=16), :]
            chosen = (from_owner == o) & (half_of == h)
            for f in range(FEATS):
                feats[f] = jnp.where(chosen, pick(block, 8 * f + within), feats[f])
    center_u = (lax.rem(ids, TILES_X) * TILE_SIDE + TILE_SIDE // 2).astype(jnp.float32)
    center_v = (ids // TILES_X * TILE_SIDE + TILE_SIDE // 2).astype(jnp.float32)
    mean_u = feats[0] * WIDTH - center_u
    mean_v = feats[1] * HEIGHT - center_v
    quad_a = feats[2] * (-0.5 / (WIDTH * WIDTH))
    quad_b = feats[3] * (-1.0 / (WIDTH * HEIGHT))
    quad_c = feats[4] * (-0.5 / (HEIGHT * HEIGHT))
    active = entry < counts
    opacity = jnp.where(active, feats[8], 0.0)
    pixel_u = lax.rem(lane, 16).astype(jnp.float32) - 7.5
    pixel_v = [(lane // 16 + 8 * p).astype(jnp.float32) - 7.5 for p in range(2)]
    ahead = [mean_u, mean_v, quad_a, quad_b, quad_c, *feats[5:8], opacity]

    def forward(e, carried):
        through, acc, place = carried
        through, acc = list(through), list(acc)
        for h in range(2):
            index = jnp.full((8, LANES), h * 64, jnp.int32) + e
            m_u, m_v, q_a, q_b, q_c, c_0, c_1, c_2, alpha_max = (
                pick(array, index) for array in ahead
            )
            place = jnp.where((pick(slot, index) == entry) & (half_of == h), e, place)
            diff_u = pixel_u - m_u
            part = diff_u * q_b
            square = diff_u * diff_u * q_a
            for p in range(2):
                diff_v = pixel_v[p] - m_v
                bell = jnp.exp(square + diff_v * (part + q_c * diff_v))
                alpha = alpha_max * bell
                n = 2 * h + p
                before = through[n]
                gauss[e, n] = bell
                trans[e, n] = before
                share = alpha * before
                through[n] = before - share
                for ch, color in enumerate((c_0, c_1, c_2)):
                    acc[3 * n + ch] = acc[3 * n + ch] + color * share
        return tuple(through), tuple(acc), place

    zero = jnp.zeros((8, LANES), jnp.float32)
    _, acc, place = lax.fori_loop(
        0,
        64,
        forward,
        ((zero + 1.0,) * 4, (zero,) * 12, jnp.zeros((8, LANES), jnp.int32)),
        unroll=64,
    )
    residual = []
    for h in range(2):
        for p in range(2):
            for ch in range(3):
                wanted = wanted_ref[pl.ds(16 * (2 * ch + p) + h, 8, stride=2), :]
                residual.append(acc[3 * (2 * h + p) + ch] - wanted)

    def backward(i, carried):
        e = 63 - i
        behind = list(carried)
        for h in range(2):
            index = jnp.full((8, LANES), h * 64, jnp.int32) + e
            c_0, c_1, c_2, alpha_max = (pick(array, index) for array in ahead[5:9])
            for p in range(2):
                n = 2 * h + p
                bell = gauss[e, n]
                before = trans[e, n]
                alpha = alpha_max * bell
                shade = (
                    c_0 * residual[3 * n] + c_1 * residual[3 * n + 1] + c_2 * residual[3 * n + 2]
                )
                gap = shade - behind[n]
                behind[n] = behind[n] + alpha * gap
                start = pl.multiple_of(512 * h + 8 * e, 8)
                gauss_grad[p, pl.ds(start, 8), :] = before * gap * bell
                weight[p, pl.ds(start, 8), :] = alpha * before
        return tuple(behind)

    lax.fori_loop(0, 64, backward, (zero,) * 4, unroll=64)

    pix = row_ids(LANES)
    col = lane_ids(LANES)
    for_moments, for_colors = [], []
    for p in range(2):
        u = lax.rem(pix, 16).astype(jnp.float32) - 7.5
        v = (pix // 16 + 8 * p).astype(jnp.float32) - 7.5
        powers = [jnp.ones_like(u), u, v, u * u, u * v, v * v]
        table = jnp.zeros_like(u)
        for m, power in enumerate(powers):
            table = jnp.where(col == m, power, table)
        for_moments.append(table)
        stacked = [zero]
        for ch in range(3):
            for h in range(2):
                stacked.append(residual[3 * (2 * h + p) + ch])
        stacked += [zero] * 9
        for_colors.append(jnp.concatenate(stacked, axis=0).T)

    for k in range(8):
        rows = pl.ds(k, LANES, stride=8)
        total = (
            dot(gauss_grad[0, rows, :], for_moments[0])
            + dot(gauss_grad[1, rows, :], for_moments[1])
            + dot(weight[0, rows, :], for_colors[0])
            + dot(weight[1, rows, :], for_colors[1])
        )
        sums[64 * k : 64 * k + 64, :] = total.T[0:64, :]

    s_0, s_u, s_v, s_uu, s_uv, s_vv = (sums[pl.ds(m, 8, stride=64), :] for m in range(6))
    d_colors = []
    for ch in range(3):
        even = sums[pl.ds(8 + 16 * ch, 8, stride=65), :]
        odd = sums[pl.ds(16 + 16 * ch, 8, stride=65), :]
        d_colors.append(jnp.where(half_of == 0, even, odd))
    m_u = opacity * (s_u - mean_u * s_0)
    m_v = opacity * (s_v - mean_v * s_0)
    m_uu = opacity * (s_uu - mean_u * (2.0 * s_u - mean_u * s_0))
    m_vv = opacity * (s_vv - mean_v * (2.0 * s_v - mean_v * s_0))
    m_uv = opacity * (s_uv - mean_u * s_v - mean_v * (s_u - mean_u * s_0))
    grads = [
        -WIDTH * (2.0 * quad_a * m_u + quad_b * m_v),
        -HEIGHT * (2.0 * quad_c * m_v + quad_b * m_u),
        (-0.5 / (WIDTH * WIDTH)) * m_uu,
        (-1.0 / (WIDTH * HEIGHT)) * m_uv,
        (-0.5 / (HEIGHT * HEIGHT)) * m_vv,
        *d_colors,
        jnp.where(active, s_0, 0.0),
    ]
    for h in range(2):
        for o in range(8):
            base = h * 64 + o * 8 + lax.rem(lane, 8)
            index = h * 64 + pick(place, base)
            message = zero
            for f in range(FEATS):
                message = jnp.where(lane // 8 == f, pick(grads[f], index), message)
            out_ref[pl.ds(8 * h + o, 8, stride=16), :] = message


def step_sizes(rows):
    return jnp.where(
        rows < 3,
        0.00016,
        jnp.where(
            rows < 6,
            0.005,
            jnp.where(
                rows < 10,
                0.001,
                jnp.where(rows < 11, 0.05, jnp.where(rows < 14, 0.0025, 0.000125)),
            ),
        ),
    )


def slot_places(rows_all):
    place = jnp.zeros((PADDED, LANES), jnp.float32)
    sub_high = row_ids(32)
    sub_low = row_ids(LANES)
    lane_value = lane_ids(32).astype(jnp.float32)
    for i in range(32):
        rows = rows_all[i // 8][i % 8 : i % 8 + 1, :]
        hit = sub_high == jnp.broadcast_to(rows // LANES, (32, LANES))
        left = jnp.concatenate(
            [jnp.where(hit, float(i), 0.0), jnp.where(hit, lane_value, 0.0)], axis=0
        )
        right = jnp.where(
            sub_low == jnp.broadcast_to(lax.rem(rows, LANES), (LANES, LANES)), 1.0, 0.0
        )
        place = place + lax.dot_general(
            left.astype(jnp.bfloat16),
            right.astype(jnp.bfloat16),
            (((1,), (1,)), ((), ())),
            preferred_element_type=jnp.float32,
        )
    return (place[0:32] + 0.5).astype(jnp.int32), (place[32:64] + 0.5).astype(jnp.int32)


def per_tile(ref):
    values = ref[...]
    row, half_of = row_ids(), lane_ids() // 64
    spread = jnp.zeros((8, LANES), jnp.int32)
    for k in range(16):
        one = jnp.broadcast_to(values[:, k : k + 1], (8, LANES))
        spread = jnp.where((row == k // 2) & (half_of == k % 2), one, spread)
    return spread


def step_kernel(
    views,
    owners,
    params_hbm,
    first_hbm,
    second_hbm,
    center_hbm,
    rows_hbm,
    order_hbm,
    lists_hbm,
    target_hbm,
    counts_hbm,
    ids_hbm,
    new_params_hbm,
    new_first_hbm,
    new_second_hbm,
    new_params_ref,
    new_first_ref,
    new_second_ref,
    params_ref,
    first_ref,
    second_ref,
    center_ref,
    rows_ref,
    order_ref,
    order_lanes_ref,
    lists_ref,
    target_ref,
    counts_ref,
    ids_ref,
    dense,
    feats,
    outgoing,
    landed,
    packed,
    packed_landed,
    before_a,
    before_b,
    moved_a,
    moved_b,
    leaving,
    arriving,
    order_rows,
    list_rows,
    wanted,
    gauss,
    trans,
    gauss_grad,
    weight,
    sums,
    slot_grads,
    returned,
    by_slot,
    leaving_grads,
    arriving_grads,
    arrived_views,
    grads,
    load_sems,
    store_sems,
    sems,
):
    view, me = lax.axis_index("view"), lax.axis_index("dev")
    barrier, expected = greet(views, owners)
    copies = (
        (center_hbm, center_ref),
        (rows_hbm, rows_ref),
        (params_hbm, params_ref),
        (first_hbm, first_ref),
        (second_hbm, second_ref),
        (order_hbm, order_ref),
        (order_hbm, order_lanes_ref),
        (lists_hbm, lists_ref),
        (target_hbm, target_ref),
        (counts_hbm, counts_ref),
        (ids_hbm, ids_ref),
    )
    loads = [
        pltpu.make_async_copy(source, place, load_sems.at[i])
        for i, (source, place) in enumerate(copies)
    ]
    for load in loads:
        load.start()
    lane = lane_ids()
    others = pl.ds(0, owners - 1)
    other_views = pl.ds(0, views - 1)
    kept = order_ref.shape[1] - owners
    zero = jnp.zeros((8, LANES), jnp.float32)

    for load in loads[0:3]:
        load.wait()
    center = [jnp.broadcast_to(center_ref[:, i : i + 1], (8, LANES)) for i in range(3)]
    for i in range(8):
        packed[i : i + 1, :] = rows_ref[0, :, LANES * i : LANES * (i + 1)].astype(jnp.float32)
    here = zero
    for i in range(3):
        here = jnp.where(lane == i, center[i], here)
    packed[8:16, :] = here
    fill_dense(params_ref, dense)
    slot_messages(
        packed[0:8, :].astype(jnp.int32),
        center,
        dense,
        feats,
        outgoing,
    )

    fill = jnp.zeros((PADDED - PARAMS, LANES), jnp.float32)
    empty = jnp.zeros((PADDED, LANES), jnp.float32)
    loads[3].wait()
    loads[4].wait()

    def to_rows(j, carried):
        columns = pl.ds(pl.multiple_of(j * LANES, LANES), LANES)
        before_a[columns, :] = jnp.concatenate(
            [params_ref[:, columns], fill, first_ref[:, columns], fill], axis=0
        ).T
        before_b[columns, :] = jnp.concatenate([second_ref[:, columns], fill, empty], axis=0).T
        return carried

    lax.fori_loop(0, 32, to_rows, 0, unroll=8)

    for load in loads[5:]:
        load.wait()
    for t in range(owners):
        row = order_ref[0, kept + t]
        leaving[0, t : t + 1, :] = before_a[pl.ds(row, 1), :]
        leaving[1, t : t + 1, :] = before_b[pl.ds(row, 1), :]

    pl.semaphore_wait(barrier, expected)
    send_each(
        owners,
        lambda d: outgoing.at[pl.ds(d, 1)],
        lambda d: landed.at[pl.ds(d, 1)],
        sems.at[0],
        sems.at[1],
    )
    send_views(views, packed, lambda v: packed_landed.at[v], sems.at[2], sems.at[3])
    landed[pl.ds(me, 1), :] = outgoing[pl.ds(me, 1), :]
    packed_landed[view] = packed[...]

    send_each(
        owners,
        lambda d: leaving.at[:, pl.ds(d, 1)],
        lambda d: arriving.at[:, pl.ds(d, 1)],
        sems.at[4],
        sems.at[5],
    )
    arriving[:, pl.ds(me, 1), :] = leaving[:, pl.ds(me, 1), :]

    def move(t, carried):
        for u in range(32):
            row = order_ref[0, t * 32 + u]
            moved_a[pl.ds(t * 32 + u, 1), :] = before_a[pl.ds(row, 1), :]
            moved_b[pl.ds(t * 32 + u, 1), :] = before_b[pl.ds(row, 1), :]
        return carried

    lax.fori_loop(0, MOVED_EARLY // 32, move, 0)
    for k in range(16):
        list_rows[k : k + 1, 0:64] = lists_ref[0, k : k + 1, :]
    for ch in range(3):
        for p in range(2):
            n = 16 * (2 * ch + p)
            wanted[n : n + 16, :] = target_ref[ch, :, LANES * p : LANES * (p + 1)]
    even = list_rows[pl.ds(0, 8, stride=2), :]
    odd = list_rows[pl.ds(1, 8, stride=2), :]
    lists = jnp.where(lane < 64, even, pick(odd, lax.rem(lane, 64)))

    wait_bytes(landed.at[others], sems.at[1])
    render(
        landed,
        lists,
        per_tile(counts_ref),
        per_tile(ids_ref),
        wanted,
        slot_grads,
        gauss,
        trans,
        gauss_grad,
        weight,
        sums,
    )
    send_each(
        owners,
        lambda d: slot_grads.at[pl.ds(d, 1)],
        lambda d: returned.at[pl.ds(d, 1)],
        sems.at[6],
        sems.at[7],
    )
    returned[pl.ds(me, 1), :] = slot_grads[pl.ds(me, 1), :]

    lax.fori_loop(MOVED_EARLY // 32, kept // 32, move, 0)
    wait_bytes(arriving.at[:, others], sems.at[5])
    moved_a[kept:, :] = arriving[0]
    moved_b[kept:, :] = arriving[1]

    def to_columns(j, carried):
        columns = pl.ds(pl.multiple_of(j * LANES, LANES), LANES)
        both = moved_a[columns, :].T
        new_params_ref[:, columns] = both[0:PARAMS, :]
        new_first_ref[:, columns] = both[PADDED : PADDED + PARAMS, :]
        new_second_ref[:, columns] = moved_b[columns, :].T[0:PARAMS, :]
        dense[pl.ds(pl.multiple_of(j * PADDED, PADDED), PADDED), :] = both[0:PADDED, :]
        return carried

    lax.fori_loop(0, 32, to_columns, 0, unroll=8)
    for j in range(32):
        order_rows[j : j + 1, :] = order_lanes_ref[:, LANES * j : LANES * (j + 1)]
    wait_bytes(packed_landed.at[other_views], sems.at[3])
    place_high, place_low = slot_places(
        [packed_landed[v, 0:8, :].astype(jnp.int32) for v in range(views)]
    )
    place = place_high * LANES + place_low
    slot_high, slot_low = [], []
    for chunk in range(4):
        order = order_rows[8 * chunk : 8 * chunk + 8, :]
        high, low = order // LANES, lax.rem(order, LANES)
        found = jnp.zeros((8, LANES), jnp.int32)
        for h in range(32):
            source = jnp.broadcast_to(place[h : h + 1, :], (8, LANES))
            found = jnp.where(high == h, pick(source, low), found)
        slot_high.append(found // LANES)
        slot_low.append(lax.rem(found, LANES))
    centers = [
        [
            jnp.broadcast_to(packed_landed[v, 8:9, i : i + 1], (8, LANES))
            for v in range(views)
        ]
        for i in range(3)
    ]

    wait_bytes(returned.at[others], sems.at[7])
    values = [zero] * FEATS
    for o in range(16):
        block = returned[pl.ds(o, 8, stride=16), :]
        chosen = lane // 8 == o
        for f in range(FEATS):
            values[f] = jnp.where(chosen, pick(block, 8 * f + lax.rem(lane, 8)), values[f])
    for f in range(FEATS):
        by_slot[view, 8 * f : 8 * f + 8, :] = values[f]
    here = slot_high[3] // 8 == view
    gone = [zero] * FEATS
    for k in range(8):
        chosen = slot_high[3] == 8 * view + k
        for f in range(FEATS):
            source = jnp.broadcast_to(by_slot[view, 8 * f + k : 8 * f + k + 1, :], (8, LANES))
            gone[f] = jnp.where(chosen, pick(source, slot_low[3]), gone[f])
    gone.append(jnp.where(here, (view + 1).astype(jnp.float32), zero))
    rows = [found[7:8, :] for found in gone]
    rows.append(jnp.zeros((LANES - len(rows), LANES), jnp.float32))
    leaving_grads[...] = jnp.concatenate(rows, axis=0).T
    send_each(
        owners,
        lambda d: leaving_grads.at[pl.ds(d, 1)],
        lambda d: arriving_grads.at[pl.ds(d, 1)],
        sems.at[10],
        sems.at[11],
    )
    arriving_grads[pl.ds(me, 1), :] = leaving_grads[pl.ds(me, 1), :]
    send_views(views, by_slot.at[view], lambda v: by_slot.at[v], sems.at[8], sems.at[9])
    wait_bytes(by_slot.at[other_views], sems.at[9])

    def collect(chunk):
        found = [zero] * FEATS
        for h in range(32):
            chosen = slot_high[chunk] == h
            for f in range(FEATS):
                row = 8 * f + h % 8
                source = jnp.broadcast_to(by_slot[h // 8, row : row + 1, :], (8, LANES))
                found[f] = jnp.where(chosen, pick(source, slot_low[chunk]), found[f])
        return found

    bias_one = 1.0 - BETA_ONE**ADAM_STEP
    bias_two = 1.0 - BETA_TWO**ADAM_STEP
    sizes = step_sizes(row_ids(PADDED)[0:PARAMS])

    stores = []

    def finish(chunk, feat_grads, view_of, first, count):
        center = []
        for i in range(3):
            at = zero
            for v in range(views):
                at = jnp.where(view_of == v, centers[i][v], at)
            center.append(at)
        arguments = [dense_at(dense, chunk, p) for p in range(PARAMS)]
        _, pull_back = jax.vjp(lambda *args: project(args, center), *arguments)
        for p, grad in enumerate(pull_back(list(feat_grads))):
            grads[pl.ds(chunk * 8 * PADDED + p, 8, stride=PADDED), :] = grad
        for j in range(first, first + count):
            columns = slice(LANES * j, LANES * (j + 1))
            gradient = grads[PADDED * j : PADDED * j + PARAMS, :]
            new_one = BETA_ONE * new_first_ref[:, columns] + (1.0 - BETA_ONE) * gradient
            new_two = BETA_TWO * new_second_ref[:, columns] + (1.0 - BETA_TWO) * gradient * gradient
            new_params_ref[:, columns] = new_params_ref[:, columns] - sizes * (
                new_one / bias_one
            ) / (jnp.sqrt(new_two / bias_two) + ADAM_EPS)
            new_first_ref[:, columns] = new_one
            new_second_ref[:, columns] = new_two
        columns = pl.ds(LANES * first, LANES * count)
        for i, (source, place) in enumerate(
            (
                (new_params_ref, new_params_hbm),
                (new_first_ref, new_first_hbm),
                (new_second_ref, new_second_hbm),
            )
        ):
            copy = pltpu.make_async_copy(
                source.at[:, columns], place.at[:, columns], store_sems.at[len(stores)]
            )
            copy.start()
            stores.append(copy)

    for chunk in range(3):
        finish(chunk, collect(chunk), slot_high[chunk] // 8, 8 * chunk, 8)
    last = collect(3)
    last_view = slot_high[3] // 8
    finish(3, last, last_view, 24, 7)
    wait_bytes(arriving_grads.at[others], sems.at[11])
    arrived_views[view] = arriving_grads[...].T[0:16, :]
    send_views(
        views, arrived_views.at[view], lambda v: arrived_views.at[v], sems.at[12], sems.at[13]
    )
    wait_bytes(arrived_views.at[other_views], sems.at[13])
    arrived = arrived_views[0]
    for v in range(1, views):
        arrived = arrived + arrived_views[v]
    is_last = row_ids() == 7
    last = [
        jnp.where(is_last, jnp.broadcast_to(arrived[f : f + 1, :], (8, LANES)), last[f])
        for f in range(FEATS)
    ]
    arrived_view = (arrived[FEATS : FEATS + 1, :] + 0.5).astype(jnp.int32) - 1
    last_view = jnp.where(is_last, jnp.broadcast_to(arrived_view, (8, LANES)), last_view)
    finish(3, last, last_view, 31, 1)
    wait_bytes(landed.at[others], sems.at[0])
    wait_bytes(packed_landed.at[other_views], sems.at[2])
    wait_bytes(arriving.at[:, others], sems.at[4])
    wait_bytes(returned.at[others], sems.at[6])
    wait_bytes(by_slot.at[other_views], sems.at[8])
    wait_bytes(arriving_grads.at[others], sems.at[10])
    wait_bytes(arrived_views.at[other_views], sems.at[12])
    for copy in stores:
        copy.wait()


def write_kernel(
    params, first, second, new_params, new_first, new_second, held, load_sems, store_sems
):
    loads, stores = [], []
    for i, (source, place) in enumerate(
        ((params, new_params), (first, new_first), (second, new_second))
    ):
        for part in range(4):
            columns = pl.ds(1024 * part, 1024)
            n = len(loads)
            middle = held.at[i, :, columns]
            loads.append(pltpu.make_async_copy(source.at[:, columns], middle, load_sems.at[n]))
            stores.append(pltpu.make_async_copy(middle, place.at[:, columns], store_sems.at[n]))
    for load in loads:
        load.start()
    for load, store in zip(loads, stores):
        load.wait()
        store.start()
    for store in stores:
        store.wait()


VMEM = pl.BlockSpec(memory_space=pltpu.VMEM)
SMEM = pl.BlockSpec(memory_space=pltpu.SMEM)
ANY = pl.BlockSpec(memory_space=pl.ANY)
HBM = pl.BlockSpec(memory_space=pltpu.HBM)
VMEM_BYTES = 60 * 1024 * 1024


def f32(*shape):
    return jax.ShapeDtypeStruct(shape, jnp.float32)


def scratch(*shape):
    return pltpu.VMEM(shape, jnp.float32)


def per_device(
    params,
    first_moment,
    second_moment,
    cam_centers,
    target,
    send_rows,
    tile_lists,
    tile_counts,
    tile_ids,
    move_order,
):
    views, owners = lax.axis_size("view"), lax.axis_size("dev")
    by_channel = target[0].transpose(1, 0, 2)
    updated = pl.pallas_call(
        functools.partial(step_kernel, views, owners),
        out_shape=(f32(PARAMS, 4096),) * 3,
        in_specs=[HBM] * 10,
        out_specs=(ANY,) * 3,
        scratch_shapes=[
            scratch(PARAMS, 4096),
            scratch(PARAMS, 4096),
            scratch(PARAMS, 4096),
            scratch(PARAMS, 4096),
            scratch(PARAMS, 4096),
            scratch(PARAMS, 4096),
            scratch(*cam_centers.shape),
            pltpu.VMEM(send_rows.shape, jnp.int32),
            pltpu.SMEM(move_order.shape, jnp.int32),
            pltpu.VMEM(move_order.shape, jnp.int32),
            pltpu.VMEM(tile_lists.shape, jnp.int32),
            scratch(*by_channel.shape),
            pltpu.VMEM(tile_counts.shape, jnp.int32),
            pltpu.VMEM(tile_ids.shape, jnp.int32),
            scratch(32 * PADDED, LANES),
            scratch(FEATS, 32, LANES),
            scratch(owners, LANES),
            scratch(owners, LANES),
            scratch(16, LANES),
            scratch(views, 16, LANES),
            scratch(4096, LANES),
            scratch(4096, LANES),
            scratch(4096, LANES),
            scratch(4096, LANES),
            scratch(2, owners, LANES),
            scratch(2, owners, LANES),
            pltpu.VMEM((32, LANES), jnp.int32),
            pltpu.VMEM((16, LANES), jnp.int32),
            scratch(96, LANES),
            scratch(64, 4, 8, LANES),
            scratch(64, 4, 8, LANES),
            scratch(2, 1024, LANES),
            scratch(2, 1024, LANES),
            scratch(512, LANES),
            scratch(owners, LANES),
            scratch(owners, LANES),
            scratch(views, 8 * FEATS, LANES),
            scratch(owners, LANES),
            scratch(owners, LANES),
            scratch(views, 16, LANES),
            scratch(32 * PADDED, LANES),
            pltpu.SemaphoreType.DMA((11,)),
            pltpu.SemaphoreType.DMA((15,)),
            pltpu.SemaphoreType.DMA((14,)),
        ],
        compiler_params=pltpu.CompilerParams(
            vmem_limit_bytes=VMEM_BYTES, collective_id=0, has_side_effects=True
        ),
        name="step",
    )(
        params,
        first_moment,
        second_moment,
        cam_centers,
        send_rows,
        move_order,
        tile_lists,
        by_channel,
        tile_counts,
        tile_ids,
    )
    return pl.pallas_call(
        write_kernel,
        out_shape=(f32(PARAMS, 4096),) * 3,
        in_specs=[ANY] * 3,
        out_specs=(HBM,) * 3,
        scratch_shapes=[
            scratch(3, PARAMS, 4096),
            pltpu.SemaphoreType.DMA((12,)),
            pltpu.SemaphoreType.DMA((12,)),
        ],
        compiler_params=pltpu.CompilerParams(vmem_limit_bytes=VMEM_BYTES),
        name="write",
    )(*updated)


def solution(mesh):
    placed = (
        P(None, "dev"),
        P(None, "dev"),
        P(None, "dev"),
        P("view", None),
        P("view", "dev", None, None),
        P("view", "dev", None),
        P("view", "dev", None),
        P("view", "dev"),
        P("view", "dev"),
        P("dev", None),
    )
    return jax.shard_map(
        per_device,
        mesh=mesh,
        in_specs=placed,
        out_specs=(P(None, "dev"), P(None, "dev"), P(None, "dev")),
        check_vma=False,
    )
```

```python
import functools

import jax
import jax.numpy as jnp
from jax import lax
from jax.experimental import pallas as pl
from jax.experimental.pallas import tpu as pltpu
from jax.sharding import PartitionSpec as P

PARAMS = 59
PADDED = 64
FEATS = 9
LANES = 128
TILE_SIDE = 16
TILES_X = 64
ADAM_STEP = 1000
FOCAL_LEN = 1.2
DILATION = 0.3
SH_C0 = 0.28209479177387814
SH_C1 = 0.4886025119029199
SH_C2 = (
    1.0925484305920792,
    -1.0925484305920792,
    0.31539156525252005,
    -1.0925484305920792,
    0.5462742152960396,
)
SH_C3 = (
    -0.5900435899266435,
    2.890611442640554,
    -0.4570457994644658,
    0.3731763325901154,
    -0.4570457994644658,
    1.445305721320277,
    -0.5900435899266435,
)
BETA_ONE = 0.9
BETA_TWO = 0.999
ADAM_EPS = 1e-08
MESH = pl.DeviceIdType.MESH
MOVED_EARLY = 2816
WIDTH = 1024.0
HEIGHT = 512.0


def sh_basis(x, y, z):
    xx, yy, zz = x * x, y * y, z * z
    return [
        SH_C0 + 0.0 * x,
        -SH_C1 * y,
        SH_C1 * z,
        -SH_C1 * x,
        SH_C2[0] * x * y,
        SH_C2[1] * y * z,
        SH_C2[2] * (2.0 * zz - xx - yy),
        SH_C2[3] * x * z,
        SH_C2[4] * (xx - yy),
        SH_C3[0] * y * (3.0 * xx - yy),
        SH_C3[1] * x * y * z,
        SH_C3[2] * y * (4.0 * zz - xx - yy),
        SH_C3[3] * z * (2.0 * zz - 3.0 * xx - 3.0 * yy),
        SH_C3[4] * x * (4.0 * zz - xx - yy),
        SH_C3[5] * z * (xx - yy),
        SH_C3[6] * x * (xx - 3.0 * yy),
    ]


def project(values, center):
    off = [values[i] - center[i] for i in range(3)]
    inverse = 1.0 / off[2]
    mean_u = 0.5 + FOCAL_LEN * off[0] * inverse
    mean_v = 0.5 + FOCAL_LEN * off[1] * inverse
    scale_sq = [jnp.exp(2.0 * values[3 + i]) for i in range(3)]
    quat = values[6:10]
    norm = lax.rsqrt(
        quat[0] * quat[0] + quat[1] * quat[1] + quat[2] * quat[2] + quat[3] * quat[3]
    )
    w, x, y, z = (q * norm for q in quat)
    rotation = [
        [1.0 - 2.0 * (y * y + z * z), 2.0 * (x * y - w * z), 2.0 * (x * z + w * y)],
        [2.0 * (x * y + w * z), 1.0 - 2.0 * (x * x + z * z), 2.0 * (y * z - w * x)],
        [2.0 * (x * z - w * y), 2.0 * (y * z + w * x), 1.0 - 2.0 * (x * x + y * y)],
    ]
    focal_now = FOCAL_LEN * inverse
    slope_u = -focal_now * off[0] * inverse
    slope_v = -focal_now * off[1] * inverse
    cov_uu = DILATION / (WIDTH * WIDTH)
    cov_vv = DILATION / (HEIGHT * HEIGHT)
    cov_uv = 0.0
    for c in range(3):
        axis_u = focal_now * rotation[0][c] + slope_u * rotation[2][c]
        axis_v = focal_now * rotation[1][c] + slope_v * rotation[2][c]
        cov_uu = cov_uu + axis_u * axis_u * scale_sq[c]
        cov_vv = cov_vv + axis_v * axis_v * scale_sq[c]
        cov_uv = cov_uv + axis_u * axis_v * scale_sq[c]
    inv_det = 1.0 / (cov_uu * cov_vv - cov_uv * cov_uv)
    inv_dist = 1.0 / jnp.sqrt(off[0] * off[0] + off[1] * off[1] + off[2] * off[2])
    basis = sh_basis(off[0] * inv_dist, off[1] * inv_dist, off[2] * inv_dist)
    colors = []
    for ch in range(3):
        total = basis[0] * values[11 + ch]
        for k in range(1, 16):
            total = total + basis[k] * values[11 + 3 * k + ch]
        colors.append(0.5 + total)
    opacity = 1.0 / (1.0 + jnp.exp(-values[10]))
    return [
        mean_u,
        mean_v,
        cov_vv * inv_det,
        -cov_uv * inv_det,
        cov_uu * inv_det,
        *colors,
        opacity,
    ]


def pick(array, index):
    return jnp.take_along_axis(array, index, axis=1, mode="promise_in_bounds")


def lane_ids(rows=8):
    return lax.broadcasted_iota(jnp.int32, (rows, LANES), 1)


def row_ids(rows=8):
    return lax.broadcasted_iota(jnp.int32, (rows, LANES), 0)


def fill_dense(array_ref, dense_ref):
    for j in range(32):
        dense_ref[PADDED * j : PADDED * j + PARAMS, :] = array_ref[
            :, LANES * j : LANES * (j + 1)
        ]


def dense_at(dense_ref, chunk, row):
    return dense_ref[pl.ds(chunk * 8 * PADDED + row, 8, stride=PADDED), :]


def for_others(owners, body):
    def step(i, carried):
        body(i)
        return carried

    for low, high in ((40, 88), (24, 40), (88, 104), (1, 24), (104, 128)):
        lax.fori_loop(low * owners // 128, high * owners // 128, step, 0, unroll=8)


def greet(views, owners):
    view, me = lax.axis_index("view"), lax.axis_index("dev")
    barrier = pltpu.get_barrier_semaphore()
    for i in range(1, views):
        pl.semaphore_signal(
            barrier, inc=1, device_id=(lax.rem(view + i, views), me), device_id_type=MESH
        )

    def signal(i):
        pl.semaphore_signal(
            barrier, inc=1, device_id=(view, lax.rem(me + i, owners)), device_id_type=MESH
        )

    for_others(owners, signal)
    return barrier, views + owners - 2


def send_each(owners, message, landing, send_sem, recv_sem):
    view, me = lax.axis_index("view"), lax.axis_index("dev")

    def send(i):
        other = lax.rem(me + i, owners)
        pltpu.make_async_remote_copy(
            src_ref=message(other),
            dst_ref=landing(me),
            send_sem=send_sem,
            recv_sem=recv_sem,
            device_id=(view, other),
            device_id_type=MESH,
        ).start()

    for_others(owners, send)


def send_views(views, block, landing, send_sem, recv_sem):
    view, me = lax.axis_index("view"), lax.axis_index("dev")
    for i in range(1, views):
        pltpu.make_async_remote_copy(
            src_ref=block,
            dst_ref=landing(view),
            send_sem=send_sem,
            recv_sem=recv_sem,
            device_id=(lax.rem(view + i, views), me),
            device_id_type=MESH,
        ).start()


def wait_bytes(ref, semaphore):
    pltpu.make_async_copy(ref, ref, semaphore).wait()


def slot_messages(rows, center, dense, feats, outgoing):
    for chunk in range(4):
        values = [dense_at(dense, chunk, p) for p in range(PARAMS)]
        for f, value in enumerate(project(values, center)):
            feats[f, 8 * chunk : 8 * chunk + 8, :] = value
    high = rows // LANES
    low = lax.rem(rows, LANES)
    slots = [jnp.zeros((8, LANES), jnp.float32)] * FEATS
    for h in range(32):
        chosen = high == h
        for f in range(FEATS):
            source = jnp.broadcast_to(feats[f, h : h + 1, :], (8, LANES))
            slots[f] = jnp.where(chosen, pick(source, low), slots[f])
    lane = lane_ids()
    sub = row_ids()
    for block in range(16):
        index = ((block % 2) * 8 + sub) * 8 + lax.rem(lane, 8)
        message = jnp.zeros((8, LANES), jnp.float32)
        for f in range(FEATS):
            source = jnp.broadcast_to(slots[f][block // 2 : block // 2 + 1, :], (8, LANES))
            message = jnp.where(lane // 8 == f, pick(source, index), message)
        outgoing[8 * block : 8 * block + 8, :] = message


def dot(a, b, dims=((1,), (0,))):
    return lax.dot_general(
        a,
        b,
        (dims, ((), ())),
        precision=lax.Precision.HIGHEST,
        preferred_element_type=jnp.float32,
    )


def render(
    arrived_ref,
    lists,
    counts,
    ids,
    wanted_ref,
    out_ref,
    gauss,
    trans,
    gauss_grad,
    weight,
    product,
    sums,
):
    lane = lane_ids()
    sub = row_ids()
    half_of = lane // 64
    entry = lax.rem(lane, 64)
    slot = lax.rem(lists, 64)
    from_owner = slot // 8
    within = lax.rem(slot, 8)
    feats = [jnp.zeros((8, LANES), jnp.float32)] * FEATS
    for h in range(2):
        for o in range(8):
            block = arrived_ref[pl.ds(8 * h + o, 8, stride=16), :]
            chosen = (from_owner == o) & (half_of == h)
            for f in range(FEATS):
                feats[f] = jnp.where(chosen, pick(block, 8 * f + within), feats[f])
    center_u = (lax.rem(ids, TILES_X) * TILE_SIDE + TILE_SIDE // 2).astype(jnp.float32)
    center_v = (ids // TILES_X * TILE_SIDE + TILE_SIDE // 2).astype(jnp.float32)
    mean_u = feats[0] * WIDTH - center_u
    mean_v = feats[1] * HEIGHT - center_v
    quad_a = feats[2] * (-0.5 / (WIDTH * WIDTH))
    quad_b = feats[3] * (-1.0 / (WIDTH * HEIGHT))
    quad_c = feats[4] * (-0.5 / (HEIGHT * HEIGHT))
    active = entry < counts
    opacity = jnp.where(active, feats[8], 0.0)
    pixel_u = lax.rem(lane, 16).astype(jnp.float32) - 7.5
    pixel_v = [(lane // 16 + 8 * p).astype(jnp.float32) - 7.5 for p in range(2)]
    ahead = [mean_u, mean_v, quad_a, quad_b, quad_c, *feats[5:8], opacity]

    def forward(e, carried):
        through, acc, place = carried
        through, acc = list(through), list(acc)
        for h in range(2):
            index = jnp.full((8, LANES), h * 64, jnp.int32) + e
            m_u, m_v, q_a, q_b, q_c, c_0, c_1, c_2, alpha_max = (
                pick(array, index) for array in ahead
            )
            place = jnp.where((pick(slot, index) == entry) & (half_of == h), e, place)
            diff_u = pixel_u - m_u
            part = diff_u * q_b
            square = diff_u * diff_u * q_a
            for p in range(2):
                diff_v = pixel_v[p] - m_v
                bell = jnp.exp(square + diff_v * (part + q_c * diff_v))
                alpha = alpha_max * bell
                n = 2 * h + p
                before = through[n]
                gauss[e, n] = bell
                trans[e, n] = before
                share = alpha * before
                through[n] = before - share
                for ch, color in enumerate((c_0, c_1, c_2)):
                    acc[3 * n + ch] = acc[3 * n + ch] + color * share
        return tuple(through), tuple(acc), place

    zero = jnp.zeros((8, LANES), jnp.float32)
    _, acc, place = lax.fori_loop(
        0,
        64,
        forward,
        ((zero + 1.0,) * 4, (zero,) * 12, jnp.zeros((8, LANES), jnp.int32)),
        unroll=64,
    )
    residual = []
    for h in range(2):
        for p in range(2):
            for ch in range(3):
                wanted = wanted_ref[pl.ds(16 * (2 * ch + p) + h, 8, stride=2), :]
                residual.append(acc[3 * (2 * h + p) + ch] - wanted)

    def backward(i, carried):
        e = 63 - i
        behind = list(carried)
        for h in range(2):
            index = jnp.full((8, LANES), h * 64, jnp.int32) + e
            c_0, c_1, c_2, alpha_max = (pick(array, index) for array in ahead[5:9])
            for p in range(2):
                n = 2 * h + p
                bell = gauss[e, n]
                before = trans[e, n]
                alpha = alpha_max * bell
                shade = (
                    c_0 * residual[3 * n] + c_1 * residual[3 * n + 1] + c_2 * residual[3 * n + 2]
                )
                gap = shade - behind[n]
                behind[n] = behind[n] + alpha * gap
                start = pl.multiple_of(512 * h + 8 * e, 8)
                gauss_grad[pl.ds(start, 8), LANES * p : LANES * (p + 1)] = before * gap * bell
                weight[pl.ds(start, 8), LANES * p : LANES * (p + 1)] = alpha * before
        return tuple(behind)

    lax.fori_loop(0, 64, backward, (zero,) * 4, unroll=64)

    pix = row_ids(LANES)
    col = lane_ids(LANES)
    for_moments, for_colors = [], []
    for p in range(2):
        u = lax.rem(pix, 16).astype(jnp.float32) - 7.5
        v = (pix // 16 + 8 * p).astype(jnp.float32) - 7.5
        powers = [jnp.ones_like(u), u, v, u * u, u * v, v * v]
        table = jnp.zeros_like(u)
        for m, power in enumerate(powers):
            table = jnp.where(col == m, power, table)
        for_moments.append(table)
        stacked = [zero]
        for ch in range(3):
            for h in range(2):
                stacked.append(residual[3 * (2 * h + p) + ch])
        stacked += [zero] * 9
        for_colors.append(jnp.concatenate(stacked, axis=0).T)

    for_moments = jnp.concatenate(for_moments, axis=0)
    for_colors = jnp.concatenate(for_colors, axis=0)
    for part in range(4):
        rows = slice(256 * part, 256 * (part + 1))
        product[rows, :] = dot(gauss_grad[rows, :], for_moments) + dot(
            weight[rows, :], for_colors
        )
    for k in range(8):
        sums[64 * k : 64 * k + 64, :] = product[pl.ds(k, LANES, stride=8), :].T[0:64, :]

    s_0, s_u, s_v, s_uu, s_uv, s_vv = (sums[pl.ds(m, 8, stride=64), :] for m in range(6))
    d_colors = []
    for ch in range(3):
        even = sums[pl.ds(8 + 16 * ch, 8, stride=65), :]
        odd = sums[pl.ds(16 + 16 * ch, 8, stride=65), :]
        d_colors.append(jnp.where(half_of == 0, even, odd))
    m_u = opacity * (s_u - mean_u * s_0)
    m_v = opacity * (s_v - mean_v * s_0)
    m_uu = opacity * (s_uu - mean_u * (2.0 * s_u - mean_u * s_0))
    m_vv = opacity * (s_vv - mean_v * (2.0 * s_v - mean_v * s_0))
    m_uv = opacity * (s_uv - mean_u * s_v - mean_v * (s_u - mean_u * s_0))
    grads = [
        -WIDTH * (2.0 * quad_a * m_u + quad_b * m_v),
        -HEIGHT * (2.0 * quad_c * m_v + quad_b * m_u),
        (-0.5 / (WIDTH * WIDTH)) * m_uu,
        (-1.0 / (WIDTH * HEIGHT)) * m_uv,
        (-0.5 / (HEIGHT * HEIGHT)) * m_vv,
        *d_colors,
        jnp.where(active, s_0, 0.0),
    ]
    for h in range(2):
        for o in range(8):
            base = h * 64 + o * 8 + lax.rem(lane, 8)
            index = h * 64 + pick(place, base)
            message = zero
            for f in range(FEATS):
                message = jnp.where(lane // 8 == f, pick(grads[f], index), message)
            out_ref[pl.ds(8 * h + o, 8, stride=16), :] = message


def step_sizes(rows):
    return jnp.where(
        rows < 3,
        0.00016,
        jnp.where(
            rows < 6,
            0.005,
            jnp.where(
                rows < 10,
                0.001,
                jnp.where(rows < 11, 0.05, jnp.where(rows < 14, 0.0025, 0.000125)),
            ),
        ),
    )


def slot_places(rows_all):
    place = jnp.zeros((PADDED, LANES), jnp.float32)
    sub_high = row_ids(32)
    sub_low = row_ids(LANES)
    lane_value = lane_ids(32).astype(jnp.float32)
    for i in range(32):
        rows = rows_all[i // 8][i % 8 : i % 8 + 1, :]
        hit = sub_high == jnp.broadcast_to(rows // LANES, (32, LANES))
        left = jnp.concatenate(
            [jnp.where(hit, float(i), 0.0), jnp.where(hit, lane_value, 0.0)], axis=0
        )
        right = jnp.where(
            sub_low == jnp.broadcast_to(lax.rem(rows, LANES), (LANES, LANES)), 1.0, 0.0
        )
        place = place + lax.dot_general(
            left.astype(jnp.bfloat16),
            right.astype(jnp.bfloat16),
            (((1,), (1,)), ((), ())),
            preferred_element_type=jnp.float32,
        )
    return (place[0:32] + 0.5).astype(jnp.int32), (place[32:64] + 0.5).astype(jnp.int32)


def adam(values, first, second, gradient):
    bias_one = 1.0 - BETA_ONE**ADAM_STEP
    bias_two = 1.0 - BETA_TWO**ADAM_STEP
    sizes = step_sizes(row_ids(PADDED)[0:PARAMS])
    new_one = BETA_ONE * first + (1.0 - BETA_ONE) * gradient
    new_two = BETA_TWO * second + (1.0 - BETA_TWO) * gradient * gradient
    updated = values - sizes * (new_one / bias_one) / (jnp.sqrt(new_two / bias_two) + ADAM_EPS)
    return updated, new_one, new_two


def per_tile(ref):
    values = ref[...]
    row, half_of = row_ids(), lane_ids() // 64
    spread = jnp.zeros((8, LANES), jnp.int32)
    for k in range(16):
        one = jnp.broadcast_to(values[:, k : k + 1], (8, LANES))
        spread = jnp.where((row == k // 2) & (half_of == k % 2), one, spread)
    return spread


def step_kernel(
    views,
    owners,
    params_hbm,
    first_hbm,
    second_hbm,
    center_hbm,
    rows_hbm,
    order_hbm,
    lists_hbm,
    target_hbm,
    counts_hbm,
    ids_hbm,
    new_params_hbm,
    new_first_hbm,
    new_second_hbm,
    last_hbm,
    new_params_ref,
    new_first_ref,
    new_second_ref,
    params_ref,
    first_ref,
    second_ref,
    center_ref,
    rows_ref,
    order_ref,
    order_lanes_ref,
    lists_ref,
    target_ref,
    counts_ref,
    ids_ref,
    dense,
    feats,
    outgoing,
    landed,
    packed,
    packed_landed,
    before_a,
    before_b,
    moved_a,
    moved_b,
    leaving,
    arriving,
    order_rows,
    list_rows,
    wanted,
    gauss,
    trans,
    gauss_grad,
    weight,
    product,
    sums,
    slot_grads,
    returned,
    by_slot,
    leaving_grads,
    arriving_grads,
    arrived_views,
    last,
    grads,
    load_sems,
    store_sems,
    sems,
):
    view, me = lax.axis_index("view"), lax.axis_index("dev")
    barrier, expected = greet(views, owners)
    copies = (
        (center_hbm, center_ref),
        (rows_hbm, rows_ref),
        (params_hbm, params_ref),
        (first_hbm, first_ref),
        (second_hbm, second_ref),
        (order_hbm, order_ref),
        (order_hbm, order_lanes_ref),
        (lists_hbm, lists_ref),
        (target_hbm, target_ref),
        (counts_hbm, counts_ref),
        (ids_hbm, ids_ref),
    )
    loads = [
        pltpu.make_async_copy(source, place, load_sems.at[i])
        for i, (source, place) in enumerate(copies)
    ]
    for load in loads:
        load.start()
    lane = lane_ids()
    others = pl.ds(0, owners - 1)
    other_views = pl.ds(0, views - 1)
    kept = order_ref.shape[1] - owners
    zero = jnp.zeros((8, LANES), jnp.float32)

    for load in loads[0:3]:
        load.wait()
    center = [jnp.broadcast_to(center_ref[:, i : i + 1], (8, LANES)) for i in range(3)]
    for i in range(8):
        packed[i : i + 1, :] = rows_ref[0, :, LANES * i : LANES * (i + 1)].astype(jnp.float32)
    here = zero
    for i in range(3):
        here = jnp.where(lane == i, center[i], here)
    packed[8:16, :] = here
    fill_dense(params_ref, dense)
    slot_messages(
        packed[0:8, :].astype(jnp.int32),
        center,
        dense,
        feats,
        outgoing,
    )

    fill = jnp.zeros((PADDED - PARAMS, LANES), jnp.float32)
    empty = jnp.zeros((PADDED, LANES), jnp.float32)
    loads[3].wait()
    loads[4].wait()

    def to_rows(j, carried):
        columns = pl.ds(pl.multiple_of(j * LANES, LANES), LANES)
        before_a[columns, :] = jnp.concatenate(
            [params_ref[:, columns], fill, first_ref[:, columns], fill], axis=0
        ).T
        before_b[columns, :] = jnp.concatenate([second_ref[:, columns], fill, empty], axis=0).T
        return carried

    lax.fori_loop(0, 32, to_rows, 0, unroll=8)

    for load in loads[5:]:
        load.wait()
    for t in range(owners):
        row = order_ref[0, kept + t]
        leaving[0, t : t + 1, :] = before_a[pl.ds(row, 1), :]
        leaving[1, t : t + 1, :] = before_b[pl.ds(row, 1), :]

    pl.semaphore_wait(barrier, expected)
    send_each(
        owners,
        lambda d: outgoing.at[pl.ds(d, 1)],
        lambda d: landed.at[pl.ds(d, 1)],
        sems.at[0],
        sems.at[1],
    )
    send_views(views, packed, lambda v: packed_landed.at[v], sems.at[2], sems.at[3])
    landed[pl.ds(me, 1), :] = outgoing[pl.ds(me, 1), :]
    packed_landed[view] = packed[...]

    send_each(
        owners,
        lambda d: leaving.at[:, pl.ds(d, 1)],
        lambda d: arriving.at[:, pl.ds(d, 1)],
        sems.at[4],
        sems.at[5],
    )
    arriving[:, pl.ds(me, 1), :] = leaving[:, pl.ds(me, 1), :]

    def move(t, carried):
        for u in range(32):
            row = order_ref[0, t * 32 + u]
            moved_a[pl.ds(t * 32 + u, 1), :] = before_a[pl.ds(row, 1), :]
            moved_b[pl.ds(t * 32 + u, 1), :] = before_b[pl.ds(row, 1), :]
        return carried

    lax.fori_loop(0, MOVED_EARLY // 32, move, 0)
    for k in range(16):
        list_rows[k : k + 1, 0:64] = lists_ref[0, k : k + 1, :]
    for ch in range(3):
        for p in range(2):
            n = 16 * (2 * ch + p)
            wanted[n : n + 16, :] = target_ref[ch, :, LANES * p : LANES * (p + 1)]
    even = list_rows[pl.ds(0, 8, stride=2), :]
    odd = list_rows[pl.ds(1, 8, stride=2), :]
    lists = jnp.where(lane < 64, even, pick(odd, lax.rem(lane, 64)))

    wait_bytes(landed.at[others], sems.at[1])
    render(
        landed,
        lists,
        per_tile(counts_ref),
        per_tile(ids_ref),
        wanted,
        slot_grads,
        gauss,
        trans,
        gauss_grad,
        weight,
        product,
        sums,
    )
    send_each(
        owners,
        lambda d: slot_grads.at[pl.ds(d, 1)],
        lambda d: returned.at[pl.ds(d, 1)],
        sems.at[6],
        sems.at[7],
    )
    returned[pl.ds(me, 1), :] = slot_grads[pl.ds(me, 1), :]

    lax.fori_loop(MOVED_EARLY // 32, kept // 32, move, 0)
    wait_bytes(arriving.at[:, others], sems.at[5])
    moved_a[kept:, :] = arriving[0]
    moved_b[kept:, :] = arriving[1]

    def to_columns(j, carried):
        columns = pl.ds(pl.multiple_of(j * LANES, LANES), LANES)
        both = moved_a[columns, :].T
        new_params_ref[:, columns] = both[0:PARAMS, :]
        new_first_ref[:, columns] = both[PADDED : PADDED + PARAMS, :]
        new_second_ref[:, columns] = moved_b[columns, :].T[0:PARAMS, :]
        dense[pl.ds(pl.multiple_of(j * PADDED, PADDED), PADDED), :] = both[0:PADDED, :]
        return carried

    lax.fori_loop(0, 32, to_columns, 0, unroll=8)
    for j in range(32):
        order_rows[j : j + 1, :] = order_lanes_ref[:, LANES * j : LANES * (j + 1)]
    wait_bytes(packed_landed.at[other_views], sems.at[3])
    place_high, place_low = slot_places(
        [packed_landed[v, 0:8, :].astype(jnp.int32) for v in range(views)]
    )
    place = place_high * LANES + place_low
    slot_high, slot_low = [], []
    for chunk in range(4):
        order = order_rows[8 * chunk : 8 * chunk + 8, :]
        high, low = order // LANES, lax.rem(order, LANES)
        found = jnp.zeros((8, LANES), jnp.int32)
        for h in range(32):
            source = jnp.broadcast_to(place[h : h + 1, :], (8, LANES))
            found = jnp.where(high == h, pick(source, low), found)
        slot_high.append(found // LANES)
        slot_low.append(lax.rem(found, LANES))
    centers = [
        [
            jnp.broadcast_to(packed_landed[v, 8:9, i : i + 1], (8, LANES))
            for v in range(views)
        ]
        for i in range(3)
    ]

    wait_bytes(returned.at[others], sems.at[7])
    values = [zero] * FEATS
    for o in range(16):
        block = returned[pl.ds(o, 8, stride=16), :]
        chosen = lane // 8 == o
        for f in range(FEATS):
            values[f] = jnp.where(chosen, pick(block, 8 * f + lax.rem(lane, 8)), values[f])
    for f in range(FEATS):
        by_slot[view, 8 * f : 8 * f + 8, :] = values[f]
    here = slot_high[3] // 8 == view
    gone = [zero] * FEATS
    for k in range(8):
        chosen = slot_high[3] == 8 * view + k
        for f in range(FEATS):
            source = jnp.broadcast_to(by_slot[view, 8 * f + k : 8 * f + k + 1, :], (8, LANES))
            gone[f] = jnp.where(chosen, pick(source, slot_low[3]), gone[f])
    gone.append(jnp.where(here, (view + 1).astype(jnp.float32), zero))
    rows = [found[7:8, :] for found in gone]
    rows.append(jnp.zeros((LANES - len(rows), LANES), jnp.float32))
    leaving_grads[...] = jnp.concatenate(rows, axis=0).T
    send_each(
        owners,
        lambda d: leaving_grads.at[pl.ds(d, 1)],
        lambda d: arriving_grads.at[pl.ds(d, 1)],
        sems.at[10],
        sems.at[11],
    )
    arriving_grads[pl.ds(me, 1), :] = leaving_grads[pl.ds(me, 1), :]
    send_views(views, by_slot.at[view], lambda v: by_slot.at[v], sems.at[8], sems.at[9])
    wait_bytes(by_slot.at[other_views], sems.at[9])

    def collect(chunk):
        found = [zero] * FEATS
        for h in range(32):
            chosen = slot_high[chunk] == h
            for f in range(FEATS):
                row = 8 * f + h % 8
                source = jnp.broadcast_to(by_slot[h // 8, row : row + 1, :], (8, LANES))
                found[f] = jnp.where(chosen, pick(source, slot_low[chunk]), found[f])
        return found

    stores = []

    def finish(chunk, feat_grads, count):
        view_of = slot_high[chunk] // 8
        center = []
        for i in range(3):
            at = zero
            for v in range(views):
                at = jnp.where(view_of == v, centers[i][v], at)
            center.append(at)
        arguments = [dense_at(dense, chunk, p) for p in range(PARAMS)]
        _, pull_back = jax.vjp(lambda *args: project(args, center), *arguments)
        for p, grad in enumerate(pull_back(list(feat_grads))):
            grads[pl.ds(chunk * 8 * PADDED + p, 8, stride=PADDED), :] = grad
        for j in range(8 * chunk, 8 * chunk + count):
            columns = slice(LANES * j, LANES * (j + 1))
            gradient = grads[PADDED * j : PADDED * j + PARAMS, :]
            (
                new_params_ref[:, columns],
                new_first_ref[:, columns],
                new_second_ref[:, columns],
            ) = adam(
                new_params_ref[:, columns],
                new_first_ref[:, columns],
                new_second_ref[:, columns],
                gradient,
            )
        columns = pl.ds(8 * LANES * chunk, 8 * LANES)
        for i, (source, place) in enumerate(
            (
                (new_params_ref, new_params_hbm),
                (new_first_ref, new_first_hbm),
                (new_second_ref, new_second_hbm),
            )
        ):
            copy = pltpu.make_async_copy(
                source.at[:, columns], place.at[:, columns], store_sems.at[len(stores)]
            )
            copy.start()
            stores.append(copy)

    for chunk in range(4):
        finish(chunk, collect(chunk), 8 if chunk < 3 else 7)
    for v in range(views):
        last[16 + 16 * v : 32 + 16 * v, :] = packed_landed[v]
    wait_bytes(arriving_grads.at[others], sems.at[11])
    arrived_views[view] = arriving_grads[...].T[0:16, :]
    send_views(
        views, arrived_views.at[view], lambda v: arrived_views.at[v], sems.at[12], sems.at[13]
    )
    wait_bytes(arrived_views.at[other_views], sems.at[13])
    arrived = arrived_views[0]
    for v in range(1, views):
        arrived = arrived + arrived_views[v]
    last[0:16, :] = arrived
    copy = pltpu.make_async_copy(last, last_hbm, store_sems.at[len(stores)])
    copy.start()
    stores.append(copy)
    wait_bytes(landed.at[others], sems.at[0])
    wait_bytes(packed_landed.at[other_views], sems.at[2])
    wait_bytes(arriving.at[:, others], sems.at[4])
    wait_bytes(returned.at[others], sems.at[6])
    wait_bytes(by_slot.at[other_views], sems.at[8])
    wait_bytes(arriving_grads.at[others], sems.at[10])
    wait_bytes(arrived_views.at[other_views], sems.at[12])
    for copy in stores:
        copy.wait()


def write_kernel(
    params,
    first,
    second,
    last_hbm,
    new_params,
    new_first,
    new_second,
    held,
    last,
    grads,
    load_sems,
    store_sems,
):
    ends = ((params, new_params), (first, new_first), (second, new_second))
    parts = [pl.ds(3968, 128)] + [pl.ds(1024 * k, 1024) for k in range(3)] + [pl.ds(3072, 896)]
    loads, stores = [pltpu.make_async_copy(last_hbm, last, load_sems.at[0])], []
    for columns in parts:
        for i, (source, place) in enumerate(ends):
            middle = held.at[i, :, columns]
            loads.append(
                pltpu.make_async_copy(source.at[:, columns], middle, load_sems.at[len(loads)])
            )
            stores.append(
                pltpu.make_async_copy(middle, place.at[:, columns], store_sems.at[len(stores)])
            )
    for load in loads:
        load.start()
    for load in loads[0:4]:
        load.wait()
    columns = slice(3968, 4096)
    view_of = (last[FEATS : FEATS + 1, :] + 0.5).astype(jnp.int32) - 1
    center = []
    for i in range(3):
        at = jnp.zeros((1, LANES), jnp.float32)
        for v in range(last.shape[0] // 16 - 1):
            row = 16 * v + 24
            one = jnp.broadcast_to(last[row : row + 1, i : i + 1], (1, LANES))
            at = jnp.where(view_of == v, one, at)
        center.append(at)
    arguments = [held[0, p : p + 1, columns] for p in range(PARAMS)]
    _, pull_back = jax.vjp(lambda *args: project(args, center), *arguments)
    for p, grad in enumerate(pull_back([last[f : f + 1, :] for f in range(FEATS)])):
        grads[p : p + 1, :] = grad
    held[0, :, columns], held[1, :, columns], held[2, :, columns] = adam(
        held[0, :, columns], held[1, :, columns], held[2, :, columns], grads[0:PARAMS, :]
    )
    for store in stores[0:3]:
        store.start()
    for load, store in zip(loads[4:], stores[3:]):
        load.wait()
        store.start()
    for store in stores:
        store.wait()


VMEM = pl.BlockSpec(memory_space=pltpu.VMEM)
SMEM = pl.BlockSpec(memory_space=pltpu.SMEM)
ANY = pl.BlockSpec(memory_space=pl.ANY)
HBM = pl.BlockSpec(memory_space=pltpu.HBM)
VMEM_BYTES = 60 * 1024 * 1024


def f32(*shape):
    return jax.ShapeDtypeStruct(shape, jnp.float32)


def scratch(*shape):
    return pltpu.VMEM(shape, jnp.float32)


def per_device(
    params,
    first_moment,
    second_moment,
    cam_centers,
    target,
    send_rows,
    tile_lists,
    tile_counts,
    tile_ids,
    move_order,
):
    views, owners = lax.axis_size("view"), lax.axis_size("dev")
    by_channel = target[0].transpose(1, 0, 2)
    updated = pl.pallas_call(
        functools.partial(step_kernel, views, owners),
        out_shape=(f32(PARAMS, 4096),) * 3 + (f32(16 + 16 * views, LANES),),
        in_specs=[HBM] * 10,
        out_specs=(ANY,) * 4,
        scratch_shapes=[
            scratch(PARAMS, 4096),
            scratch(PARAMS, 4096),
            scratch(PARAMS, 4096),
            scratch(PARAMS, 4096),
            scratch(PARAMS, 4096),
            scratch(PARAMS, 4096),
            scratch(*cam_centers.shape),
            pltpu.VMEM(send_rows.shape, jnp.int32),
            pltpu.SMEM(move_order.shape, jnp.int32),
            pltpu.VMEM(move_order.shape, jnp.int32),
            pltpu.VMEM(tile_lists.shape, jnp.int32),
            scratch(*by_channel.shape),
            pltpu.VMEM(tile_counts.shape, jnp.int32),
            pltpu.VMEM(tile_ids.shape, jnp.int32),
            scratch(32 * PADDED, LANES),
            scratch(FEATS, 32, LANES),
            scratch(owners, LANES),
            scratch(owners, LANES),
            scratch(16, LANES),
            scratch(views, 16, LANES),
            scratch(4096, LANES),
            scratch(4096, LANES),
            scratch(4096, LANES),
            scratch(4096, LANES),
            scratch(2, owners, LANES),
            scratch(2, owners, LANES),
            pltpu.VMEM((32, LANES), jnp.int32),
            pltpu.VMEM((16, LANES), jnp.int32),
            scratch(96, LANES),
            scratch(64, 4, 8, LANES),
            scratch(64, 4, 8, LANES),
            scratch(1024, 2 * LANES),
            scratch(1024, 2 * LANES),
            scratch(1024, LANES),
            scratch(512, LANES),
            scratch(owners, LANES),
            scratch(owners, LANES),
            scratch(views, 8 * FEATS, LANES),
            scratch(owners, LANES),
            scratch(owners, LANES),
            scratch(views, 16, LANES),
            scratch(16 + 16 * views, LANES),
            scratch(32 * PADDED, LANES),
            pltpu.SemaphoreType.DMA((11,)),
            pltpu.SemaphoreType.DMA((13,)),
            pltpu.SemaphoreType.DMA((14,)),
        ],
        compiler_params=pltpu.CompilerParams(
            vmem_limit_bytes=VMEM_BYTES, collective_id=0, has_side_effects=True
        ),
        name="step",
    )(
        params,
        first_moment,
        second_moment,
        cam_centers,
        send_rows,
        move_order,
        tile_lists,
        by_channel,
        tile_counts,
        tile_ids,
    )
    return pl.pallas_call(
        write_kernel,
        out_shape=(f32(PARAMS, 4096),) * 3,
        in_specs=[ANY] * 4,
        out_specs=(HBM,) * 3,
        scratch_shapes=[
            scratch(3, PARAMS, 4096),
            scratch(16 + 16 * views, LANES),
            scratch(PADDED, LANES),
            pltpu.SemaphoreType.DMA((16,)),
            pltpu.SemaphoreType.DMA((15,)),
        ],
        compiler_params=pltpu.CompilerParams(vmem_limit_bytes=VMEM_BYTES),
        name="write",
    )(*updated)


def solution(mesh):
    placed = (
        P(None, "dev"),
        P(None, "dev"),
        P(None, "dev"),
        P("view", None),
        P("view", "dev", None, None),
        P("view", "dev", None),
        P("view", "dev", None),
        P("view", "dev"),
        P("view", "dev"),
        P("dev", None),
    )
    return jax.shard_map(
        per_device,
        mesh=mesh,
        in_specs=placed,
        out_specs=(P(None, "dev"), P(None, "dev"), P(None, "dev")),
        check_vma=False,
    )
```

```python
import functools

import jax
import jax.numpy as jnp
from jax import lax
from jax.experimental import pallas as pl
from jax.experimental.pallas import tpu as pltpu
from jax.sharding import PartitionSpec as P

PARAMS = 59
PADDED = 64
FEATS = 9
LANES = 128
TILE_SIDE = 16
TILES_X = 64
ADAM_STEP = 1000
FOCAL_LEN = 1.2
DILATION = 0.3
SH_C0 = 0.28209479177387814
SH_C1 = 0.4886025119029199
SH_C2 = (
    1.0925484305920792,
    -1.0925484305920792,
    0.31539156525252005,
    -1.0925484305920792,
    0.5462742152960396,
)
SH_C3 = (
    -0.5900435899266435,
    2.890611442640554,
    -0.4570457994644658,
    0.3731763325901154,
    -0.4570457994644658,
    1.445305721320277,
    -0.5900435899266435,
)
BETA_ONE = 0.9
BETA_TWO = 0.999
ADAM_EPS = 1e-08
MESH = pl.DeviceIdType.MESH
MOVED_EARLY = 2816
WIDTH = 1024.0
HEIGHT = 512.0


def sh_basis(x, y, z):
    xx, yy, zz = x * x, y * y, z * z
    return [
        SH_C0 + 0.0 * x,
        -SH_C1 * y,
        SH_C1 * z,
        -SH_C1 * x,
        SH_C2[0] * x * y,
        SH_C2[1] * y * z,
        SH_C2[2] * (2.0 * zz - xx - yy),
        SH_C2[3] * x * z,
        SH_C2[4] * (xx - yy),
        SH_C3[0] * y * (3.0 * xx - yy),
        SH_C3[1] * x * y * z,
        SH_C3[2] * y * (4.0 * zz - xx - yy),
        SH_C3[3] * z * (2.0 * zz - 3.0 * xx - 3.0 * yy),
        SH_C3[4] * x * (4.0 * zz - xx - yy),
        SH_C3[5] * z * (xx - yy),
        SH_C3[6] * x * (xx - 3.0 * yy),
    ]


def project(values, center):
    off = [values[i] - center[i] for i in range(3)]
    inverse = 1.0 / off[2]
    mean_u = 0.5 + FOCAL_LEN * off[0] * inverse
    mean_v = 0.5 + FOCAL_LEN * off[1] * inverse
    scale_sq = [jnp.exp(2.0 * values[3 + i]) for i in range(3)]
    quat = values[6:10]
    norm = lax.rsqrt(
        quat[0] * quat[0] + quat[1] * quat[1] + quat[2] * quat[2] + quat[3] * quat[3]
    )
    w, x, y, z = (q * norm for q in quat)
    rotation = [
        [1.0 - 2.0 * (y * y + z * z), 2.0 * (x * y - w * z), 2.0 * (x * z + w * y)],
        [2.0 * (x * y + w * z), 1.0 - 2.0 * (x * x + z * z), 2.0 * (y * z - w * x)],
        [2.0 * (x * z - w * y), 2.0 * (y * z + w * x), 1.0 - 2.0 * (x * x + y * y)],
    ]
    focal_now = FOCAL_LEN * inverse
    slope_u = -focal_now * off[0] * inverse
    slope_v = -focal_now * off[1] * inverse
    cov_uu = DILATION / (WIDTH * WIDTH)
    cov_vv = DILATION / (HEIGHT * HEIGHT)
    cov_uv = 0.0
    for c in range(3):
        axis_u = focal_now * rotation[0][c] + slope_u * rotation[2][c]
        axis_v = focal_now * rotation[1][c] + slope_v * rotation[2][c]
        cov_uu = cov_uu + axis_u * axis_u * scale_sq[c]
        cov_vv = cov_vv + axis_v * axis_v * scale_sq[c]
        cov_uv = cov_uv + axis_u * axis_v * scale_sq[c]
    inv_det = 1.0 / (cov_uu * cov_vv - cov_uv * cov_uv)
    inv_dist = 1.0 / jnp.sqrt(off[0] * off[0] + off[1] * off[1] + off[2] * off[2])
    basis = sh_basis(off[0] * inv_dist, off[1] * inv_dist, off[2] * inv_dist)
    colors = []
    for ch in range(3):
        total = basis[0] * values[11 + ch]
        for k in range(1, 16):
            total = total + basis[k] * values[11 + 3 * k + ch]
        colors.append(0.5 + total)
    opacity = 1.0 / (1.0 + jnp.exp(-values[10]))
    return [
        mean_u,
        mean_v,
        cov_vv * inv_det,
        -cov_uv * inv_det,
        cov_uu * inv_det,
        *colors,
        opacity,
    ]


def pick(array, index):
    return jnp.take_along_axis(array, index, axis=1, mode="promise_in_bounds")


def lane_ids(rows=8):
    return lax.broadcasted_iota(jnp.int32, (rows, LANES), 1)


def row_ids(rows=8):
    return lax.broadcasted_iota(jnp.int32, (rows, LANES), 0)


def fill_dense(array_ref, dense_ref):
    for j in range(32):
        dense_ref[PADDED * j : PADDED * j + PARAMS, :] = array_ref[
            :, LANES * j : LANES * (j + 1)
        ]


def dense_at(dense_ref, chunk, row):
    return dense_ref[pl.ds(chunk * 8 * PADDED + row, 8, stride=PADDED), :]


def for_others(owners, body):
    def step(i, carried):
        body(i)
        return carried

    for low, high in ((40, 88), (24, 40), (88, 104), (1, 24), (104, 128)):
        lax.fori_loop(low * owners // 128, high * owners // 128, step, 0, unroll=8)


def greet(views, owners):
    view, me = lax.axis_index("view"), lax.axis_index("dev")
    barrier = pltpu.get_barrier_semaphore()
    for i in range(1, views):
        pl.semaphore_signal(
            barrier, inc=1, device_id=(lax.rem(view + i, views), me), device_id_type=MESH
        )

    def signal(i):
        pl.semaphore_signal(
            barrier, inc=1, device_id=(view, lax.rem(me + i, owners)), device_id_type=MESH
        )

    for_others(owners, signal)
    return barrier, views + owners - 2


def send_each(owners, message, landing, send_sem, recv_sem):
    view, me = lax.axis_index("view"), lax.axis_index("dev")

    def send(i):
        other = lax.rem(me + i, owners)
        pltpu.make_async_remote_copy(
            src_ref=message(other),
            dst_ref=landing(me),
            send_sem=send_sem,
            recv_sem=recv_sem,
            device_id=(view, other),
            device_id_type=MESH,
        ).start()

    for_others(owners, send)


def send_views(views, block, landing, send_sem, recv_sem):
    view, me = lax.axis_index("view"), lax.axis_index("dev")
    for i in range(1, views):
        pltpu.make_async_remote_copy(
            src_ref=block,
            dst_ref=landing(view),
            send_sem=send_sem,
            recv_sem=recv_sem,
            device_id=(lax.rem(view + i, views), me),
            device_id_type=MESH,
        ).start()


def wait_bytes(ref, semaphore):
    pltpu.make_async_copy(ref, ref, semaphore).wait()


def slot_messages(rows, center, dense, feats, outgoing):
    for chunk in range(4):
        values = [dense_at(dense, chunk, p) for p in range(PARAMS)]
        for f, value in enumerate(project(values, center)):
            feats[f, 8 * chunk : 8 * chunk + 8, :] = value
    high = rows // LANES
    low = lax.rem(rows, LANES)
    slots = [jnp.zeros((8, LANES), jnp.float32)] * FEATS
    for h in range(32):
        chosen = high == h
        for f in range(FEATS):
            source = jnp.broadcast_to(feats[f, h : h + 1, :], (8, LANES))
            slots[f] = jnp.where(chosen, pick(source, low), slots[f])
    lane = lane_ids()
    sub = row_ids()
    for block in range(16):
        index = ((block % 2) * 8 + sub) * 8 + lax.rem(lane, 8)
        message = jnp.zeros((8, LANES), jnp.float32)
        for f in range(FEATS):
            source = jnp.broadcast_to(slots[f][block // 2 : block // 2 + 1, :], (8, LANES))
            message = jnp.where(lane // 8 == f, pick(source, index), message)
        outgoing[8 * block : 8 * block + 8, :] = message


def dot(a, b, dims=((1,), (0,))):
    return lax.dot_general(
        a,
        b,
        (dims, ((), ())),
        precision=lax.Precision.HIGHEST,
        preferred_element_type=jnp.float32,
    )


def render(
    arrived_ref,
    lists,
    counts,
    ids,
    wanted_ref,
    out_ref,
    gauss,
    trans,
    gauss_grad,
    weight,
    product,
    sums,
):
    lane = lane_ids()
    sub = row_ids()
    half_of = lane // 64
    entry = lax.rem(lane, 64)
    slot = lax.rem(lists, 64)
    from_owner = slot // 8
    within = lax.rem(slot, 8)
    feats = [jnp.zeros((8, LANES), jnp.float32)] * FEATS
    for h in range(2):
        for o in range(8):
            block = arrived_ref[pl.ds(8 * h + o, 8, stride=16), :]
            chosen = (from_owner == o) & (half_of == h)
            for f in range(FEATS):
                feats[f] = jnp.where(chosen, pick(block, 8 * f + within), feats[f])
    center_u = (lax.rem(ids, TILES_X) * TILE_SIDE + TILE_SIDE // 2).astype(jnp.float32)
    center_v = (ids // TILES_X * TILE_SIDE + TILE_SIDE // 2).astype(jnp.float32)
    mean_u = feats[0] * WIDTH - center_u
    mean_v = feats[1] * HEIGHT - center_v
    quad_a = feats[2] * (-0.5 / (WIDTH * WIDTH))
    quad_b = feats[3] * (-1.0 / (WIDTH * HEIGHT))
    quad_c = feats[4] * (-0.5 / (HEIGHT * HEIGHT))
    active = entry < counts
    opacity = jnp.where(active, feats[8], 0.0)
    pixel_u = lax.rem(lane, 16).astype(jnp.float32) - 7.5
    pixel_v = [(lane // 16 + 8 * p).astype(jnp.float32) - 7.5 for p in range(2)]
    ahead = [mean_u, mean_v, quad_a, quad_b, quad_c, *feats[5:8], opacity]

    def forward(e, carried):
        through, acc, place = carried
        through, acc = list(through), list(acc)
        for h in range(2):
            index = jnp.full((8, LANES), h * 64, jnp.int32) + e
            m_u, m_v, q_a, q_b, q_c, c_0, c_1, c_2, alpha_max = (
                pick(array, index) for array in ahead
            )
            place = jnp.where((pick(slot, index) == entry) & (half_of == h), e, place)
            diff_u = pixel_u - m_u
            part = diff_u * q_b
            square = diff_u * diff_u * q_a
            for p in range(2):
                diff_v = pixel_v[p] - m_v
                bell = jnp.exp(square + diff_v * (part + q_c * diff_v))
                alpha = alpha_max * bell
                n = 2 * h + p
                before = through[n]
                gauss[e, n] = bell
                trans[e, n] = before
                share = alpha * before
                through[n] = before - share
                for ch, color in enumerate((c_0, c_1, c_2)):
                    acc[3 * n + ch] = acc[3 * n + ch] + color * share
        return tuple(through), tuple(acc), place

    zero = jnp.zeros((8, LANES), jnp.float32)
    _, acc, place = lax.fori_loop(
        0,
        64,
        forward,
        ((zero + 1.0,) * 4, (zero,) * 12, jnp.zeros((8, LANES), jnp.int32)),
        unroll=64,
    )
    residual = []
    for h in range(2):
        for p in range(2):
            for ch in range(3):
                wanted = wanted_ref[pl.ds(16 * (2 * ch + p) + h, 8, stride=2), :]
                residual.append(acc[3 * (2 * h + p) + ch] - wanted)

    def backward(i, carried):
        e = 63 - i
        behind = list(carried)
        for h in range(2):
            index = jnp.full((8, LANES), h * 64, jnp.int32) + e
            c_0, c_1, c_2, alpha_max = (pick(array, index) for array in ahead[5:9])
            for p in range(2):
                n = 2 * h + p
                bell = gauss[e, n]
                before = trans[e, n]
                alpha = alpha_max * bell
                shade = (
                    c_0 * residual[3 * n] + c_1 * residual[3 * n + 1] + c_2 * residual[3 * n + 2]
                )
                gap = shade - behind[n]
                behind[n] = behind[n] + alpha * gap
                start = pl.multiple_of(512 * h + 8 * e, 8)
                gauss_grad[pl.ds(start, 8), LANES * p : LANES * (p + 1)] = before * gap * bell
                weight[pl.ds(start, 8), LANES * p : LANES * (p + 1)] = alpha * before
        return tuple(behind)

    lax.fori_loop(0, 64, backward, (zero,) * 4, unroll=64)

    pix = row_ids(LANES)
    col = lane_ids(LANES)
    for_moments, for_colors = [], []
    for p in range(2):
        u = lax.rem(pix, 16).astype(jnp.float32) - 7.5
        v = (pix // 16 + 8 * p).astype(jnp.float32) - 7.5
        powers = [jnp.ones_like(u), u, v, u * u, u * v, v * v]
        table = jnp.zeros_like(u)
        for m, power in enumerate(powers):
            table = jnp.where(col == m, power, table)
        for_moments.append(table)
        stacked = [zero]
        for ch in range(3):
            for h in range(2):
                stacked.append(residual[3 * (2 * h + p) + ch])
        stacked += [zero] * 9
        for_colors.append(jnp.concatenate(stacked, axis=0).T)

    for_moments = jnp.concatenate(for_moments, axis=0)
    for_colors = jnp.concatenate(for_colors, axis=0)
    for part in range(4):
        rows = slice(256 * part, 256 * (part + 1))
        product[rows, :] = dot(gauss_grad[rows, :], for_moments) + dot(
            weight[rows, :], for_colors
        )
    for k in range(8):
        sums[64 * k : 64 * k + 64, :] = product[pl.ds(k, LANES, stride=8), :].T[0:64, :]

    s_0, s_u, s_v, s_uu, s_uv, s_vv = (sums[pl.ds(m, 8, stride=64), :] for m in range(6))
    d_colors = []
    for ch in range(3):
        even = sums[pl.ds(8 + 16 * ch, 8, stride=65), :]
        odd = sums[pl.ds(16 + 16 * ch, 8, stride=65), :]
        d_colors.append(jnp.where(half_of == 0, even, odd))
    m_u = opacity * (s_u - mean_u * s_0)
    m_v = opacity * (s_v - mean_v * s_0)
    m_uu = opacity * (s_uu - mean_u * (2.0 * s_u - mean_u * s_0))
    m_vv = opacity * (s_vv - mean_v * (2.0 * s_v - mean_v * s_0))
    m_uv = opacity * (s_uv - mean_u * s_v - mean_v * (s_u - mean_u * s_0))
    grads = [
        -WIDTH * (2.0 * quad_a * m_u + quad_b * m_v),
        -HEIGHT * (2.0 * quad_c * m_v + quad_b * m_u),
        (-0.5 / (WIDTH * WIDTH)) * m_uu,
        (-1.0 / (WIDTH * HEIGHT)) * m_uv,
        (-0.5 / (HEIGHT * HEIGHT)) * m_vv,
        *d_colors,
        jnp.where(active, s_0, 0.0),
    ]
    for h in range(2):
        for o in range(8):
            base = h * 64 + o * 8 + lax.rem(lane, 8)
            index = h * 64 + pick(place, base)
            message = zero
            for f in range(FEATS):
                message = jnp.where(lane // 8 == f, pick(grads[f], index), message)
            out_ref[pl.ds(8 * h + o, 8, stride=16), :] = message


def step_sizes(rows):
    return jnp.where(
        rows < 3,
        0.00016,
        jnp.where(
            rows < 6,
            0.005,
            jnp.where(
                rows < 10,
                0.001,
                jnp.where(rows < 11, 0.05, jnp.where(rows < 14, 0.0025, 0.000125)),
            ),
        ),
    )


def slot_places(rows_all):
    place = jnp.zeros((PADDED, LANES), jnp.float32)
    sub_high = row_ids(32)
    sub_low = row_ids(LANES)
    lane_value = lane_ids(32).astype(jnp.float32)
    for i in range(32):
        rows = rows_all[i // 8][i % 8 : i % 8 + 1, :]
        hit = sub_high == jnp.broadcast_to(rows // LANES, (32, LANES))
        left = jnp.concatenate(
            [jnp.where(hit, float(i), 0.0), jnp.where(hit, lane_value, 0.0)], axis=0
        )
        right = jnp.where(
            sub_low == jnp.broadcast_to(lax.rem(rows, LANES), (LANES, LANES)), 1.0, 0.0
        )
        place = place + lax.dot_general(
            left.astype(jnp.bfloat16),
            right.astype(jnp.bfloat16),
            (((1,), (1,)), ((), ())),
            preferred_element_type=jnp.float32,
        )
    return (place[0:32] + 0.5).astype(jnp.int32), (place[32:64] + 0.5).astype(jnp.int32)


def adam(values, first, second, gradient):
    bias_one = 1.0 - BETA_ONE**ADAM_STEP
    bias_two = 1.0 - BETA_TWO**ADAM_STEP
    sizes = step_sizes(row_ids(PADDED)[0:PARAMS])
    new_one = BETA_ONE * first + (1.0 - BETA_ONE) * gradient
    new_two = BETA_TWO * second + (1.0 - BETA_TWO) * gradient * gradient
    updated = values - sizes * (new_one / bias_one) / (jnp.sqrt(new_two / bias_two) + ADAM_EPS)
    return updated, new_one, new_two


def per_tile(ref):
    values = ref[...]
    row, half_of = row_ids(), lane_ids() // 64
    spread = jnp.zeros((8, LANES), jnp.int32)
    for k in range(16):
        one = jnp.broadcast_to(values[:, k : k + 1], (8, LANES))
        spread = jnp.where((row == k // 2) & (half_of == k % 2), one, spread)
    return spread


def step_kernel(
    views,
    owners,
    params_hbm,
    first_hbm,
    second_hbm,
    center_hbm,
    rows_hbm,
    order_hbm,
    lists_hbm,
    target_hbm,
    counts_hbm,
    ids_hbm,
    new_params_hbm,
    new_first_hbm,
    new_second_hbm,
    last_hbm,
    new_params_ref,
    new_first_ref,
    new_second_ref,
    params_ref,
    first_ref,
    second_ref,
    center_ref,
    rows_ref,
    order_ref,
    order_lanes_ref,
    lists_ref,
    target_ref,
    counts_ref,
    ids_ref,
    dense,
    feats,
    outgoing,
    landed,
    packed,
    packed_landed,
    before_a,
    before_b,
    moved_a,
    moved_b,
    leaving,
    arriving,
    order_rows,
    list_rows,
    wanted,
    gauss,
    trans,
    gauss_grad,
    weight,
    product,
    sums,
    slot_grads,
    returned,
    by_slot,
    leaving_grads,
    arriving_grads,
    arrived_views,
    last,
    taken,
    lanes_taken,
    marked,
    grads,
    load_sems,
    store_sems,
    sems,
):
    view, me = lax.axis_index("view"), lax.axis_index("dev")
    barrier, expected = greet(views, owners)
    copies = (
        (center_hbm, center_ref),
        (rows_hbm, rows_ref),
        (params_hbm, params_ref),
        (first_hbm, first_ref),
        (second_hbm, second_ref),
        (order_hbm, order_ref),
        (order_hbm, order_lanes_ref),
        (lists_hbm, lists_ref),
        (target_hbm, target_ref),
        (counts_hbm, counts_ref),
        (ids_hbm, ids_ref),
    )
    loads = [
        pltpu.make_async_copy(source, place, load_sems.at[i])
        for i, (source, place) in enumerate(copies)
    ]
    for load in loads:
        load.start()
    lane = lane_ids()
    others = pl.ds(0, owners - 1)
    other_views = pl.ds(0, views - 1)
    kept = order_ref.shape[1] - owners
    zero = jnp.zeros((8, LANES), jnp.float32)

    for load in loads[0:3]:
        load.wait()
    center = [jnp.broadcast_to(center_ref[:, i : i + 1], (8, LANES)) for i in range(3)]
    for i in range(8):
        packed[i : i + 1, :] = rows_ref[0, :, LANES * i : LANES * (i + 1)].astype(jnp.float32)
    here = zero
    for i in range(3):
        here = jnp.where(lane == i, center[i], here)
    packed[8:16, :] = here
    fill_dense(params_ref, dense)
    slot_messages(
        packed[0:8, :].astype(jnp.int32),
        center,
        dense,
        feats,
        outgoing,
    )

    fill = jnp.zeros((PADDED - PARAMS, LANES), jnp.float32)
    empty = jnp.zeros((PADDED, LANES), jnp.float32)
    loads[3].wait()
    loads[4].wait()

    def to_rows(j, carried):
        columns = pl.ds(pl.multiple_of(j * LANES, LANES), LANES)
        before_a[columns, :] = jnp.concatenate(
            [params_ref[:, columns], fill, first_ref[:, columns], fill], axis=0
        ).T
        before_b[columns, :] = jnp.concatenate([second_ref[:, columns], fill, empty], axis=0).T
        return carried

    lax.fori_loop(0, 32, to_rows, 0, unroll=8)

    for load in loads[5:]:
        load.wait()
    for t in range(owners):
        row = order_ref[0, kept + t]
        leaving[0, t : t + 1, :] = before_a[pl.ds(row, 1), :]
        leaving[1, t : t + 1, :] = before_b[pl.ds(row, 1), :]

    pl.semaphore_wait(barrier, expected)
    send_each(
        owners,
        lambda d: outgoing.at[pl.ds(d, 1)],
        lambda d: landed.at[pl.ds(d, 1)],
        sems.at[0],
        sems.at[1],
    )
    send_views(views, packed, lambda v: packed_landed.at[v], sems.at[2], sems.at[3])
    landed[pl.ds(me, 1), :] = outgoing[pl.ds(me, 1), :]
    packed_landed[view] = packed[...]

    send_each(
        owners,
        lambda d: leaving.at[:, pl.ds(d, 1)],
        lambda d: arriving.at[:, pl.ds(d, 1)],
        sems.at[4],
        sems.at[5],
    )
    arriving[:, pl.ds(me, 1), :] = leaving[:, pl.ds(me, 1), :]

    def move(t, carried):
        for u in range(32):
            row = order_ref[0, t * 32 + u]
            moved_a[pl.ds(t * 32 + u, 1), :] = before_a[pl.ds(row, 1), :]
            moved_b[pl.ds(t * 32 + u, 1), :] = before_b[pl.ds(row, 1), :]
        return carried

    lax.fori_loop(0, MOVED_EARLY // 32, move, 0)
    for k in range(16):
        list_rows[k : k + 1, 0:64] = lists_ref[0, k : k + 1, :]
    for ch in range(3):
        for p in range(2):
            n = 16 * (2 * ch + p)
            wanted[n : n + 16, :] = target_ref[ch, :, LANES * p : LANES * (p + 1)]
    even = list_rows[pl.ds(0, 8, stride=2), :]
    odd = list_rows[pl.ds(1, 8, stride=2), :]
    lists = jnp.where(lane < 64, even, pick(odd, lax.rem(lane, 64)))

    wait_bytes(landed.at[others], sems.at[1])
    render(
        landed,
        lists,
        per_tile(counts_ref),
        per_tile(ids_ref),
        wanted,
        slot_grads,
        gauss,
        trans,
        gauss_grad,
        weight,
        product,
        sums,
    )
    send_each(
        owners,
        lambda d: slot_grads.at[pl.ds(d, 1)],
        lambda d: returned.at[pl.ds(d, 1)],
        sems.at[6],
        sems.at[7],
    )
    returned[pl.ds(me, 1), :] = slot_grads[pl.ds(me, 1), :]

    lax.fori_loop(MOVED_EARLY // 32, kept // 32, move, 0)
    wait_bytes(arriving.at[:, others], sems.at[5])
    moved_a[kept:, :] = arriving[0]
    moved_b[kept:, :] = arriving[1]

    def to_columns(j, carried):
        columns = pl.ds(pl.multiple_of(j * LANES, LANES), LANES)
        both = moved_a[columns, :].T
        new_params_ref[:, columns] = both[0:PARAMS, :]
        new_first_ref[:, columns] = both[PADDED : PADDED + PARAMS, :]
        new_second_ref[:, columns] = moved_b[columns, :].T[0:PARAMS, :]
        dense[pl.ds(pl.multiple_of(j * PADDED, PADDED), PADDED), :] = both[0:PADDED, :]
        return carried

    lax.fori_loop(0, 32, to_columns, 0, unroll=8)
    for j in range(32):
        order_rows[j : j + 1, :] = order_lanes_ref[:, LANES * j : LANES * (j + 1)]
    wait_bytes(packed_landed.at[other_views], sems.at[3])
    place_high, place_low = slot_places(
        [packed_landed[v, 0:8, :].astype(jnp.int32) for v in range(views)]
    )
    place = place_high * LANES + place_low
    slot_high, slot_low = [], []
    for chunk in range(4):
        order = order_rows[8 * chunk : 8 * chunk + 8, :]
        high, low = order // LANES, lax.rem(order, LANES)
        found = jnp.zeros((8, LANES), jnp.int32)
        for h in range(32):
            source = jnp.broadcast_to(place[h : h + 1, :], (8, LANES))
            found = jnp.where(high == h, pick(source, low), found)
        slot_high.append(found // LANES)
        slot_low.append(lax.rem(found, LANES))
    centers = [
        [
            jnp.broadcast_to(packed_landed[v, 8:9, i : i + 1], (8, LANES))
            for v in range(views)
        ]
        for i in range(3)
    ]

    slots = (slot_high[3] * LANES + slot_low[3])[7:8, :].astype(jnp.float32)
    slots = (jnp.broadcast_to(slots, (LANES, LANES)).T + 0.5).astype(jnp.int32)
    column = lane_ids(LANES)
    here = slots // 1024 == view
    taken[...] = jnp.where((lax.rem(slots, 1024) // 8 == column) & here, 1.0, 0.0)
    lanes_taken[...] = jnp.where(column < FEATS, column * 8 + lax.rem(slots, 8), 0)
    marked[...] = jnp.where((column == FEATS) & here, (view + 1).astype(jnp.float32), 0.0)

    wait_bytes(returned.at[others], sems.at[7])
    found = dot(taken[...], returned[...])
    for i in range(16):
        rows = slice(8 * i, 8 * i + 8)
        leaving_grads[rows, :] = jnp.where(
            lane < FEATS, pick(found[rows, :], lanes_taken[rows, :]), marked[rows, :]
        )
    send_each(
        owners,
        lambda d: leaving_grads.at[pl.ds(d, 1)],
        lambda d: arriving_grads.at[pl.ds(d, 1)],
        sems.at[10],
        sems.at[11],
    )
    arriving_grads[pl.ds(me, 1), :] = leaving_grads[pl.ds(me, 1), :]

    values = [zero] * FEATS
    for o in range(16):
        block = returned[pl.ds(o, 8, stride=16), :]
        chosen = lane // 8 == o
        for f in range(FEATS):
            values[f] = jnp.where(chosen, pick(block, 8 * f + lax.rem(lane, 8)), values[f])
    for f in range(FEATS):
        by_slot[view, 8 * f : 8 * f + 8, :] = values[f]
    send_views(views, by_slot.at[view], lambda v: by_slot.at[v], sems.at[8], sems.at[9])
    wait_bytes(by_slot.at[other_views], sems.at[9])

    def collect(chunk):
        found = [zero] * FEATS
        for h in range(32):
            chosen = slot_high[chunk] == h
            for f in range(FEATS):
                row = 8 * f + h % 8
                source = jnp.broadcast_to(by_slot[h // 8, row : row + 1, :], (8, LANES))
                found[f] = jnp.where(chosen, pick(source, slot_low[chunk]), found[f])
        return found

    stores = []

    def finish(chunk, feat_grads, count):
        view_of = slot_high[chunk] // 8
        center = []
        for i in range(3):
            at = zero
            for v in range(views):
                at = jnp.where(view_of == v, centers[i][v], at)
            center.append(at)
        arguments = [dense_at(dense, chunk, p) for p in range(PARAMS)]
        _, pull_back = jax.vjp(lambda *args: project(args, center), *arguments)
        for p, grad in enumerate(pull_back(list(feat_grads))):
            grads[pl.ds(chunk * 8 * PADDED + p, 8, stride=PADDED), :] = grad
        for j in range(8 * chunk, 8 * chunk + count):
            columns = slice(LANES * j, LANES * (j + 1))
            gradient = grads[PADDED * j : PADDED * j + PARAMS, :]
            (
                new_params_ref[:, columns],
                new_first_ref[:, columns],
                new_second_ref[:, columns],
            ) = adam(
                new_params_ref[:, columns],
                new_first_ref[:, columns],
                new_second_ref[:, columns],
                gradient,
            )
        columns = pl.ds(8 * LANES * chunk, 8 * LANES)
        for i, (source, place) in enumerate(
            (
                (new_params_ref, new_params_hbm),
                (new_first_ref, new_first_hbm),
                (new_second_ref, new_second_hbm),
            )
        ):
            copy = pltpu.make_async_copy(
                source.at[:, columns], place.at[:, columns], store_sems.at[len(stores)]
            )
            copy.start()
            stores.append(copy)

    for chunk in range(2):
        finish(chunk, collect(chunk), 8)
    for v in range(views):
        last[16 + 16 * v : 32 + 16 * v, :] = packed_landed[v]
    wait_bytes(arriving_grads.at[others], sems.at[11])
    arrived_views[view] = arriving_grads[...].T[0:16, :]
    send_views(
        views, arrived_views.at[view], lambda v: arrived_views.at[v], sems.at[12], sems.at[13]
    )
    for chunk in (2, 3):
        finish(chunk, collect(chunk), 8 if chunk < 3 else 7)
    wait_bytes(arrived_views.at[other_views], sems.at[13])
    arrived = arrived_views[0]
    for v in range(1, views):
        arrived = arrived + arrived_views[v]
    last[0:16, :] = arrived
    copy = pltpu.make_async_copy(last, last_hbm, store_sems.at[len(stores)])
    copy.start()
    stores.append(copy)
    wait_bytes(landed.at[others], sems.at[0])
    wait_bytes(packed_landed.at[other_views], sems.at[2])
    wait_bytes(arriving.at[:, others], sems.at[4])
    wait_bytes(returned.at[others], sems.at[6])
    wait_bytes(by_slot.at[other_views], sems.at[8])
    wait_bytes(arriving_grads.at[others], sems.at[10])
    wait_bytes(arrived_views.at[other_views], sems.at[12])
    for copy in stores:
        copy.wait()


def write_kernel(
    params,
    first,
    second,
    last_hbm,
    new_params,
    new_first,
    new_second,
    held,
    last,
    grads,
    load_sems,
    store_sems,
):
    ends = ((params, new_params), (first, new_first), (second, new_second))
    parts = [pl.ds(3968, 128)] + [pl.ds(1024 * k, 1024) for k in range(3)] + [pl.ds(3072, 896)]
    loads, stores = [pltpu.make_async_copy(last_hbm, last, load_sems.at[0])], []
    for columns in parts:
        for i, (source, place) in enumerate(ends):
            middle = held.at[i, :, columns]
            loads.append(
                pltpu.make_async_copy(source.at[:, columns], middle, load_sems.at[len(loads)])
            )
            stores.append(
                pltpu.make_async_copy(middle, place.at[:, columns], store_sems.at[len(stores)])
            )
    for load in loads:
        load.start()
    for load in loads[0:4]:
        load.wait()
    columns = slice(3968, 4096)
    view_of = (last[FEATS : FEATS + 1, :] + 0.5).astype(jnp.int32) - 1
    center = []
    for i in range(3):
        at = jnp.zeros((1, LANES), jnp.float32)
        for v in range(last.shape[0] // 16 - 1):
            row = 16 * v + 24
            one = jnp.broadcast_to(last[row : row + 1, i : i + 1], (1, LANES))
            at = jnp.where(view_of == v, one, at)
        center.append(at)
    arguments = [held[0, p : p + 1, columns] for p in range(PARAMS)]
    _, pull_back = jax.vjp(lambda *args: project(args, center), *arguments)
    for p, grad in enumerate(pull_back([last[f : f + 1, :] for f in range(FEATS)])):
        grads[p : p + 1, :] = grad
    held[0, :, columns], held[1, :, columns], held[2, :, columns] = adam(
        held[0, :, columns], held[1, :, columns], held[2, :, columns], grads[0:PARAMS, :]
    )
    for store in stores[0:3]:
        store.start()
    for load, store in zip(loads[4:], stores[3:]):
        load.wait()
        store.start()
    for store in stores:
        store.wait()


VMEM = pl.BlockSpec(memory_space=pltpu.VMEM)
SMEM = pl.BlockSpec(memory_space=pltpu.SMEM)
ANY = pl.BlockSpec(memory_space=pl.ANY)
HBM = pl.BlockSpec(memory_space=pltpu.HBM)
VMEM_BYTES = 60 * 1024 * 1024


def f32(*shape):
    return jax.ShapeDtypeStruct(shape, jnp.float32)


def scratch(*shape):
    return pltpu.VMEM(shape, jnp.float32)


def per_device(
    params,
    first_moment,
    second_moment,
    cam_centers,
    target,
    send_rows,
    tile_lists,
    tile_counts,
    tile_ids,
    move_order,
):
    views, owners = lax.axis_size("view"), lax.axis_size("dev")
    by_channel = target[0].transpose(1, 0, 2)
    updated = pl.pallas_call(
        functools.partial(step_kernel, views, owners),
        out_shape=(f32(PARAMS, 4096),) * 3 + (f32(16 + 16 * views, LANES),),
        in_specs=[HBM] * 10,
        out_specs=(ANY,) * 4,
        scratch_shapes=[
            scratch(PARAMS, 4096),
            scratch(PARAMS, 4096),
            scratch(PARAMS, 4096),
            scratch(PARAMS, 4096),
            scratch(PARAMS, 4096),
            scratch(PARAMS, 4096),
            scratch(*cam_centers.shape),
            pltpu.VMEM(send_rows.shape, jnp.int32),
            pltpu.SMEM(move_order.shape, jnp.int32),
            pltpu.VMEM(move_order.shape, jnp.int32),
            pltpu.VMEM(tile_lists.shape, jnp.int32),
            scratch(*by_channel.shape),
            pltpu.VMEM(tile_counts.shape, jnp.int32),
            pltpu.VMEM(tile_ids.shape, jnp.int32),
            scratch(32 * PADDED, LANES),
            scratch(FEATS, 32, LANES),
            scratch(owners, LANES),
            scratch(owners, LANES),
            scratch(16, LANES),
            scratch(views, 16, LANES),
            scratch(4096, LANES),
            scratch(4096, LANES),
            scratch(4096, LANES),
            scratch(4096, LANES),
            scratch(2, owners, LANES),
            scratch(2, owners, LANES),
            pltpu.VMEM((32, LANES), jnp.int32),
            pltpu.VMEM((16, LANES), jnp.int32),
            scratch(96, LANES),
            scratch(64, 4, 8, LANES),
            scratch(64, 4, 8, LANES),
            scratch(1024, 2 * LANES),
            scratch(1024, 2 * LANES),
            scratch(1024, LANES),
            scratch(512, LANES),
            scratch(owners, LANES),
            scratch(owners, LANES),
            scratch(views, 8 * FEATS, LANES),
            scratch(owners, LANES),
            scratch(owners, LANES),
            scratch(views, 16, LANES),
            scratch(16 + 16 * views, LANES),
            scratch(owners, LANES),
            pltpu.VMEM((owners, LANES), jnp.int32),
            scratch(owners, LANES),
            scratch(32 * PADDED, LANES),
            pltpu.SemaphoreType.DMA((11,)),
            pltpu.SemaphoreType.DMA((13,)),
            pltpu.SemaphoreType.DMA((14,)),
        ],
        compiler_params=pltpu.CompilerParams(
            vmem_limit_bytes=VMEM_BYTES, collective_id=0, has_side_effects=True
        ),
        name="step",
    )(
        params,
        first_moment,
        second_moment,
        cam_centers,
        send_rows,
        move_order,
        tile_lists,
        by_channel,
        tile_counts,
        tile_ids,
    )
    return pl.pallas_call(
        write_kernel,
        out_shape=(f32(PARAMS, 4096),) * 3,
        in_specs=[ANY] * 4,
        out_specs=(HBM,) * 3,
        scratch_shapes=[
            scratch(3, PARAMS, 4096),
            scratch(16 + 16 * views, LANES),
            scratch(PADDED, LANES),
            pltpu.SemaphoreType.DMA((16,)),
            pltpu.SemaphoreType.DMA((15,)),
        ],
        compiler_params=pltpu.CompilerParams(vmem_limit_bytes=VMEM_BYTES),
        name="write",
    )(*updated)


def solution(mesh):
    placed = (
        P(None, "dev"),
        P(None, "dev"),
        P(None, "dev"),
        P("view", None),
        P("view", "dev", None, None),
        P("view", "dev", None),
        P("view", "dev", None),
        P("view", "dev"),
        P("view", "dev"),
        P("dev", None),
    )
    return jax.shard_map(
        per_device,
        mesh=mesh,
        in_specs=placed,
        out_specs=(P(None, "dev"), P(None, "dev"), P(None, "dev")),
        check_vma=False,
    )
```

```python
import functools

import jax
import jax.numpy as jnp
from jax import lax
from jax.experimental import pallas as pl
from jax.experimental.pallas import tpu as pltpu
from jax.sharding import PartitionSpec as P

PARAMS = 59
PADDED = 64
FEATS = 9
LANES = 128
TILE_SIDE = 16
TILES_X = 64
ADAM_STEP = 1000
FOCAL_LEN = 1.2
DILATION = 0.3
SH_C0 = 0.28209479177387814
SH_C1 = 0.4886025119029199
SH_C2 = (
    1.0925484305920792,
    -1.0925484305920792,
    0.31539156525252005,
    -1.0925484305920792,
    0.5462742152960396,
)
SH_C3 = (
    -0.5900435899266435,
    2.890611442640554,
    -0.4570457994644658,
    0.3731763325901154,
    -0.4570457994644658,
    1.445305721320277,
    -0.5900435899266435,
)
BETA_ONE = 0.9
BETA_TWO = 0.999
ADAM_EPS = 1e-08
MESH = pl.DeviceIdType.MESH
MOVED_EARLY = 2816
WIDTH = 1024.0
HEIGHT = 512.0


def sh_basis(x, y, z):
    xx, yy, zz = x * x, y * y, z * z
    return [
        SH_C0 + 0.0 * x,
        -SH_C1 * y,
        SH_C1 * z,
        -SH_C1 * x,
        SH_C2[0] * x * y,
        SH_C2[1] * y * z,
        SH_C2[2] * (2.0 * zz - xx - yy),
        SH_C2[3] * x * z,
        SH_C2[4] * (xx - yy),
        SH_C3[0] * y * (3.0 * xx - yy),
        SH_C3[1] * x * y * z,
        SH_C3[2] * y * (4.0 * zz - xx - yy),
        SH_C3[3] * z * (2.0 * zz - 3.0 * xx - 3.0 * yy),
        SH_C3[4] * x * (4.0 * zz - xx - yy),
        SH_C3[5] * z * (xx - yy),
        SH_C3[6] * x * (xx - 3.0 * yy),
    ]


def project(values, center):
    off = [values[i] - center[i] for i in range(3)]
    inverse = 1.0 / off[2]
    mean_u = 0.5 + FOCAL_LEN * off[0] * inverse
    mean_v = 0.5 + FOCAL_LEN * off[1] * inverse
    scale_sq = [jnp.exp(2.0 * values[3 + i]) for i in range(3)]
    quat = values[6:10]
    norm = lax.rsqrt(
        quat[0] * quat[0] + quat[1] * quat[1] + quat[2] * quat[2] + quat[3] * quat[3]
    )
    w, x, y, z = (q * norm for q in quat)
    rotation = [
        [1.0 - 2.0 * (y * y + z * z), 2.0 * (x * y - w * z), 2.0 * (x * z + w * y)],
        [2.0 * (x * y + w * z), 1.0 - 2.0 * (x * x + z * z), 2.0 * (y * z - w * x)],
        [2.0 * (x * z - w * y), 2.0 * (y * z + w * x), 1.0 - 2.0 * (x * x + y * y)],
    ]
    focal_now = FOCAL_LEN * inverse
    slope_u = -focal_now * off[0] * inverse
    slope_v = -focal_now * off[1] * inverse
    cov_uu = DILATION / (WIDTH * WIDTH)
    cov_vv = DILATION / (HEIGHT * HEIGHT)
    cov_uv = 0.0
    for c in range(3):
        axis_u = focal_now * rotation[0][c] + slope_u * rotation[2][c]
        axis_v = focal_now * rotation[1][c] + slope_v * rotation[2][c]
        cov_uu = cov_uu + axis_u * axis_u * scale_sq[c]
        cov_vv = cov_vv + axis_v * axis_v * scale_sq[c]
        cov_uv = cov_uv + axis_u * axis_v * scale_sq[c]
    inv_det = 1.0 / (cov_uu * cov_vv - cov_uv * cov_uv)
    inv_dist = 1.0 / jnp.sqrt(off[0] * off[0] + off[1] * off[1] + off[2] * off[2])
    basis = sh_basis(off[0] * inv_dist, off[1] * inv_dist, off[2] * inv_dist)
    colors = []
    for ch in range(3):
        total = basis[0] * values[11 + ch]
        for k in range(1, 16):
            total = total + basis[k] * values[11 + 3 * k + ch]
        colors.append(0.5 + total)
    opacity = 1.0 / (1.0 + jnp.exp(-values[10]))
    return [
        mean_u,
        mean_v,
        cov_vv * inv_det,
        -cov_uv * inv_det,
        cov_uu * inv_det,
        *colors,
        opacity,
    ]


def pick(array, index):
    return jnp.take_along_axis(array, index, axis=1, mode="promise_in_bounds")


def lane_ids(rows=8):
    return lax.broadcasted_iota(jnp.int32, (rows, LANES), 1)


def row_ids(rows=8):
    return lax.broadcasted_iota(jnp.int32, (rows, LANES), 0)


def fill_dense(array_ref, dense_ref):
    for j in range(32):
        dense_ref[PADDED * j : PADDED * j + PARAMS, :] = array_ref[
            :, LANES * j : LANES * (j + 1)
        ]


def dense_at(dense_ref, chunk, row):
    return dense_ref[pl.ds(chunk * 8 * PADDED + row, 8, stride=PADDED), :]


def for_others(owners, body):
    def step(i, carried):
        body(i)
        return carried

    for low, high in ((40, 88), (24, 40), (88, 104), (1, 24), (104, 128)):
        lax.fori_loop(low * owners // 128, high * owners // 128, step, 0, unroll=8)


def greet(views, owners):
    view, me = lax.axis_index("view"), lax.axis_index("dev")
    barrier = pltpu.get_barrier_semaphore()
    for i in range(1, views):
        pl.semaphore_signal(
            barrier, inc=1, device_id=(lax.rem(view + i, views), me), device_id_type=MESH
        )

    def signal(i):
        pl.semaphore_signal(
            barrier, inc=1, device_id=(view, lax.rem(me + i, owners)), device_id_type=MESH
        )

    for_others(owners, signal)
    return barrier, views + owners - 2


def send_each(owners, message, landing, send_sem, recv_sem):
    view, me = lax.axis_index("view"), lax.axis_index("dev")

    def send(i):
        other = lax.rem(me + i, owners)
        pltpu.make_async_remote_copy(
            src_ref=message(other),
            dst_ref=landing(me),
            send_sem=send_sem,
            recv_sem=recv_sem,
            device_id=(view, other),
            device_id_type=MESH,
        ).start()

    for_others(owners, send)


def send_views(views, block, landing, send_sem, recv_sem):
    view, me = lax.axis_index("view"), lax.axis_index("dev")
    for i in range(1, views):
        pltpu.make_async_remote_copy(
            src_ref=block,
            dst_ref=landing(view),
            send_sem=send_sem,
            recv_sem=recv_sem,
            device_id=(lax.rem(view + i, views), me),
            device_id_type=MESH,
        ).start()


def wait_bytes(ref, semaphore):
    pltpu.make_async_copy(ref, ref, semaphore).wait()


def slot_messages(rows, center, dense, feats, outgoing):
    for chunk in range(4):
        values = [dense_at(dense, chunk, p) for p in range(PARAMS)]
        for f, value in enumerate(project(values, center)):
            feats[f, 8 * chunk : 8 * chunk + 8, :] = value
    high = rows // LANES
    low = lax.rem(rows, LANES)
    slots = [jnp.zeros((8, LANES), jnp.float32)] * FEATS
    for h in range(32):
        chosen = high == h
        for f in range(FEATS):
            source = jnp.broadcast_to(feats[f, h : h + 1, :], (8, LANES))
            slots[f] = jnp.where(chosen, pick(source, low), slots[f])
    lane = lane_ids()
    sub = row_ids()
    for block in range(16):
        index = ((block % 2) * 8 + sub) * 8 + lax.rem(lane, 8)
        message = jnp.zeros((8, LANES), jnp.float32)
        for f in range(FEATS):
            source = jnp.broadcast_to(slots[f][block // 2 : block // 2 + 1, :], (8, LANES))
            message = jnp.where(lane // 8 == f, pick(source, index), message)
        outgoing[8 * block : 8 * block + 8, :] = message


def dot(a, b, dims=((1,), (0,))):
    return lax.dot_general(
        a,
        b,
        (dims, ((), ())),
        precision=lax.Precision.HIGHEST,
        preferred_element_type=jnp.float32,
    )


def render(
    arrived_ref,
    lists,
    counts,
    ids,
    wanted_ref,
    out_ref,
    gauss,
    trans,
    gauss_grad,
    weight,
    product,
    sums,
):
    lane = lane_ids()
    sub = row_ids()
    half_of = lane // 64
    entry = lax.rem(lane, 64)
    slot = lax.rem(lists, 64)
    from_owner = slot // 8
    within = lax.rem(slot, 8)
    feats = [jnp.zeros((8, LANES), jnp.float32)] * FEATS
    for h in range(2):
        for o in range(8):
            block = arrived_ref[pl.ds(8 * h + o, 8, stride=16), :]
            chosen = (from_owner == o) & (half_of == h)
            for f in range(FEATS):
                feats[f] = jnp.where(chosen, pick(block, 8 * f + within), feats[f])
    center_u = (lax.rem(ids, TILES_X) * TILE_SIDE + TILE_SIDE // 2).astype(jnp.float32)
    center_v = (ids // TILES_X * TILE_SIDE + TILE_SIDE // 2).astype(jnp.float32)
    mean_u = feats[0] * WIDTH - center_u
    mean_v = feats[1] * HEIGHT - center_v
    quad_a = feats[2] * (-0.5 / (WIDTH * WIDTH))
    quad_b = feats[3] * (-1.0 / (WIDTH * HEIGHT))
    quad_c = feats[4] * (-0.5 / (HEIGHT * HEIGHT))
    active = entry < counts
    opacity = jnp.where(active, feats[8], 0.0)
    pixel_u = lax.rem(lane, 16).astype(jnp.float32) - 7.5
    pixel_v = [(lane // 16 + 8 * p).astype(jnp.float32) - 7.5 for p in range(2)]
    ahead = [mean_u, mean_v, quad_a, quad_b, quad_c, *feats[5:8], opacity]

    def forward(e, carried):
        through, acc, place = carried
        through, acc = list(through), list(acc)
        for h in range(2):
            index = jnp.full((8, LANES), h * 64, jnp.int32) + e
            m_u, m_v, q_a, q_b, q_c, c_0, c_1, c_2, alpha_max = (
                pick(array, index) for array in ahead
            )
            place = jnp.where((pick(slot, index) == entry) & (half_of == h), e, place)
            diff_u = pixel_u - m_u
            part = diff_u * q_b
            square = diff_u * diff_u * q_a
            for p in range(2):
                diff_v = pixel_v[p] - m_v
                bell = jnp.exp(square + diff_v * (part + q_c * diff_v))
                alpha = alpha_max * bell
                n = 2 * h + p
                before = through[n]
                gauss[e, n] = bell
                trans[e, n] = before
                share = alpha * before
                through[n] = before - share
                for ch, color in enumerate((c_0, c_1, c_2)):
                    acc[3 * n + ch] = acc[3 * n + ch] + color * share
        return tuple(through), tuple(acc), place

    zero = jnp.zeros((8, LANES), jnp.float32)
    _, acc, place = lax.fori_loop(
        0,
        64,
        forward,
        ((zero + 1.0,) * 4, (zero,) * 12, jnp.zeros((8, LANES), jnp.int32)),
        unroll=64,
    )
    residual = []
    for h in range(2):
        for p in range(2):
            for ch in range(3):
                wanted = wanted_ref[pl.ds(16 * (2 * ch + p) + h, 8, stride=2), :]
                residual.append(acc[3 * (2 * h + p) + ch] - wanted)

    def backward(i, carried):
        e = 63 - i
        behind = list(carried)
        for h in range(2):
            index = jnp.full((8, LANES), h * 64, jnp.int32) + e
            c_0, c_1, c_2, alpha_max = (pick(array, index) for array in ahead[5:9])
            for p in range(2):
                n = 2 * h + p
                bell = gauss[e, n]
                before = trans[e, n]
                alpha = alpha_max * bell
                shade = (
                    c_0 * residual[3 * n] + c_1 * residual[3 * n + 1] + c_2 * residual[3 * n + 2]
                )
                gap = shade - behind[n]
                behind[n] = behind[n] + alpha * gap
                start = pl.multiple_of(512 * h + 8 * e, 8)
                gauss_grad[pl.ds(start, 8), LANES * p : LANES * (p + 1)] = before * gap * bell
                weight[pl.ds(start, 8), LANES * p : LANES * (p + 1)] = alpha * before
        return tuple(behind)

    lax.fori_loop(0, 64, backward, (zero,) * 4, unroll=64)

    pix = row_ids(LANES)
    col = lane_ids(LANES)
    for_moments, for_colors = [], []
    for p in range(2):
        u = lax.rem(pix, 16).astype(jnp.float32) - 7.5
        v = (pix // 16 + 8 * p).astype(jnp.float32) - 7.5
        powers = [jnp.ones_like(u), u, v, u * u, u * v, v * v]
        table = jnp.zeros_like(u)
        for m, power in enumerate(powers):
            table = jnp.where(col == m, power, table)
        for_moments.append(table)
        stacked = [zero]
        for ch in range(3):
            for h in range(2):
                stacked.append(residual[3 * (2 * h + p) + ch])
        stacked += [zero] * 9
        for_colors.append(jnp.concatenate(stacked, axis=0).T)

    for_moments = jnp.concatenate(for_moments, axis=0)
    for_colors = jnp.concatenate(for_colors, axis=0)
    for part in range(4):
        rows = slice(256 * part, 256 * (part + 1))
        product[rows, :] = dot(gauss_grad[rows, :], for_moments) + dot(
            weight[rows, :], for_colors
        )
    for k in range(8):
        sums[64 * k : 64 * k + 64, :] = product[pl.ds(k, LANES, stride=8), :].T[0:64, :]

    s_0, s_u, s_v, s_uu, s_uv, s_vv = (sums[pl.ds(m, 8, stride=64), :] for m in range(6))
    d_colors = []
    for ch in range(3):
        even = sums[pl.ds(8 + 16 * ch, 8, stride=65), :]
        odd = sums[pl.ds(16 + 16 * ch, 8, stride=65), :]
        d_colors.append(jnp.where(half_of == 0, even, odd))
    m_u = opacity * (s_u - mean_u * s_0)
    m_v = opacity * (s_v - mean_v * s_0)
    m_uu = opacity * (s_uu - mean_u * (2.0 * s_u - mean_u * s_0))
    m_vv = opacity * (s_vv - mean_v * (2.0 * s_v - mean_v * s_0))
    m_uv = opacity * (s_uv - mean_u * s_v - mean_v * (s_u - mean_u * s_0))
    grads = [
        -WIDTH * (2.0 * quad_a * m_u + quad_b * m_v),
        -HEIGHT * (2.0 * quad_c * m_v + quad_b * m_u),
        (-0.5 / (WIDTH * WIDTH)) * m_uu,
        (-1.0 / (WIDTH * HEIGHT)) * m_uv,
        (-0.5 / (HEIGHT * HEIGHT)) * m_vv,
        *d_colors,
        jnp.where(active, s_0, 0.0),
    ]
    for h in range(2):
        for o in range(8):
            base = h * 64 + o * 8 + lax.rem(lane, 8)
            index = h * 64 + pick(place, base)
            message = zero
            for f in range(FEATS):
                message = jnp.where(lane // 8 == f, pick(grads[f], index), message)
            out_ref[pl.ds(8 * h + o, 8, stride=16), :] = message


def step_sizes(rows):
    return jnp.where(
        rows < 3,
        0.00016,
        jnp.where(
            rows < 6,
            0.005,
            jnp.where(
                rows < 10,
                0.001,
                jnp.where(rows < 11, 0.05, jnp.where(rows < 14, 0.0025, 0.000125)),
            ),
        ),
    )


def slot_places(rows_all):
    place = jnp.zeros((PADDED, LANES), jnp.float32)
    sub_high = row_ids(32)
    sub_low = row_ids(LANES)
    lane_value = lane_ids(32).astype(jnp.float32)
    for i in range(32):
        rows = rows_all[i // 8][i % 8 : i % 8 + 1, :]
        hit = sub_high == jnp.broadcast_to(rows // LANES, (32, LANES))
        left = jnp.concatenate(
            [jnp.where(hit, float(i), 0.0), jnp.where(hit, lane_value, 0.0)], axis=0
        )
        right = jnp.where(
            sub_low == jnp.broadcast_to(lax.rem(rows, LANES), (LANES, LANES)), 1.0, 0.0
        )
        place = place + lax.dot_general(
            left.astype(jnp.bfloat16),
            right.astype(jnp.bfloat16),
            (((1,), (1,)), ((), ())),
            preferred_element_type=jnp.float32,
        )
    return (place[0:32] + 0.5).astype(jnp.int32), (place[32:64] + 0.5).astype(jnp.int32)


def adam(values, first, second, gradient):
    bias_one = 1.0 - BETA_ONE**ADAM_STEP
    bias_two = 1.0 - BETA_TWO**ADAM_STEP
    sizes = step_sizes(row_ids(PADDED)[0:PARAMS])
    new_one = BETA_ONE * first + (1.0 - BETA_ONE) * gradient
    new_two = BETA_TWO * second + (1.0 - BETA_TWO) * gradient * gradient
    updated = values - sizes * (new_one / bias_one) / (jnp.sqrt(new_two / bias_two) + ADAM_EPS)
    return updated, new_one, new_two


def per_tile(ref):
    values = ref[...]
    row, half_of = row_ids(), lane_ids() // 64
    spread = jnp.zeros((8, LANES), jnp.int32)
    for k in range(16):
        one = jnp.broadcast_to(values[:, k : k + 1], (8, LANES))
        spread = jnp.where((row == k // 2) & (half_of == k % 2), one, spread)
    return spread


def step_kernel(
    views,
    owners,
    params_hbm,
    first_hbm,
    second_hbm,
    center_hbm,
    rows_hbm,
    order_hbm,
    lists_hbm,
    target_hbm,
    counts_hbm,
    ids_hbm,
    new_params_hbm,
    new_first_hbm,
    new_second_hbm,
    last_hbm,
    new_params_ref,
    new_first_ref,
    new_second_ref,
    params_ref,
    first_ref,
    second_ref,
    center_ref,
    rows_ref,
    order_ref,
    order_lanes_ref,
    lists_ref,
    target_ref,
    counts_ref,
    ids_ref,
    dense,
    feats,
    outgoing,
    landed,
    packed,
    packed_landed,
    before_a,
    before_b,
    moved_a,
    moved_b,
    leaving,
    arriving,
    order_rows,
    list_rows,
    wanted,
    gauss,
    trans,
    gauss_grad,
    weight,
    product,
    sums,
    slot_grads,
    returned,
    by_slot,
    leaving_grads,
    arriving_grads,
    arrived_views,
    last,
    taken,
    lanes_taken,
    marked,
    grads,
    load_sems,
    store_sems,
    sems,
):
    view, me = lax.axis_index("view"), lax.axis_index("dev")
    copies = (
        (center_hbm, center_ref),
        (rows_hbm, rows_ref),
        (params_hbm, params_ref),
        (first_hbm, first_ref),
        (second_hbm, second_ref),
        (order_hbm, order_ref),
        (order_hbm, order_lanes_ref),
        (lists_hbm, lists_ref),
        (target_hbm, target_ref),
        (counts_hbm, counts_ref),
        (ids_hbm, ids_ref),
    )
    loads = [
        pltpu.make_async_copy(source, place, load_sems.at[i])
        for i, (source, place) in enumerate(copies)
    ]
    for load in loads[0:3]:
        load.start()
    barrier, expected = greet(views, owners)
    for load in loads[3:]:
        load.start()
    lane = lane_ids()
    others = pl.ds(0, owners - 1)
    other_views = pl.ds(0, views - 1)
    kept = order_ref.shape[1] - owners
    zero = jnp.zeros((8, LANES), jnp.float32)

    for load in loads[0:3]:
        load.wait()
    center = [jnp.broadcast_to(center_ref[:, i : i + 1], (8, LANES)) for i in range(3)]
    for i in range(8):
        packed[i : i + 1, :] = rows_ref[0, :, LANES * i : LANES * (i + 1)].astype(jnp.float32)
    here = zero
    for i in range(3):
        here = jnp.where(lane == i, center[i], here)
    packed[8:16, :] = here
    fill_dense(params_ref, dense)
    slot_messages(
        packed[0:8, :].astype(jnp.int32),
        center,
        dense,
        feats,
        outgoing,
    )

    fill = jnp.zeros((PADDED - PARAMS, LANES), jnp.float32)
    empty = jnp.zeros((PADDED, LANES), jnp.float32)
    loads[3].wait()
    loads[4].wait()

    def to_rows(j, carried):
        columns = pl.ds(pl.multiple_of(j * LANES, LANES), LANES)
        before_a[columns, :] = jnp.concatenate(
            [params_ref[:, columns], fill, first_ref[:, columns], fill], axis=0
        ).T
        before_b[columns, :] = jnp.concatenate([second_ref[:, columns], fill, empty], axis=0).T
        return carried

    lax.fori_loop(0, 32, to_rows, 0, unroll=8)

    for load in loads[5:]:
        load.wait()
    for t in range(owners):
        row = order_ref[0, kept + t]
        leaving[0, t : t + 1, :] = before_a[pl.ds(row, 1), :]
        leaving[1, t : t + 1, :] = before_b[pl.ds(row, 1), :]

    pl.semaphore_wait(barrier, expected)
    send_each(
        owners,
        lambda d: outgoing.at[pl.ds(d, 1)],
        lambda d: landed.at[pl.ds(d, 1)],
        sems.at[0],
        sems.at[1],
    )
    send_views(views, packed, lambda v: packed_landed.at[v], sems.at[2], sems.at[3])
    landed[pl.ds(me, 1), :] = outgoing[pl.ds(me, 1), :]
    packed_landed[view] = packed[...]

    send_each(
        owners,
        lambda d: leaving.at[:, pl.ds(d, 1)],
        lambda d: arriving.at[:, pl.ds(d, 1)],
        sems.at[4],
        sems.at[5],
    )
    arriving[:, pl.ds(me, 1), :] = leaving[:, pl.ds(me, 1), :]

    def move(t, carried):
        for u in range(32):
            row = order_ref[0, t * 32 + u]
            moved_a[pl.ds(t * 32 + u, 1), :] = before_a[pl.ds(row, 1), :]
            moved_b[pl.ds(t * 32 + u, 1), :] = before_b[pl.ds(row, 1), :]
        return carried

    lax.fori_loop(0, MOVED_EARLY // 32, move, 0)
    for k in range(16):
        list_rows[k : k + 1, 0:64] = lists_ref[0, k : k + 1, :]
    for ch in range(3):
        for p in range(2):
            n = 16 * (2 * ch + p)
            wanted[n : n + 16, :] = target_ref[ch, :, LANES * p : LANES * (p + 1)]
    even = list_rows[pl.ds(0, 8, stride=2), :]
    odd = list_rows[pl.ds(1, 8, stride=2), :]
    lists = jnp.where(lane < 64, even, pick(odd, lax.rem(lane, 64)))

    counts, ids = per_tile(counts_ref), per_tile(ids_ref)
    wait_bytes(landed.at[others], sems.at[1])
    render(
        landed,
        lists,
        counts,
        ids,
        wanted,
        slot_grads,
        gauss,
        trans,
        gauss_grad,
        weight,
        product,
        sums,
    )
    send_each(
        owners,
        lambda d: slot_grads.at[pl.ds(d, 1)],
        lambda d: returned.at[pl.ds(d, 1)],
        sems.at[6],
        sems.at[7],
    )
    returned[pl.ds(me, 1), :] = slot_grads[pl.ds(me, 1), :]

    lax.fori_loop(MOVED_EARLY // 32, kept // 32, move, 0)
    wait_bytes(arriving.at[:, others], sems.at[5])
    moved_a[kept:, :] = arriving[0]
    moved_b[kept:, :] = arriving[1]

    def to_columns(j, carried):
        columns = pl.ds(pl.multiple_of(j * LANES, LANES), LANES)
        both = moved_a[columns, :].T
        new_params_ref[:, columns] = both[0:PARAMS, :]
        new_first_ref[:, columns] = both[PADDED : PADDED + PARAMS, :]
        new_second_ref[:, columns] = moved_b[columns, :].T[0:PARAMS, :]
        dense[pl.ds(pl.multiple_of(j * PADDED, PADDED), PADDED), :] = both[0:PADDED, :]
        return carried

    lax.fori_loop(0, 32, to_columns, 0, unroll=8)
    for j in range(32):
        order_rows[j : j + 1, :] = order_lanes_ref[:, LANES * j : LANES * (j + 1)]
    wait_bytes(packed_landed.at[other_views], sems.at[3])
    place_high, place_low = slot_places(
        [packed_landed[v, 0:8, :].astype(jnp.int32) for v in range(views)]
    )
    place = place_high * LANES + place_low
    slot_high, slot_low = [], []
    for chunk in range(4):
        order = order_rows[8 * chunk : 8 * chunk + 8, :]
        high, low = order // LANES, lax.rem(order, LANES)
        found = jnp.zeros((8, LANES), jnp.int32)
        for h in range(32):
            source = jnp.broadcast_to(place[h : h + 1, :], (8, LANES))
            found = jnp.where(high == h, pick(source, low), found)
        slot_high.append(found // LANES)
        slot_low.append(lax.rem(found, LANES))
    centers = [
        [
            jnp.broadcast_to(packed_landed[v, 8:9, i : i + 1], (8, LANES))
            for v in range(views)
        ]
        for i in range(3)
    ]

    slots = (slot_high[3] * LANES + slot_low[3])[7:8, :].astype(jnp.float32)
    slots = (jnp.broadcast_to(slots, (LANES, LANES)).T + 0.5).astype(jnp.int32)
    column = lane_ids(LANES)
    here = slots // 1024 == view
    taken[...] = jnp.where((lax.rem(slots, 1024) // 8 == column) & here, 1.0, 0.0)
    lanes_taken[...] = jnp.where(column < FEATS, column * 8 + lax.rem(slots, 8), 0)
    marked[...] = jnp.where((column == FEATS) & here, (view + 1).astype(jnp.float32), 0.0)

    wait_bytes(returned.at[others], sems.at[7])
    found = dot(taken[...], returned[...])
    for i in range(16):
        rows = slice(8 * i, 8 * i + 8)
        leaving_grads[rows, :] = jnp.where(
            lane < FEATS, pick(found[rows, :], lanes_taken[rows, :]), marked[rows, :]
        )
    send_each(
        owners,
        lambda d: leaving_grads.at[pl.ds(d, 1)],
        lambda d: arriving_grads.at[pl.ds(d, 1)],
        sems.at[10],
        sems.at[11],
    )
    arriving_grads[pl.ds(me, 1), :] = leaving_grads[pl.ds(me, 1), :]

    values = [zero] * FEATS
    for o in range(16):
        block = returned[pl.ds(o, 8, stride=16), :]
        chosen = lane // 8 == o
        for f in range(FEATS):
            values[f] = jnp.where(chosen, pick(block, 8 * f + lax.rem(lane, 8)), values[f])
    for f in range(FEATS):
        by_slot[view, 8 * f : 8 * f + 8, :] = values[f]
    send_views(views, by_slot.at[view], lambda v: by_slot.at[v], sems.at[8], sems.at[9])
    wait_bytes(by_slot.at[other_views], sems.at[9])

    def collect(chunk):
        found = [zero] * FEATS
        for h in range(32):
            chosen = slot_high[chunk] == h
            for f in range(FEATS):
                row = 8 * f + h % 8
                source = jnp.broadcast_to(by_slot[h // 8, row : row + 1, :], (8, LANES))
                found[f] = jnp.where(chosen, pick(source, slot_low[chunk]), found[f])
        return found

    stores = []

    def finish(chunk, feat_grads, count):
        view_of = slot_high[chunk] // 8
        center = []
        for i in range(3):
            at = zero
            for v in range(views):
                at = jnp.where(view_of == v, centers[i][v], at)
            center.append(at)
        arguments = [dense_at(dense, chunk, p) for p in range(PARAMS)]
        _, pull_back = jax.vjp(lambda *args: project(args, center), *arguments)
        for p, grad in enumerate(pull_back(list(feat_grads))):
            grads[pl.ds(chunk * 8 * PADDED + p, 8, stride=PADDED), :] = grad
        for j in range(8 * chunk, 8 * chunk + count):
            columns = slice(LANES * j, LANES * (j + 1))
            gradient = grads[PADDED * j : PADDED * j + PARAMS, :]
            (
                new_params_ref[:, columns],
                new_first_ref[:, columns],
                new_second_ref[:, columns],
            ) = adam(
                new_params_ref[:, columns],
                new_first_ref[:, columns],
                new_second_ref[:, columns],
                gradient,
            )
        columns = pl.ds(8 * LANES * chunk, 8 * LANES)
        for i, (source, place) in enumerate(
            (
                (new_params_ref, new_params_hbm),
                (new_first_ref, new_first_hbm),
                (new_second_ref, new_second_hbm),
            )
        ):
            copy = pltpu.make_async_copy(
                source.at[:, columns], place.at[:, columns], store_sems.at[len(stores)]
            )
            copy.start()
            stores.append(copy)

    for chunk in range(2):
        finish(chunk, collect(chunk), 8)
    for v in range(views):
        last[16 + 16 * v : 32 + 16 * v, :] = packed_landed[v]
    wait_bytes(arriving_grads.at[others], sems.at[11])
    arrived_views[view] = arriving_grads[...].T[0:16, :]
    send_views(
        views, arrived_views.at[view], lambda v: arrived_views.at[v], sems.at[12], sems.at[13]
    )
    for chunk in (2, 3):
        finish(chunk, collect(chunk), 8 if chunk < 3 else 7)
    wait_bytes(arrived_views.at[other_views], sems.at[13])
    arrived = arrived_views[0]
    for v in range(1, views):
        arrived = arrived + arrived_views[v]
    last[0:16, :] = arrived
    copy = pltpu.make_async_copy(last, last_hbm, store_sems.at[len(stores)])
    copy.start()
    stores.append(copy)
    wait_bytes(landed.at[others], sems.at[0])
    wait_bytes(packed_landed.at[other_views], sems.at[2])
    wait_bytes(arriving.at[:, others], sems.at[4])
    wait_bytes(returned.at[others], sems.at[6])
    wait_bytes(by_slot.at[other_views], sems.at[8])
    wait_bytes(arriving_grads.at[others], sems.at[10])
    wait_bytes(arrived_views.at[other_views], sems.at[12])
    for copy in stores:
        copy.wait()


def write_kernel(
    params,
    first,
    second,
    last_hbm,
    new_params,
    new_first,
    new_second,
    held,
    last,
    grads,
    load_sems,
    store_sems,
):
    ends = ((params, new_params), (first, new_first), (second, new_second))
    parts = [pl.ds(3968, 128)] + [pl.ds(1024 * k, 1024) for k in range(3)] + [pl.ds(3072, 896)]
    loads, stores = [pltpu.make_async_copy(last_hbm, last, load_sems.at[0])], []
    for columns in parts:
        for i, (source, place) in enumerate(ends):
            middle = held.at[i, :, columns]
            loads.append(
                pltpu.make_async_copy(source.at[:, columns], middle, load_sems.at[len(loads)])
            )
            stores.append(
                pltpu.make_async_copy(middle, place.at[:, columns], store_sems.at[len(stores)])
            )
    for load in loads:
        load.start()
    for load in loads[0:4]:
        load.wait()
    columns = slice(3968, 4096)
    view_of = (last[FEATS : FEATS + 1, :] + 0.5).astype(jnp.int32) - 1
    center = []
    for i in range(3):
        at = jnp.zeros((1, LANES), jnp.float32)
        for v in range(last.shape[0] // 16 - 1):
            row = 16 * v + 24
            one = jnp.broadcast_to(last[row : row + 1, i : i + 1], (1, LANES))
            at = jnp.where(view_of == v, one, at)
        center.append(at)
    arguments = [held[0, p : p + 1, columns] for p in range(PARAMS)]
    _, pull_back = jax.vjp(lambda *args: project(args, center), *arguments)
    for p, grad in enumerate(pull_back([last[f : f + 1, :] for f in range(FEATS)])):
        grads[p : p + 1, :] = grad
    held[0, :, columns], held[1, :, columns], held[2, :, columns] = adam(
        held[0, :, columns], held[1, :, columns], held[2, :, columns], grads[0:PARAMS, :]
    )
    for store in stores[0:3]:
        store.start()
    for load, store in zip(loads[4:], stores[3:]):
        load.wait()
        store.start()
    for store in stores:
        store.wait()


VMEM = pl.BlockSpec(memory_space=pltpu.VMEM)
SMEM = pl.BlockSpec(memory_space=pltpu.SMEM)
ANY = pl.BlockSpec(memory_space=pl.ANY)
HBM = pl.BlockSpec(memory_space=pltpu.HBM)
VMEM_BYTES = 60 * 1024 * 1024


def f32(*shape):
    return jax.ShapeDtypeStruct(shape, jnp.float32)


def scratch(*shape):
    return pltpu.VMEM(shape, jnp.float32)


def per_device(
    params,
    first_moment,
    second_moment,
    cam_centers,
    target,
    send_rows,
    tile_lists,
    tile_counts,
    tile_ids,
    move_order,
):
    views, owners = lax.axis_size("view"), lax.axis_size("dev")
    by_channel = target[0].transpose(1, 0, 2)
    updated = pl.pallas_call(
        functools.partial(step_kernel, views, owners),
        out_shape=(f32(PARAMS, 4096),) * 3 + (f32(16 + 16 * views, LANES),),
        in_specs=[HBM] * 10,
        out_specs=(ANY,) * 4,
        scratch_shapes=[
            scratch(PARAMS, 4096),
            scratch(PARAMS, 4096),
            scratch(PARAMS, 4096),
            scratch(PARAMS, 4096),
            scratch(PARAMS, 4096),
            scratch(PARAMS, 4096),
            scratch(*cam_centers.shape),
            pltpu.VMEM(send_rows.shape, jnp.int32),
            pltpu.SMEM(move_order.shape, jnp.int32),
            pltpu.VMEM(move_order.shape, jnp.int32),
            pltpu.VMEM(tile_lists.shape, jnp.int32),
            scratch(*by_channel.shape),
            pltpu.VMEM(tile_counts.shape, jnp.int32),
            pltpu.VMEM(tile_ids.shape, jnp.int32),
            scratch(32 * PADDED, LANES),
            scratch(FEATS, 32, LANES),
            scratch(owners, LANES),
            scratch(owners, LANES),
            scratch(16, LANES),
            scratch(views, 16, LANES),
            scratch(4096, LANES),
            scratch(4096, LANES),
            scratch(4096, LANES),
            scratch(4096, LANES),
            scratch(2, owners, LANES),
            scratch(2, owners, LANES),
            pltpu.VMEM((32, LANES), jnp.int32),
            pltpu.VMEM((16, LANES), jnp.int32),
            scratch(96, LANES),
            scratch(64, 4, 8, LANES),
            scratch(64, 4, 8, LANES),
            scratch(1024, 2 * LANES),
            scratch(1024, 2 * LANES),
            scratch(1024, LANES),
            scratch(512, LANES),
            scratch(owners, LANES),
            scratch(owners, LANES),
            scratch(views, 8 * FEATS, LANES),
            scratch(owners, LANES),
            scratch(owners, LANES),
            scratch(views, 16, LANES),
            scratch(16 + 16 * views, LANES),
            scratch(owners, LANES),
            pltpu.VMEM((owners, LANES), jnp.int32),
            scratch(owners, LANES),
            scratch(32 * PADDED, LANES),
            pltpu.SemaphoreType.DMA((11,)),
            pltpu.SemaphoreType.DMA((13,)),
            pltpu.SemaphoreType.DMA((14,)),
        ],
        compiler_params=pltpu.CompilerParams(
            vmem_limit_bytes=VMEM_BYTES, collective_id=0, has_side_effects=True
        ),
        name="step",
    )(
        params,
        first_moment,
        second_moment,
        cam_centers,
        send_rows,
        move_order,
        tile_lists,
        by_channel,
        tile_counts,
        tile_ids,
    )
    return pl.pallas_call(
        write_kernel,
        out_shape=(f32(PARAMS, 4096),) * 3,
        in_specs=[ANY] * 4,
        out_specs=(HBM,) * 3,
        scratch_shapes=[
            scratch(3, PARAMS, 4096),
            scratch(16 + 16 * views, LANES),
            scratch(PADDED, LANES),
            pltpu.SemaphoreType.DMA((16,)),
            pltpu.SemaphoreType.DMA((15,)),
        ],
        compiler_params=pltpu.CompilerParams(vmem_limit_bytes=VMEM_BYTES),
        name="write",
    )(*updated)


def solution(mesh):
    placed = (
        P(None, "dev"),
        P(None, "dev"),
        P(None, "dev"),
        P("view", None),
        P("view", "dev", None, None),
        P("view", "dev", None),
        P("view", "dev", None),
        P("view", "dev"),
        P("view", "dev"),
        P("dev", None),
    )
    return jax.shard_map(
        per_device,
        mesh=mesh,
        in_specs=placed,
        out_specs=(P(None, "dev"), P(None, "dev"), P(None, "dev")),
        check_vma=False,
    )
```
